128 devices in a mesh: batch: 32 (over y, x, core), seq: 4 (over z).
Axes of the slice: x: 4, y: 4, z: 4, core: 2. Of those that a mesh axis runs over, the one named last changes fastest.
Arguments:
- token_ids: int32 [96, 512], P('batch', 'seq'), may hold values from 0 to 500735, as said below
- lengths: int32 [96], P('batch'), may hold values from 128 to 512, as said below
- word_table: bfloat16 [500736, 768], P(('batch', 'seq')), may hold values from -6 to 6
- positions: bfloat16 [512, 768], P('seq'), may hold values from -3 to 3
- query_weight: bfloat16 [768, 768], replicated, may hold values from -0.21875 to 0.21875
- key_weight: bfloat16 [768, 768], replicated, may hold values from -0.21875 to 0.21875
- value_weight: bfloat16 [768, 768], replicated, may hold values from -0.21875 to 0.21875
- query_bias: bfloat16 [768], replicated, may hold values from -1.75 to 1.75
- value_bias: bfloat16 [768], replicated, may hold values from -1.75 to 1.75
- output_weight: bfloat16 [768, 768], replicated, may hold values from -1.25 to 1.25
- output_bias: bfloat16 [768], replicated, may hold values from -1.75 to 1.75
- first_gain: bfloat16 [768], replicated, may hold values from 0.5 to 1.5
- first_shift: bfloat16 [768], replicated, may hold values from -1.75 to 1.75
- inner_weight: bfloat16 [768, 3072], replicated, may hold values from -0.21875 to 0.21875
- inner_bias: bfloat16 [3072], replicated, may hold values from -1.75 to 1.75
- outer_weight: bfloat16 [3072, 768], replicated, may hold values from -0.109375 to 0.109375
- outer_bias: bfloat16 [768], replicated, may hold values from -1.75 to 1.75
- second_gain: bfloat16 [768], replicated, may hold values from 0.5 to 1.5
- second_shift: bfloat16 [768], replicated, may hold values from -1.75 to 1.75
- pooler_weight: bfloat16 [768, 768], replicated, may hold values from -0.21875 to 0.21875
- pooler_bias: bfloat16 [768], replicated, may hold values from -1.75 to 1.75
- out_grad: bfloat16 [96, 512, 768], P('batch', 'seq'), may hold values from -6 to 6
- pooled_grad: float32 [96, 768], P('batch', 'seq'), may hold values from -6 to 6
Outputs:
- hidden_out: bfloat16 [96, 512, 768], P('batch', 'seq')
- pooled: float32 [96, 768], P('batch', 'seq')
- grad_table: float32 [500736, 768], P(('batch', 'seq'))
- grad_positions: float32 [512, 768], P('seq')
- grad_query_weight: float32 [768, 768], P('seq')
- grad_key_weight: float32 [768, 768], P('seq')
- grad_value_weight: float32 [768, 768], P('seq')
- grad_query_bias: float32 [768], P('seq')
- grad_value_bias: float32 [768], P('seq')
- grad_output_weight: float32 [768, 768], P('seq')
- grad_output_bias: float32 [768], P('seq')
- grad_first_gain: float32 [768], P('seq')
- grad_first_shift: float32 [768], P('seq')
- grad_inner_weight: float32 [768, 3072], P('seq')
- grad_inner_bias: float32 [3072], P('seq')
- grad_outer_weight: float32 [3072, 768], P('seq')
- grad_outer_bias: float32 [768], P('seq')
- grad_second_gain: float32 [768], P('seq')
- grad_second_shift: float32 [768], P('seq')
- grad_pooler_weight: float32 [768, 768], P('seq')
- grad_pooler_bias: float32 [768], P('seq')
The draws below stay inside these ranges and needn't reach their ends.
Inputs may be any that keep to these rules, and one draw needn't show every extreme that they name: `token_ids`: on the tokens of one device (one index of batch and of seq), no range of 3912 consecutive table rows that one device holds is named by more than 6 tokens, and some ranges are named by exactly 6 tokens of every device. `lengths`: among the 3 sentences of each index of batch, at least one has length 512.
All inputs are finite; a program needn't handle non-finite values.
Results may differ from the reference program's by a relative error of at most 0.02.
Values may be sent and summed in bfloat16 or wider, within the bound.
No kernel may reach another device: no remote copies, remote signals or barrier semaphores. Data moves between devices by JAX's collectives and lax.ppermute only.
A program may use at most 256 MiB of HBM per device.

```python
import math
import jax
import jax.numpy as jnp
from jax import lax

D = 768
HEAD_DIM = 64
FF = 3072
SEQ_LEN = 512
VOC_DEV = 3912
SENT_DEV = 3
TOK_SPLIT = 128
TOK_DEV = 384
SENTS = 96
VOCAB = 500736
N_BATCH = 32
N_SEQ = 4


def draw_token_ids(key, part):
    key = jax.random.fold_in(key, 11)
    devices = N_BATCH * N_SEQ
    order_key, place_key, row_key, skew_key = jax.random.split(key, 4)
    ranking = jax.random.permutation(order_key, devices)
    residue = jnp.arange(devices, dtype=jnp.int32)
    moved = jnp.where(residue < devices // 4, residue + devices // 2, residue)
    owner_of = ranking[moved]
    slot_ids = jnp.arange(TOK_DEV, dtype=jnp.int32) % devices
    shuffled = jax.vmap(lambda sub_key: jax.random.permutation(sub_key, slot_ids))(jax.random.split(place_key, devices))
    owners = owner_of[shuffled]
    first_pick = jax.random.randint(row_key, (devices, TOK_DEV), 0, VOC_DEV)
    second_pick = jax.random.randint(skew_key, (devices, TOK_DEV), 0, VOC_DEV)
    local_rows = first_pick * second_pick // VOC_DEV
    token_ids = owners * VOC_DEV + local_rows
    token_ids = token_ids.reshape(N_BATCH, N_SEQ, SENT_DEV, TOK_SPLIT).transpose(0, 2, 1, 3).reshape(N_BATCH * SENT_DEV, SEQ_LEN)
    return token_ids.astype(jnp.int32)


def draw_lengths(key, part):
    key = jax.random.fold_in(key, 23)
    pick_key, length_key = jax.random.split(key)
    drawn = jax.random.randint(length_key, (N_BATCH, SENT_DEV), SEQ_LEN // 4, SEQ_LEN + 1)
    full_one = jax.random.randint(pick_key, (N_BATCH, 1), 0, SENT_DEV)
    drawn = jnp.where(jnp.arange(SENT_DEV, dtype=jnp.int32)[None, :] == full_one, SEQ_LEN, drawn)
    return drawn.reshape(-1).astype(jnp.int32)


def shard_levels(rng, extent, shards, low, largest):
    def one(dim, blocks):
        draws = jax.random.uniform(jax.random.fold_in(jax.random.fold_in(rng, 6), dim), (blocks,), jnp.float32, low / len(shards), largest / len(shards))
        return jnp.repeat(jnp.exp(draws), extent[dim] // blocks).reshape((-1,) + (1,) * (len(extent) - dim - 1))

    factor_of = one(*shards[0])
    for cut in shards[1:]:
        factor_of = factor_of * one(*cut)
    return factor_of


def noise(rng, shape, deviation, reach, shards=(), held_as=jnp.bfloat16):
    entries = deviation * jax.random.normal(rng, shape, jnp.float32)
    if shards:
        entries = entries * shard_levels(rng, shape, shards, -0.22, 0.18)
    return jnp.clip(entries, -reach, reach).astype(held_as)


def setup_inputs(seed: int = 0) -> dict:
    arg_keys = jax.random.split(jax.random.key(seed), 24)
    token_ids = draw_token_ids(jax.random.fold_in(arg_keys[23], 71), 0)
    lengths = draw_lengths(jax.random.fold_in(arg_keys[23], 71), 0)
    word_table = noise(arg_keys[2], (VOCAB, D), 1.0, 6.0, ((0, 128),))
    positions = noise(arg_keys[3], (SEQ_LEN, D), 0.5, 3.0, ((0, 4),))
    query_weight = noise(arg_keys[4], (D, D), D ** -0.5, 0.21875)
    key_weight = noise(arg_keys[5], (D, D), D ** -0.5, 0.21875)
    value_weight = noise(arg_keys[6], (D, D), D ** -0.5, 0.21875)
    query_bias = noise(arg_keys[7], (D,), 0.3, 1.75)
    value_bias = noise(arg_keys[8], (D,), 0.3, 1.75)
    output_weight = noise(arg_keys[9], (D, D), (D // 32) ** -0.5, 1.25)
    output_bias = noise(arg_keys[10], (D,), 0.3, 1.75)
    first_gain = jnp.clip(1.0 + 0.1 * jax.random.normal(arg_keys[11], (D,), jnp.float32), 0.5, 1.5).astype(jnp.bfloat16)
    first_shift = noise(arg_keys[12], (D,), 0.3, 1.75)
    inner_weight = noise(arg_keys[13], (D, FF), D ** -0.5, 0.21875)
    inner_bias = noise(arg_keys[14], (FF,), 0.3, 1.75)
    outer_weight = noise(arg_keys[15], (FF, D), FF ** -0.5, 0.109375)
    outer_bias = noise(arg_keys[16], (D,), 0.3, 1.75)
    second_gain = jnp.clip(1.0 + 0.1 * jax.random.normal(arg_keys[17], (D,), jnp.float32), 0.5, 1.5).astype(jnp.bfloat16)
    second_shift = noise(arg_keys[18], (D,), 0.3, 1.75)
    pooler_weight = noise(arg_keys[19], (D, D), D ** -0.5, 0.21875)
    pooler_bias = noise(arg_keys[20], (D,), 0.3, 1.75)
    out_grad = noise(arg_keys[21], (SENTS, SEQ_LEN, D), 1.0, 6.0, ((0, 32), (1, 4)))
    pooled_grad = noise(arg_keys[22], (SENTS, D), 1.0, 6.0, ((0, 32), (1, 4)), jnp.float32)
    return {"token_ids": token_ids, "lengths": lengths, "word_table": word_table, "positions": positions, "query_weight": query_weight, "key_weight": key_weight, "value_weight": value_weight, "query_bias": query_bias, "value_bias": value_bias, "output_weight": output_weight, "output_bias": output_bias, "first_gain": first_gain, "first_shift": first_shift, "inner_weight": inner_weight, "inner_bias": inner_bias, "outer_weight": outer_weight, "outer_bias": outer_bias, "second_gain": second_gain, "second_shift": second_shift, "pooler_weight": pooler_weight, "pooler_bias": pooler_bias, "out_grad": out_grad, "pooled_grad": pooled_grad}


EPSILON = 1e-12
MASKED = -1000000000.0
HIGHEST = lax.Precision.HIGHEST

@jax.custom_vjp
def low(v):
    return lax.optimization_barrier(v.astype(jnp.bfloat16)).astype(jnp.float32)

@jax.custom_vjp
def low_back(v):
    return v

def low_keep(v):
    return (low(v), None)

def low_pass(kept, grad):
    return (grad,)

def back_keep(v):
    return (v, None)

def back_low(kept, grad):
    return (low(grad),)
low.defvjp(low_keep, low_pass)
low_back.defvjp(back_keep, back_low)

def dense(left_mat, right_mat):
    return jnp.dot(left_mat, right_mat, precision=HIGHEST)

def normalize(values, gain_vec, shift_vec):
    center = values - lax.optimization_barrier(jnp.mean(values, axis=-1, keepdims=True))
    inverse = lax.rsqrt(lax.optimization_barrier(jnp.mean(center * center, axis=-1, keepdims=True)) + EPSILON)
    return center * inverse * gain_vec + shift_vec

def forward(params, word_rows, block_lengths):
    positions, query_weight, key_weight, value_weight, query_bias, value_bias, output_weight, output_bias, first_gain, first_shift, inner_weight, inner_bias, outer_weight, outer_bias, second_gain, second_shift, pooler_weight, pooler_bias = params
    group = word_rows.shape[0]
    head_count = D // HEAD_DIM
    query_scale = HEAD_DIM ** (-0.5)
    embed = low(word_rows + positions[None]).reshape(-1, D)
    query_heads = low(low_back((dense(embed, query_weight) + query_bias) * query_scale)).reshape(group, SEQ_LEN, head_count, HEAD_DIM)
    key_heads = low(low_back(dense(embed, key_weight))).reshape(group, SEQ_LEN, head_count, HEAD_DIM)
    value_heads = low(low_back(dense(embed, value_weight) + value_bias)).reshape(group, SEQ_LEN, head_count, HEAD_DIM)
    scores = low_back(jnp.einsum('sqhd,skhd->shqk', query_heads, key_heads, precision=HIGHEST))
    live_key = jnp.arange(SEQ_LEN, dtype=jnp.int32)[None, :] < block_lengths[:, None]
    scores = jnp.where(live_key[:, None, None, :], scores, MASKED)
    probs_low = low(jax.nn.softmax(scores, axis=-1))
    mixed_low = low(low_back(jnp.einsum('shqk,skhd->sqhd', probs_low, value_heads, precision=HIGHEST))).reshape(-1, D)
    attention = low_back(dense(mixed_low, output_weight) + output_bias)
    hidden = low(normalize(embed + attention, first_gain, first_shift))
    inner_pre = low_back(dense(hidden, inner_weight) + inner_bias)
    active = low(jax.nn.gelu(inner_pre, approximate=False))
    outer_pre = low_back(dense(active, outer_weight) + outer_bias)
    result_rows = low(normalize(hidden + outer_pre, second_gain, second_shift)).reshape(group, SEQ_LEN, D)
    pool_pre = low_back(dense(result_rows[:, 0], pooler_weight) + pooler_bias)
    return (result_rows, jnp.tanh(pool_pre))

def reference(token_ids, lengths, word_table, positions, query_weight, key_weight, value_weight, query_bias, value_bias, output_weight, output_bias, first_gain, first_shift, inner_weight, inner_bias, outer_weight, outer_bias, second_gain, second_shift, pooler_weight, pooler_bias, out_grad, pooled_grad):
    params = tuple((member.astype(jnp.float32) for member in (positions, query_weight, key_weight, value_weight, query_bias, value_bias, output_weight, output_bias, first_gain, first_shift, inner_weight, inner_bias, outer_weight, outer_bias, second_gain, second_shift, pooler_weight, pooler_bias)))
    group = math.gcd(SENTS, max(1, 4096 // SEQ_LEN))
    block_count = SENTS // group
    words_all = word_table[token_ids].astype(jnp.float32).reshape(block_count, group, SEQ_LEN, D)
    lengths_all = lengths.reshape(block_count, group)
    upstream_all = out_grad.astype(jnp.float32).reshape(block_count, group, SEQ_LEN, D)
    pooled_all = pooled_grad.astype(jnp.float32).reshape(block_count, group, D)

    def step(total, block):
        block_words, block_lengths, block_upstream, block_pooled = block

        def layer(weights, rows_in):
            return forward(weights, rows_in, block_lengths)
        outputs, pull = jax.vjp(layer, params, block_words)
        grad_params, grad_words = pull((block_upstream, block_pooled))
        return (jax.tree.map(jnp.add, total, grad_params), (outputs[0], outputs[1], grad_words))
    start_total = tuple((jnp.zeros_like(member) for member in params))
    total, (hidden_blocks, pooled_blocks, grad_words) = lax.scan(step, start_total, (words_all, lengths_all, upstream_all, pooled_all))
    grad_positions, grad_query_weight, grad_key_weight, grad_value_weight, grad_query_bias, grad_value_bias, grad_output_weight, grad_output_bias, grad_first_gain, grad_first_shift, grad_inner_weight, grad_inner_bias, grad_outer_weight, grad_outer_bias, grad_second_gain, grad_second_shift, grad_pooler_weight, grad_pooler_bias = total
    hidden_out = hidden_blocks.reshape(SENTS, SEQ_LEN, D).astype(jnp.bfloat16)
    pooled = pooled_blocks.reshape(SENTS, D)
    grad_table = jnp.zeros((VOCAB, D), jnp.float32).at[token_ids.reshape(-1)].add(grad_words.reshape(-1, D))
    return (hidden_out, pooled, grad_table, grad_positions, grad_query_weight, grad_key_weight, grad_value_weight, grad_query_bias, grad_value_bias, grad_output_weight, grad_output_bias, grad_first_gain, grad_first_shift, grad_inner_weight, grad_inner_bias, grad_outer_weight, grad_outer_bias, grad_second_gain, grad_second_shift, grad_pooler_weight, grad_pooler_bias)
```

```python
import functools
import jax
import jax.numpy as jnp
from jax import lax
from jax.experimental import pallas as pl
from jax.experimental.pallas import tpu as pltpu
from jax.sharding import PartitionSpec as P

F32 = jnp.float32
LOW = jnp.bfloat16
EPSILON = 1e-12
MASKED = -1000000000.0
HEAD_DIM = 64
VMEM = 56 * 1024 * 1024
HALF = 384
SHARE = 0.02


def nn(a, b):
    return lax.dot_general(a, b, (((1,), (0,)), ((), ())), preferred_element_type=F32)


def nt(a, b):
    return lax.dot_general(a, b, (((1,), (1,)), ((), ())), preferred_element_type=F32)


def struct(shape, dtype):
    return jax.ShapeDtypeStruct(shape, dtype)


def whole(shape):
    zeros = (0,) * len(shape)
    return pl.BlockSpec(shape, lambda *_: zeros)


def cost(flops, size):
    return pl.CostEstimate(
        flops=int(flops * SHARE), bytes_accessed=int(size * SHARE), transcendentals=0
    )


def params(**kw):
    return pltpu.CompilerParams(vmem_limit_bytes=VMEM, **kw)


def attn_fwd_kernel(
    x0, x1, x2, x3, wq, wk, wv, bq, bv, live, x_o, q_o, k_o, v_o, e_o, inv_o, mt_o, mixed_o, x
):
    scale = HEAD_DIM ** (-0.5)
    n = x0.shape[0]

    @pl.when(pl.program_id(0) == 0)
    def _():
        for m, part in enumerate((x0, x1, x2, x3)):
            x[m * n : m * n + n, :] = part[...]
            x_o[m * n : m * n + n, :] = part[...]

    q = ((nn(x[...], wq[...]) + bq[...].astype(F32)) * scale).astype(LOW)
    q_o[...] = q
    k = nn(x[...], wk[...]).astype(LOW)
    k_o[...] = k
    v = nn(x[...], wv[...]) + bv[...].astype(F32)
    v_o[...] = v.astype(LOW)
    keep = live[...] > 0.0
    lane = lax.broadcasted_iota(jnp.int32, (1, 128), 1)
    for pair in range(q.shape[1] // 128):
        cols = slice(128 * pair, 128 * pair + 128)
        q2, k2 = q[:, cols], k[:, cols]
        vt = v[:, cols].T.astype(LOW)
        parts = []
        for h in range(2):
            kz = jnp.where((lane // 64) == h, k2, jnp.zeros((), LOW))
            s = nt(kz, q2)
            s = jnp.where(keep, s, MASKED)
            e = jnp.exp(s - jnp.max(s, axis=0, keepdims=True))
            inv = 1.0 / jnp.sum(e, axis=0, keepdims=True)
            eb = e.astype(LOW)
            e_o[2 * pair + h] = eb
            inv_o[2 * pair + h] = inv
            parts.append(nn(vt[64 * h : 64 * h + 64], eb) * inv)
        mt = jnp.concatenate(parts, axis=0)
        mt_o[cols, :] = mt.astype(LOW)
        mixed_o[:, cols] = mt.T.astype(LOW)


def attn_fwd(parts, wq, wk, wv, bq, bv, live, group=256):
    n, d = parts[0].shape
    s = 4 * n
    hg = group // HEAD_DIM
    col = pl.BlockSpec((s, group), lambda h: (0, h))
    wcol = pl.BlockSpec((d, group), lambda h: (0, h))
    brow = pl.BlockSpec((1, group), lambda h: (0, h))
    heads = d // HEAD_DIM
    return pl.pallas_call(
        attn_fwd_kernel,
        grid=(d // group,),
        in_specs=[whole((n, d))] * 4 + [wcol, wcol, wcol, brow, brow, whole((s, 1))],
        out_specs=[
            whole((s, d)),
            col,
            col,
            col,
            pl.BlockSpec((hg, s, s), lambda h: (h, 0, 0)),
            pl.BlockSpec((hg, 1, s), lambda h: (h, 0, 0)),
            pl.BlockSpec((group, s), lambda h: (h, 0)),
            col,
        ],
        out_shape=[
            struct((s, d), LOW),
            struct((s, d), LOW),
            struct((s, d), LOW),
            struct((s, d), LOW),
            struct((heads, s, s), LOW),
            struct((heads, 1, s), F32),
            struct((d, s), LOW),
            struct((s, d), LOW),
        ],
        scratch_shapes=[pltpu.VMEM((s, d), LOW)],
        compiler_params=params(),
        cost_estimate=cost(6 * s * d * d + 4 * s * s * 256 * heads, 16e6),
        name="attention_forward",
    )(*parts, wq, wk, wv, bq, bv, live)


def attn_bwd_heads(al, wo, q, k, v, e_i, inv_i, mt_i, dm, dq, dk, dv):
    step = pl.program_id(0)

    @pl.when(step == 0)
    def _():
        dm[...] = nt(al[...], wo[...]).astype(LOW)

    lane = lax.broadcasted_iota(jnp.int32, (1, 128), 1)
    cols = pl.ds(pl.multiple_of(step * 128, 128), 128)
    q2, k2, v2 = q[...], k[...], v[...]
    dmt = dm[:, cols].astype(F32).T
    kt = k2.astype(F32).T.astype(LOW)
    prod = dmt * mt_i[...].astype(F32)
    inv2 = [inv_i[h] for h in range(2)]
    dots = jnp.concatenate([dmt[64 * h : 64 * h + 64] * inv2[h] for h in range(2)], axis=0)
    dot_low = dots.astype(LOW)
    dout = dots.T.astype(LOW)
    dqt, dk2, dv2 = [], [], []
    for h in range(2):
        mine = (lane // 64) == h
        e = e_i[h]
        delta = jnp.sum(prod[64 * h : 64 * h + 64], axis=0, keepdims=True) * inv2[h]
        vz = jnp.where(mine, v2, jnp.zeros((), LOW))
        dp = nn(vz, dot_low)
        ds = (e.astype(F32) * (dp - delta)).astype(LOW)
        dv2.append(nn(e, dout))
        dk2.append(nn(ds, q2))
        dqt.append(nn(kt[64 * h : 64 * h + 64], ds))
    first = lane < 64
    dv[:, cols] = jnp.where(first, dv2[0], dv2[1]).astype(LOW)
    dk[:, cols] = jnp.where(first, dk2[0], dk2[1]).astype(LOW)
    dq[:, cols] = jnp.concatenate(dqt, axis=0).T.astype(LOW)


def embed_part(dq, dk, dv, wq, wk, wv, rows):
    return (
        nt(dq[rows, :], wq[...]) * HEAD_DIM ** (-0.5) + nt(dk[rows, :], wk[...]) + nt(dv[rows, :], wv[...])
    )


def attn_bwd_kernel(
    place, al, wo, q, k, v, e_i, inv_i, mt_i, wq, wk, wv, x, base,
    p0, p1, p2, p3, send, keep, qb_o, vb_o, dm, dq, dk, dv
):
    attn_bwd_heads(al, wo, q, k, v, e_i, inv_i, mt_i, dm, dq, dk, dv)

    @pl.when(pl.program_id(0) == pl.num_programs(0) - 1)
    def _():
        n = p0.shape[0]
        for m, part in enumerate((p0, p1, p2, p3)):
            rows = slice(m * n, m * n + n)
            part[...] = (base[rows, :] + embed_part(dq, dk, dv, wq, wk, wv, rows)).astype(LOW)
        core = place[0]
        for out, half in ((send, 1 - core), (keep, core)):
            cols = pl.ds(pl.multiple_of(half * HALF, 128), HALF)
            for i, grad in enumerate((dq, dk, dv)):
                scale = HEAD_DIM ** (-0.5) if i == 0 else 1.0
                out[i] = (tn(x[...], grad[:, cols]) * scale).astype(LOW).reshape(out.shape[1:])
        qb_o[...] = jnp.sum(dq[...].astype(F32), axis=0, keepdims=True) * HEAD_DIM ** (-0.5)
        vb_o[...] = jnp.sum(dv[...].astype(F32), axis=0, keepdims=True)


def attn_bwd(place, al, wo, q, k, v, e, inv, mt, wq, wk, wv, x, base):
    s, d = q.shape
    steps = d // 128
    heads = d // HEAD_DIM
    col = pl.BlockSpec((s, 128), lambda h, p: (0, h))
    row = whole((1, d))
    ins = [
        whole((s, d)),
        whole((d, d)),
        col,
        col,
        col,
        pl.BlockSpec((2, s, s), lambda h, p: (h, 0, 0)),
        pl.BlockSpec((2, 1, s), lambda h, p: (h, 0, 0)),
        pl.BlockSpec((128, s), lambda h, p: (h, 0)),
        whole((d, d)),
        whole((d, d)),
        whole((d, d)),
        whole((s, d)),
        whole((s, d)),
    ]
    block = (4, d // 4, HALF)
    shapes = (
        [((s // 4, d), LOW)] * 4
        + [((3,) + block, LOW)] * 2
        + [((1, d), F32)] * 2
    )
    return pl.pallas_call(
        attn_bwd_kernel,
        grid_spec=prefetch(
            1,
            (steps,),
            ins,
            [whole(shape) for shape, _ in shapes],
            [pltpu.VMEM((s, d), LOW)] * 4,
        ),
        out_shape=[struct(*one) for one in shapes],
        compiler_params=params(),
        cost_estimate=cost(14 * s * d * d + 8 * s * s * 256 * heads, 28e6),
        name="attention_backward",
    )(place, al, wo, q, k, v, e, inv, mt, wq, wk, wv, x, base)


def normalize(values):
    center = values - jnp.mean(values, axis=-1, keepdims=True)
    root = lax.rsqrt(jnp.mean(center * center, axis=-1, keepdims=True) + EPSILON)
    return center * root, root


def normalize_back(upstream, normed, root, gain):
    scaled = upstream * gain
    plain = jnp.mean(scaled, axis=-1, keepdims=True)
    crossed = jnp.mean(scaled * normed, axis=-1, keepdims=True)
    return root * (scaled - plain - normed * crossed)


def gelu_pair(v):
    x = jnp.abs(v) * 0.7071067811865476
    t = 1.0 / (1.0 + 0.3275911 * x)
    bell = jnp.exp(v * v * -0.5)
    poly = t * (
        0.127414796 + t * (-0.142248368 + t * (0.7107068705 + t * (-0.7265760135 + t * 0.5307027145)))
    )
    tail = poly * bell
    cdf = jnp.where(v >= 0.0, 1.0 - tail, tail)
    return v * cdf, cdf + v * (bell * 0.3989422804014327)


def mid_kernel(
    row0, mixed, wo, bo, x, g1, s1, w1, b1, w2, b2, g2, s2, wp, bp, u0, u1, u2, u3, pu,
    normed_o, root_o, hid_o, act_o, gp_o, t0, t1, t2, t3, sb_o, ol_o, vec_o,
    hid, acc, *, chunk
):
    f = pl.program_id(0)
    s, d = x.shape
    ups = (u0, u1, u2, u3)
    n = u0.shape[0]
    per = chunk // n
    outs = (t0, t1, t2, t3)

    @pl.when(f == 0)
    def _():
        for r in range(0, s, chunk):
            rows = slice(r, r + chunk)
            val = nn(mixed[rows, :], wo[...]) + bo[...].astype(F32) + x[rows, :].astype(F32)
            normed, root = normalize(val)
            normed_o[rows, :] = normed
            root_o[rows, :] = root
            h = (normed * g1[...].astype(F32) + s1[...].astype(F32)).astype(LOW)
            hid[rows, :] = h
            hid_o[rows, :] = h
            acc[rows, :] = h.astype(F32) + b2[...].astype(F32)

    for r in range(0, s, chunk):
        rows = slice(r, r + chunk)
        pre = nn(hid[rows, :], w1[...]) + b1[...].astype(F32)
        act, gp = gelu_pair(pre)
        act = act.astype(LOW)
        act_o[rows, :] = act
        gp_o[rows, :] = gp.astype(LOW)
        acc[rows, :] += nn(act, w2[...])

    @pl.when(f == pl.num_programs(0) - 1)
    def _():
        gain = g2[...].astype(F32)
        for r in range(0, s, chunk):
            rows = slice(r, r + chunk)
            normed, root = normalize(acc[rows, :])
            res = (normed * gain + s2[...].astype(F32)).astype(LOW)
            hid[rows, :] = res
            for j in range(per):
                outs[r // n + j][0:n, :] = res[j * n : j * n + n, :]
            acc[rows, :] = normed
            sb_o[rows, :] = jnp.broadcast_to(root, (chunk, d))
        start = pl.multiple_of(row0[0], 128)
        cls = hid[pl.ds(start, 16), :]
        pooled = jnp.tanh(nn(cls, wp[...]) + bp[...].astype(F32))
        pre = pu[...] * (1.0 - pooled * pooled)
        cls_grad = nt(pre.astype(LOW), wp[...])[:1]
        high = pooled[:1].astype(LOW).astype(F32)
        pool = [cls[:1].astype(F32), pre[:1], high, pooled[:1] - high, jnp.zeros((12, d), F32)]
        pool = jnp.concatenate(pool, axis=0).astype(LOW)
        for out in outs:
            out[n : n + 16, :] = pool
        gs, ss, bs = 0.0, 0.0, 0.0
        for r in range(0, s, chunk):
            rows = slice(r, r + chunk)
            ids = lax.broadcasted_iota(jnp.int32, (chunk, 1), 0) + r
            up = [u[...].astype(F32) for u in ups[r // chunk * per : r // chunk * per + per]]
            upstream = jnp.concatenate(up, axis=0) + jnp.where(ids == row0[0], cls_grad, 0.0)
            normed = acc[rows, :]
            back = normalize_back(upstream, normed, sb_o[rows, :1], gain)
            sb_o[rows, :] = back
            low = back.astype(LOW)
            ol_o[rows, :] = low
            gs = gs + jnp.sum(upstream * normed, axis=0, keepdims=True)
            ss = ss + jnp.sum(upstream, axis=0, keepdims=True)
            bs = bs + jnp.sum(low.astype(F32), axis=0, keepdims=True)
        live = row0[1].astype(F32)
        vec_o[0:1, :] = gs * live
        vec_o[1:2, :] = ss * live
        vec_o[2:3, :] = bs * live


def mid(row0, mixed, wo, bo, x, g1, s1, w1, b1, w2, b2, g2, s2, wp, bp, ups, pu, blk=768, chunk=256):
    s, d = x.shape
    ff = w1.shape[1]
    full, row = whole((s, d)), whole((1, d))
    fcol = pl.BlockSpec((s, blk), lambda f, *_: (0, f))
    return pl.pallas_call(
        functools.partial(mid_kernel, chunk=chunk),
        grid_spec=prefetch(
            1,
            (ff // blk,),
            [
                full, whole((d, d)), row, full, row, row,
                pl.BlockSpec((d, blk), lambda f, *_: (0, f)),
                pl.BlockSpec((1, blk), lambda f, *_: (0, f)),
                pl.BlockSpec((blk, d), lambda f, *_: (f, 0)),
                row, row, row, whole((d, d)), row,
            ]
            + [whole((s // 4, d))] * 4
            + [row],
            [full, whole((s, 1)), full, fcol, fcol]
            + [whole((s // 4 + 16, d))] * 4
            + [full, full, whole((8, d))],
            [pltpu.VMEM((s, d), LOW), pltpu.VMEM((s, d), F32)],
        ),
        out_shape=[
            struct((s, d), F32), struct((s, 1), F32), struct((s, d), LOW), struct((s, ff), LOW),
            struct((s, ff), LOW)]
        + [struct((s // 4 + 16, d), LOW)] * 4
        + [ struct((s, d), F32),
            struct((s, d), LOW), struct((8, d), F32),
        ],
        compiler_params=params(),
        cost_estimate=cost(2 * s * d * d + 4 * s * d * ff, 25e6),
        name="feed_forward",
    )(row0, mixed, wo, bo, x, g1, s1, w1, b1, w2, b2, g2, s2, wp, bp, *ups, pu)


def ff_bwd_kernel(ol, gp, w2, w1, sb, normed, root, g1, il_o, ib_o, fb_o, al_o, vec_o, acc, *, chunk):
    f = pl.program_id(0)
    s = ol.shape[0]
    bias = 0.0
    for r in range(0, s, chunk):
        rows = slice(r, r + chunk)
        low = (nt(ol[rows, :], w2[...]) * gp[rows, :].astype(F32)).astype(LOW)
        il_o[rows, :] = low
        bias = bias + jnp.sum(low.astype(F32), axis=0, keepdims=True)
        part = nt(low, w1[...])

        @pl.when(f == 0)
        def _():
            acc[rows, :] = part + sb[rows, :]

        @pl.when(f > 0)
        def _():
            acc[rows, :] += part
    ib_o[...] = bias

    @pl.when(f == pl.num_programs(0) - 1)
    def _():
        gs, ss, bs = 0.0, 0.0, 0.0
        gain = g1[...].astype(F32)
        for r in range(0, s, chunk):
            rows = slice(r, r + chunk)
            upstream = acc[rows, :]
            nrm = normed[rows, :].astype(F32)
            back = normalize_back(upstream, nrm, root[rows, :], gain)
            fb_o[rows, :] = back
            low = back.astype(LOW)
            al_o[rows, :] = low
            gs = gs + jnp.sum(upstream * nrm, axis=0, keepdims=True)
            ss = ss + jnp.sum(upstream, axis=0, keepdims=True)
            bs = bs + jnp.sum(low.astype(F32), axis=0, keepdims=True)
        vec_o[0:1, :] = gs
        vec_o[1:2, :] = ss
        vec_o[2:3, :] = bs


def ff_bwd(ol, gp, w2, w1, sb, normed, root, g1, blk=768, chunk=256):
    s, d = ol.shape
    ff = w1.shape[1]
    full, row = whole((s, d)), whole((1, d))
    fcol = pl.BlockSpec((s, blk), lambda f: (0, f))
    return pl.pallas_call(
        functools.partial(ff_bwd_kernel, chunk=chunk),
        grid=(ff // blk,),
        in_specs=[
            full, fcol, pl.BlockSpec((blk, d), lambda f: (f, 0)), pl.BlockSpec((d, blk), lambda f: (0, f)),
            full, full, whole((s, 1)), row,
        ],
        out_specs=[fcol, pl.BlockSpec((1, blk), lambda f: (0, f)), full, full, whole((8, d))],
        out_shape=[
            struct((s, ff), LOW), struct((1, ff), F32), struct((s, d), F32), struct((s, d), LOW), struct((8, d), F32),
        ],
        scratch_shapes=[pltpu.VMEM((s, d), F32)],
        compiler_params=params(),
        cost_estimate=cost(4 * s * d * ff, 22e6),
        name="feed_forward_backward",
    )(ol, gp, w2, w1, sb, normed, root, g1)


def tn(a, b):
    return lax.dot_general(a, b, (((0,), (0,)), ((), ())), preferred_element_type=F32)


def prefetch(count, grid, in_specs, out_specs, scratch=()):
    return pltpu.PrefetchScalarGridSpec(
        num_scalar_prefetch=count,
        grid=grid,
        in_specs=in_specs,
        out_specs=out_specs,
        scratch_shapes=list(scratch),
    )


def index_kernel(ids, req_o, col_o, row_o, *, rows, slots):
    count, n = ids.shape
    owners = req_o.shape[0]
    owner = ((ids[...].astype(F32) + 0.5) * (1.0 / rows)).astype(jnp.int32)
    local = ids[...] - owner * rows + 1
    flat = [owner.astype(F32), (local // 64).astype(F32), (local % 64).astype(F32)]
    flat = jnp.concatenate(flat + [jnp.zeros((16 - 3 * count, n), F32)], axis=0)
    cols = flat.T
    lane = lax.broadcasted_iota(jnp.int32, (n, owners), 1).astype(F32)
    before = lax.broadcasted_iota(jnp.int32, (n, n), 1) < lax.broadcasted_iota(jnp.int32, (n, n), 0)
    before = jnp.where(before, 1.0, 0.0).astype(LOW)
    seen = jnp.zeros((1, owners), F32)
    high, low, places = 0.0, 0.0, []
    slot_lane = lax.broadcasted_iota(jnp.int32, (n, 128), 1).astype(F32)
    for s in range(count):
        hot = jnp.where(lane == cols[:, s : s + 1], 1.0, 0.0)
        hot_low = hot.astype(LOW)
        within = jnp.sum((nn(before, hot_low) + seen) * hot, axis=1, keepdims=True)
        seen = seen + jnp.sum(hot, axis=0, keepdims=True)
        place = cols[:, s : s + 1] * slots + within
        places.append(place)
        here = slot_lane == within
        put_high = jnp.where(here, cols[:, count + s : count + s + 1], 0.0).astype(LOW)
        put_low = jnp.where(here, cols[:, 2 * count + s : 2 * count + s + 1], 0.0).astype(LOW)
        high = high + tn(hot_low, put_high)
        low = low + tn(hot_low, put_low)
    req_o[...] = (high * 64.0 + low).astype(jnp.int32)[:, :slots] - 1
    places.append(jnp.full((n, 1), -1.0, F32))
    table = jnp.concatenate([jnp.broadcast_to(p, (n, 8)) for p in places], axis=1)
    table = jnp.concatenate([table, jnp.zeros((n, 128 - table.shape[1]), F32)], axis=1)
    turned = table.T.astype(jnp.int32)
    for s in range(count + 1):
        col_o[s] = places[s].astype(jnp.int32)
        row_o[s] = turned[8 * s : 8 * s + 1, :]


def index_requests(ids, rows, owners, slots):
    count, n = ids.shape
    return pl.pallas_call(
        functools.partial(index_kernel, rows=rows, slots=slots),
        grid=(1,),
        in_specs=[whole((count, n))],
        out_specs=[whole((owners, slots)), whole((count + 1, n, 1)), whole((count + 1, 1, n))],
        out_shape=[
            struct((owners, slots), jnp.int32),
            struct((count + 1, n, 1), jnp.int32),
            struct((count + 1, 1, n), jnp.int32),
        ],
        compiler_params=params(),
        cost_estimate=cost(0, 1e6),
        name="index_requests",
    )(ids)


def gather_kernel(fetch, table, out, acc, *, rows):
    step = pl.program_id(0)
    last = pl.num_programs(0) - 1
    blk = table.shape[0]
    ids = lax.broadcasted_iota(jnp.int32, (1, blk), 1) + step * blk
    hot = jnp.where(ids == fetch[...], 1.0, 0.0).astype(LOW)

    def add(block):
        part = nn(hot, block)

        @pl.when(step == 0)
        def _():
            acc[...] = part

        @pl.when(step > 0)
        def _():
            acc[...] += part

    @pl.when(step < last)
    def _():
        add(table[...])

    @pl.when(step == last)
    def _():
        ids_col = lax.broadcasted_iota(jnp.int32, (blk, 1), 0) + step * blk
        add(jnp.where(ids_col < rows, table[...], jnp.zeros((), LOW)))
        out[...] = acc[...].astype(LOW)


def gather_rows(fetch, table, blk=1024):
    slots = fetch.shape[0]
    rows, d = table.shape
    return pl.pallas_call(
        functools.partial(gather_kernel, rows=rows),
        grid=(pl.cdiv(rows, blk),),
        in_specs=[whole((slots, 1)), pl.BlockSpec((blk, d), lambda i: (i, 0))],
        out_specs=whole((slots, d)),
        out_shape=struct((slots, d), LOW),
        scratch_shapes=[pltpu.VMEM((slots, d), F32)],
        compiler_params=params(),
        cost_estimate=cost(2 * slots * rows * d, 8e6),
        name="gather_rows",
    )(fetch, table)


def embed_kernel(place, slot, replies, pos, o0, o1, o2, o3):
    ids = lax.broadcasted_iota(jnp.int32, (1, replies.shape[0]), 1)
    for m, out in enumerate((o0, o1, o2, o3)):
        sent = (place[0] + m) % 4
        hot = jnp.where(ids == slot[sent], 1.0, 0.0).astype(LOW)
        live = jnp.where(sent < 3, 1.0, 0.0)
        out[...] = ((nn(hot, replies[...]) + pos[...].astype(F32)) * live).astype(LOW)


def embed_parts(place, slot, replies, pos):
    slots, d = replies.shape
    n = pos.shape[0]
    out = pl.BlockSpec((n, d), lambda i, p: (0, 0))
    return pl.pallas_call(
        embed_kernel,
        grid_spec=prefetch(
            1,
            (1,),
            [whole((4, n, 1)), whole((slots, d)), whole((n, d))],
            [out] * 4,
        ),
        out_shape=[struct((n, d), LOW)] * 4,
        compiler_params=params(),
        cost_estimate=cost(2 * slots * 4 * n * d, 3e6),
        name="embed_parts",
    )(place, slot, replies, pos)


def outgoing_kernel(place, slot, p0, p1, p2, p3, out):
    ids = lax.broadcasted_iota(jnp.int32, (out.shape[0], 1), 0)
    total = 0.0
    for m, part in enumerate((p0, p1, p2, p3)):
        sent = (place[0] + m) % 4
        hot = jnp.where(ids == slot[sent], 1.0, 0.0).astype(LOW)
        total = total + nn(hot, part[...])
    out[...] = total.astype(LOW)


def outgoing_rows(place, slot, parts, slots):
    n, d = parts[0].shape
    return pl.pallas_call(
        outgoing_kernel,
        grid_spec=prefetch(
            1, (1,), [whole((4, 1, n))] + [whole((n, d))] * 4, whole((slots, d))
        ),
        out_shape=struct((slots, d), LOW),
        compiler_params=params(),
        cost_estimate=cost(2 * slots * 4 * n * d, 3e6),
        name="outgoing_rows",
    )(place, slot, *parts)


def table_kernel(fetch, incoming, out):
    blk = out.shape[0]
    ids = lax.broadcasted_iota(jnp.int32, (blk, 1), 0) + pl.program_id(0) * blk
    out[...] = nn(jnp.where(ids == fetch[...], 1.0, 0.0).astype(LOW), incoming[...])


def table_grad(fetch, incoming, rows, blk=1024):
    slots, d = incoming.shape
    return pl.pallas_call(
        table_kernel,
        grid=(pl.cdiv(rows, blk),),
        in_specs=[whole((1, slots)), whole((slots, d))],
        out_specs=pl.BlockSpec((blk, d), lambda i: (i, 0)),
        out_shape=struct((rows, d), F32),
        compiler_params=params(),
        cost_estimate=cost(2 * slots * rows * d, 13e6),
        name="table_gradient",
    )(fetch, incoming)


def unpermute_kernel(place, p0, p1, p2, p3, out):
    for m, part in enumerate((p0, p1, p2, p3)):
        sent = (place[0] + m) % 4

        @pl.when(sent < 3)
        def _():
            out[sent] = part[...]


def unpermute(place, parts, n):
    d = parts[0].shape[1]
    return pl.pallas_call(
        unpermute_kernel,
        grid_spec=prefetch(1, (1,), [whole((n, d))] * 4, whole((3, n, d))),
        out_shape=struct((3, n, d), parts[0].dtype),
        compiler_params=params(),
        cost_estimate=cost(0, 2e6),
        name="unpermute",
    )(place, *parts)


def outer_grad_kernel(act, ol, out, acc):
    z = pl.program_id(0)
    acc[...] = tn(act[...], ol[...])
    rows = out.shape[2]
    for b in range(out.shape[0]):
        out[b, z] = acc[b * rows : b * rows + rows, :].astype(LOW)


def outer_grad(act, ol, places):
    s, ff = act.shape
    d = ol.shape[1]
    blk = ff // 4
    return pl.pallas_call(
        outer_grad_kernel,
        grid=(4,),
        in_specs=[pl.BlockSpec((s, blk), lambda z: (0, z)), whole((s, d))],
        out_specs=whole((places, 4, blk // places, d)),
        out_shape=struct((places, 4, blk // places, d), LOW),
        scratch_shapes=[pltpu.VMEM((blk, d), F32)],
        compiler_params=params(),
        cost_estimate=cost(2 * s * ff * d, 9e6),
        name="outer_grad",
    )(act, ol)


def spread_kernel(place, src, o0, o1, o2, o3):
    for m, out in enumerate((o0, o1, o2, o3)):
        out[...] = src[(place[0] + m) % 4]


def spread(place, src):
    shape = src.shape[1:]
    return pl.pallas_call(
        spread_kernel,
        grid_spec=prefetch(1, (1,), [whole(src.shape)], [whole(shape)] * 4),
        out_shape=[struct(shape, src.dtype)] * 4,
        compiler_params=params(),
        cost_estimate=cost(0, 1e6),
        name="spread",
    )(place, src)


INNER_ROWS = 256


def inner_block(hid, il, wo_acc, index, put):
    put(slice(0, 192), tn(hid[...], il[...]).reshape(4, 192, HALF))
    start = pl.multiple_of(index * 48, 16)
    put(slice(192, 240), jnp.stack([wo_acc[pl.ds(192 * z + start, 48), :] for z in range(4)]))
    put(slice(240, 256), jnp.zeros((4, 16, HALF), F32))


def inner_send_kernel(half, hid, il, mixed, al, out, wo_acc):
    step = pl.program_id(0)

    @pl.when(step == 0)
    def _():
        wo_acc[...] = tn(mixed[...], al[...])

    def put(rows, value):
        out[0, :, rows, :] = value.astype(LOW)

    inner_block(hid, il, wo_acc, step, put)


def inner_send(half, hid, il, mixed, al):
    s, d = hid.shape
    return pl.pallas_call(
        inner_send_kernel,
        grid_spec=prefetch(
            1,
            (4,),
            [
                whole((s, d)),
                pl.BlockSpec((s, HALF), lambda i, h: (0, h[0] * 4 + i)),
                whole((s, d)),
                pl.BlockSpec((s, HALF), lambda i, h: (0, h[0])),
            ],
            pl.BlockSpec((1, 4, INNER_ROWS, HALF), lambda i, h: (i, 0, 0, 0)),
            [pltpu.VMEM((d, HALF), F32)],
        ),
        out_shape=struct((4, 4, INNER_ROWS, HALF), LOW),
        compiler_params=params(),
        cost_estimate=cost(2 * s * d * 5 * HALF, 7e6),
        name="inner_send",
    )(half, hid, il, mixed, al)


def inner_keep_kernel(half, hid, il, mixed, al, got, out, wo_acc):
    step = pl.program_id(0)

    @pl.when(step == 0)
    def _():
        wo_acc[...] = tn(mixed[...], al[...])

    def put(rows, value):
        value = value + got[0, :, rows, :].astype(F32)
        for x in range(rows.start // 64, -(-rows.stop // 64)):
            low, high = max(rows.start, 64 * x), min(rows.stop, 64 * x + 64)
            part = value[:, low - rows.start : high - rows.start, :].astype(LOW)
            for z in range(4):
                out[(step * 4 + x) * 4 + z, low - 64 * x : high - 64 * x, :] = part[z]

    inner_block(hid, il, wo_acc, step, put)


def inner_keep(half, hid, il, mixed, al, got):
    s, d = hid.shape
    return pl.pallas_call(
        inner_keep_kernel,
        grid_spec=prefetch(
            1,
            (4,),
            [
                whole((s, d)),
                pl.BlockSpec((s, HALF), lambda i, h: (0, h[0] * 4 + i)),
                whole((s, d)),
                pl.BlockSpec((s, HALF), lambda i, h: (0, h[0])),
                pl.BlockSpec((1, 4, INNER_ROWS, HALF), lambda i, h: (i, 0, 0, 0)),
            ],
            whole((64, 64, HALF)),
            [pltpu.VMEM((d, HALF), F32)],
        ),
        out_shape=struct((64, 64, HALF), LOW),
        compiler_params=params(),
        cost_estimate=cost(2 * s * d * 5 * HALF, 10e6),
        name="inner_keep",
    )(half, hid, il, mixed, al, got)


def extra_kernel(place, p0, p1, p2, p3, vec2, vec1, ib, qb, vb, send, keep, eg):
    core, z = place[0], place[1]
    n = p0.shape[0]
    for m, part in enumerate((p0, p1, p2, p3)):
        eg[m] = part[...]
    for out, half in ((send, 1 - core), (keep, core)):
        cols = pl.ds(pl.multiple_of(half * HALF, 128), HALF)
        rows = [
            qb[:, cols],
            vb[:, cols],
            vec1[2:3, cols],
            vec1[0:1, cols],
            vec1[1:2, cols],
            vec2[2:3, cols],
            vec2[0:1, cols],
            vec2[1:2, cols],
        ]
        for j in range(4):
            rows.append(ib[:, pl.ds(pl.multiple_of(half * HALF + 768 * j, 128), HALF)])
        vec = jnp.concatenate(rows + [jnp.zeros((192 - n - 12, HALF), F32)], axis=0).astype(LOW)
        for j in range(4):
            out[j, 0:n, :] = eg[(z + 4 - j) % 4, :, cols]
            out[j, n:192, :] = vec


def extra_rows(place, parts, vec2, vec1, ib, qb, vb):
    n, d = parts[0].shape
    row = whole((1, d))
    out = whole((4, 192, HALF))
    return pl.pallas_call(
        extra_kernel,
        grid_spec=prefetch(
            1,
            (1,),
            [whole((n, d))] * 4
            + [whole((8, d)), whole((8, d)), whole(ib.shape), row, row],
            [out] * 2,
            [pltpu.VMEM((4, n, d), LOW)],
        ),
        out_shape=[struct((4, 192, HALF), LOW)] * 2,
        compiler_params=params(),
        cost_estimate=cost(0, 3e6),
        name="extra_rows",
    )(place, *parts, vec2, vec1, ib, qb, vb)


def core_add_kernel(place, mats, got, own, more, o0, o1, o2, o3, acc):
    acc[0:3] = (mats[...].astype(F32) + got[...].astype(F32)).astype(LOW)
    acc[3] = (own[...].astype(F32) + more[...].astype(F32)).astype(LOW)
    for m, out in enumerate((o0, o1, o2, o3)):
        out[...] = acc[(place[0] + m) % 4]


def core_add(place, mats, got, own, more):
    shape = own.shape
    return pl.pallas_call(
        core_add_kernel,
        grid_spec=prefetch(
            1,
            (1,),
            [whole(mats.shape)] * 2 + [whole(shape)] * 2,
            [whole(shape)] * 4,
            [pltpu.VMEM((4,) + shape, LOW)],
        ),
        out_shape=[struct(shape, LOW)] * 4,
        compiler_params=params(),
        cost_estimate=cost(0, 8e6),
        name="core_add",
    )(place, mats, got, own, more)


def add4(a, b, c, d):
    return a[...].astype(F32) + b[...].astype(F32) + c[...].astype(F32) + d[...].astype(F32)


def ring_add_kernel(place, p0, p1, p2, p3, o0, o1, o2, o3, acc):
    acc[...] = add4(p0, p1, p2, p3)
    for m, out in enumerate((o0, o1, o2, o3)):
        out[...] = acc[(place[0] + m) % 4].astype(LOW)


def ring_add(place, parts):
    shape = parts[0].shape
    return pl.pallas_call(
        ring_add_kernel,
        grid_spec=prefetch(
            1, (1,), [whole(shape)] * 4, [whole(shape[1:])] * 4, [pltpu.VMEM(shape, F32)]
        ),
        out_shape=[struct(shape[1:], LOW)] * 4,
        compiler_params=params(),
        cost_estimate=cost(0, 8 * shape[0] * shape[1] * shape[2]),
        name="ring_add",
    )(place, *parts)


def sum_copies_kernel(p0, p1, p2, p3, out):
    out[...] = jnp.broadcast_to(add4(p0, p1, p2, p3).astype(LOW)[None], out.shape)


def sum_copies(parts, copies):
    shape = parts[0].shape
    return pl.pallas_call(
        sum_copies_kernel,
        grid=(1,),
        in_specs=[whole(shape)] * 4,
        out_specs=whole((copies,) + shape),
        out_shape=struct((copies,) + shape, LOW),
        compiler_params=params(),
        cost_estimate=cost(0, 2e6),
        name="sum_copies",
    )(*parts)


def piece_kernel(parts, a0, a1, a2, a3, r0, r1, r2, r3, out, acc):
    step = pl.program_id(0)
    total = parts[0].astype(F32)
    for i in range(1, parts.shape[0]):
        total = total + parts[i].astype(F32)

    @pl.when(step == 0)
    def _():
        acc[...] = total

    @pl.when(step > 0)
    def _():
        acc[...] += total

    @pl.when(step == pl.num_programs(0) - 1)
    def _():
        outer = add4(a0, a1, a2, a3)
        pool = []
        for part in (r0, r1, r2, r3):
            two = part[...].astype(F32)
            pool += [two[r : r + 1, c * HALF : c * HALF + HALF] for r in range(2) for c in range(2)]
        rows = [outer[:, 0:HALF], outer[:, HALF:], acc[...]] + pool
        out[...] = jnp.concatenate(rows, axis=0).astype(LOW)


def piece_rows(parts, outer, pool):
    count, rows, wide = parts.shape
    return pl.pallas_call(
        piece_kernel,
        grid=(4,),
        in_specs=[pl.BlockSpec((count // 4, rows, wide), lambda i: (i, 0, 0))]
        + [whole(p.shape) for p in outer]
        + [pl.BlockSpec((16, p.shape[1]), lambda i: (8, 0)) for p in pool],
        out_specs=whole((128, wide)),
        out_shape=struct((128, wide), LOW),
        scratch_shapes=[pltpu.VMEM((rows, wide), F32)],
        compiler_params=params(),
        cost_estimate=cost(0, 6e6),
        name="piece_rows",
    )(parts, *outer, *pool)


def finish_ff_kernel(place, g, outer_o, inner_o, out_o, pw_o, pb_o, acc):
    for y in range(4):
        for x in range(4):
            for c in range(2):
                b = (y * 4 + x) * 2 + c
                src = g.at[b]
                cols = slice(c * HALF, c * HALF + HALF)
                outer = src[0:48, :].astype(F32)
                outer_o[24 * b : 24 * b + 24, 0:HALF] = outer[0:24]
                outer_o[24 * b : 24 * b + 24, HALF:] = outer[24:48]
                if x < 3:
                    wide = slice(c * 4 * HALF + y * HALF, c * 4 * HALF + y * HALF + HALF)
                    inner_o[x * 64 : x * 64 + 64, wide] = src[48:112, :].astype(F32)
                else:
                    out_o[y * 48 : y * 48 + 48, cols] = src[48:96, :].astype(F32)
    pool = g[:, 112:128, :].astype(F32)
    cls, pre = [], []
    for m in range(4):
        cls.append(jnp.concatenate([pool[:, 4 * m, :], pool[:, 4 * m + 1, :]], axis=1))
        pre.append(jnp.concatenate([pool[:, 4 * m + 2, :], pool[:, 4 * m + 3, :]], axis=1))
    cls = jnp.concatenate(cls, axis=0)
    pre = jnp.concatenate(pre, axis=0)
    acc[...] = tn(cls.astype(LOW), pre.astype(LOW))
    pw_o[...] = acc[pl.ds(pl.multiple_of(place[0] * 192, 192), 192), :]
    pb_o[...] = jnp.sum(pre, axis=0, keepdims=True)


def finish_ff(place, g):
    shapes = [(768, 768), (192, 3072), (192, 768), (192, 768), (1, 768)]
    return pl.pallas_call(
        finish_ff_kernel,
        grid_spec=prefetch(
            1,
            (1,),
            [whole(g.shape)],
            [whole(s) for s in shapes],
            [pltpu.VMEM((768, 768), F32)],
        ),
        out_shape=[struct(s, F32) for s in shapes],
        compiler_params=params(),
        cost_estimate=cost(0, 9e6),
        name="finish_ff",
    )(place, g)


def finish_rest_kernel(g, q_o, k_o, v_o, pos_o, vec_o):
    for y in range(4):
        for x in range(4):
            for c in range(2):
                src = g[(y * 4 + x) * 2 + c].astype(F32)
                cols = slice(c * HALF, c * HALF + HALF)
                r = 48 * y
                if x < 3:
                    (q_o, k_o, v_o)[x][r : r + 48, cols] = src
                elif y < 2:
                    pos_o[r : r + 48, cols] = src
                elif y == 2:
                    pos_o[96:128, cols] = src[0:32]
                    vec_o[0:16, cols] = src[32:48]


def finish_rest(g):
    shapes = [(192, 768)] * 3 + [(128, 768), (16, 768)]
    return pl.pallas_call(
        finish_rest_kernel,
        grid=(1,),
        in_specs=[whole(g.shape)],
        out_specs=[whole(s) for s in shapes],
        out_shape=[struct(s, F32) for s in shapes],
        compiler_params=params(),
        cost_estimate=cost(0, 4e6),
        name="finish_rest",
    )(g)


def pooled_kernel(place, p0, p1, p2, p3, out):
    for m, part in enumerate((p0, p1, p2, p3)):
        two = part[...].astype(F32)
        row = two[2:3] + two[3:4]
        out[(place[0] + m) % 4] = pltpu.roll(
            jnp.broadcast_to(row, (8, row.shape[1])), row.shape[1] - 192 * place[0], 1
        )


def pooled_rows(place, parts):
    d = parts[0].shape[1]
    below = pl.BlockSpec((16, d), lambda i, p: (8, 0))
    return pl.pallas_call(
        pooled_kernel,
        grid_spec=prefetch(1, (1,), [below] * 4, whole((4, 8, d))),
        out_shape=struct((4, 8, d), F32),
        compiler_params=params(),
        name="pooled_rows",
    )(place, *parts)


def shift_x(array, step):
    pairs = []
    for y in range(4):
        for x in range(4):
            for c in range(2):
                pairs.append(((y * 4 + x) * 2 + c, (y * 4 + (x + step) % 4) * 2 + c))
    return lax.ppermute(array, "batch", pairs)


def shift_y(array, step):
    pairs = []
    for y in range(4):
        for x in range(4):
            for c in range(2):
                pairs.append(((y * 4 + x) * 2 + c, (((y + step) % 4) * 4 + x) * 2 + c))
    return lax.ppermute(array, "batch", pairs)


def shift_z(array, step):
    return lax.ppermute(array, "seq", [(z, (z + step) % 4) for z in range(4)])


def swap_core(array):
    return lax.ppermute(array, "batch", [(i, i ^ 1) for i in range(32)])


def ring_send(parts, shift):
    return [parts[0], shift(parts[1], 1), shift(parts[2], 2), shift(parts[3], 3)]


SAME_CORE = [[(p * 2 + core) * 4 + z for p in range(16) for z in range(4)] for core in range(2)]


def exchange(blocks):
    return lax.all_to_all(
        blocks,
        ("batch", "seq"),
        split_axis=0,
        concat_axis=0,
        tiled=True,
        axis_index_groups=SAME_CORE,
    )


def to_sentence(parts):
    out = [parts[0]]
    for step in (1, 2, 3):
        pairs = [(z, (z + step) % 4) for z in range(4) if (z + step) % 4 < 3]
        out.append(lax.ppermute(parts[step], "seq", pairs))
    return out


def from_sentence(parts):
    out = [parts[0]]
    for step in (1, 2, 3):
        pairs = [((z + step) % 4, z) for z in range(4) if (z + step) % 4 < 3]
        out.append(lax.ppermute(parts[step], "seq", pairs))
    return out


def tie(array, *after):
    return lax.optimization_barrier((array,) + after)[0]


def per_device(
    token_ids,
    lengths,
    word_table,
    positions,
    query_weight,
    key_weight,
    value_weight,
    query_bias,
    value_bias,
    output_weight,
    output_bias,
    first_gain,
    first_shift,
    inner_weight,
    inner_bias,
    outer_weight,
    outer_bias,
    second_gain,
    second_shift,
    pooler_weight,
    pooler_bias,
    out_grad,
    pooled_grad,
):
    num_sent, local_len = token_ids.shape
    table_rows, width = word_table.shape
    all_count = lax.axis_size("seq") * lax.axis_size("batch")
    z = lax.axis_index("seq")
    batch_place = lax.axis_index("batch")
    core = batch_place % 2
    x = (batch_place // 2) % 4
    y = batch_place // 8

    def scalars(*values):
        return jnp.stack([jnp.asarray(v, jnp.int32) for v in values])

    slots = 2 * num_sent * local_len // all_count
    all_slots = slots * all_count
    requests, slot_cols, slot_rows = index_requests(token_ids, table_rows, all_count, slots)
    arrived = lax.all_to_all(requests, ("batch", "seq"), split_axis=0, concat_axis=0, tiled=True)
    fetch = arrived.reshape(-1)
    found = gather_rows(fetch[:, None], word_table)
    replies = lax.all_to_all(
        found.reshape(all_count, slots, width),
        ("batch", "seq"),
        split_axis=0,
        concat_axis=0,
        tiled=True,
    ).reshape(all_slots, width)
    live = (z < 3).astype(jnp.int32)
    sentence = jnp.minimum(z, 2)

    def rows_for(array, m):
        return lax.dynamic_index_in_dim(array, jnp.minimum((z + m) % 4, 2), 0, keepdims=False)

    ups = [rows_for(out_grad, m) for m in range(4)]
    ups = to_sentence([jnp.where(z < 3, ups[0], jnp.zeros((), LOW))] + ups[1:])
    pulls = [rows_for(pooled_grad, m)[None] for m in range(4)]
    pulls = to_sentence([jnp.where(z < 3, pulls[0], 0.0)] + pulls[1:])
    pulls = jnp.concatenate(pulls[::-1] + pulls[::-1])
    pulls = lax.dynamic_slice_in_dim(pulls, (3 - z) % 4, 4, 0).reshape(1, width)

    def row(vector):
        return vector.reshape(1, -1)

    vectors = (
        query_bias,
        value_bias,
        output_bias,
        first_gain,
        first_shift,
        inner_bias,
        outer_bias,
        second_gain,
        second_shift,
        pooler_bias,
    )
    block_of = (z - jnp.arange(4, dtype=jnp.int32)) % 4
    place_of = block_of[:, None] * local_len + jnp.arange(local_len, dtype=jnp.int32)[None, :]
    live_keys = (place_of.reshape(-1, 1) < lengths[sentence]).astype(F32)

    early = [live_keys, pulls] + [row(v) for v in vectors] + ups
    replies, *early = lax.optimization_barrier([replies] + early)
    live_keys, pulls = early[:2]
    q_bias, v_bias, o_bias, gain1, shift1, in_bias, out_bias, gain2, shift2, pool_bias = early[2:12]
    ups = early[12:]
    embeds = to_sentence(embed_parts(scalars(z), slot_cols, replies, positions))

    embed, query, key, value, expo, inverse, mixed_t, mixed = attn_fwd(
        embeds, query_weight, key_weight, value_weight, q_bias, v_bias, live_keys
    )
    normed, root, hidden, active, slope, *result, second_back, outer_low, vec2 = mid(
        scalars(sentence * local_len, live),
        mixed,
        output_weight,
        o_bias,
        embed,
        gain1,
        shift1,
        inner_weight,
        in_bias,
        outer_weight,
        out_bias,
        gain2,
        shift2,
        pooler_weight,
        pool_bias,
        ups,
        pulls,
    )
    other = scalars(1 - core)

    outer_blocks = outer_grad(active, outer_low, lax.axis_size("batch"))
    outer_low = tie(outer_low, outer_blocks)
    outer_sum = lax.psum_scatter(
        outer_blocks.reshape(-1, width), "batch", scatter_dimension=0, tiled=True
    )
    result = from_sentence(result)
    inner_low, inner_bias_grad, first_back, attention_low, vec1 = ff_bwd(
        outer_low, slope, outer_weight, inner_weight, second_back, normed, root, gain1
    )

    inner_other = inner_send(other, tie(hidden, *result), inner_low, mixed, attention_low)
    inner_got = swap_core(inner_other)
    own = scalars(core)
    inner_blocks = inner_keep(own, hidden, inner_low, mixed, attention_low, inner_got)
    attention_low = tie(attention_low, inner_blocks)
    inner_blocks = exchange(inner_blocks)
    *embed_grad, rest_other, rest_own, qb_grad, vb_grad = attn_bwd(
        own,
        attention_low,
        output_weight,
        query,
        key,
        value,
        expo,
        inverse,
        mixed_t,
        query_weight,
        key_weight,
        value_weight,
        embed,
        first_back,
    )

    returned = from_sentence(embed_grad)
    rest_got = swap_core(rest_other)
    extra_other, extra_own = extra_rows(
        scalars(core, z), embed_grad, vec2, vec1, inner_bias_grad, qb_grad, vb_grad
    )
    rest_parts = core_add(scalars(x), rest_own, rest_got, extra_own, swap_core(extra_other))
    result, returned[0] = lax.optimization_barrier((result, tie(returned[0], rest_parts[0])))
    rest_parts = ring_send(rest_parts, shift_x)
    pooled = pooled_rows(scalars(z), result)[:num_sent, 0, : width // 4]
    hidden_out = unpermute(scalars(z), result, local_len)
    returned[0] = tie(returned[0], pooled, hidden_out)
    outgoing = outgoing_rows(scalars(z), slot_rows, returned, all_slots)
    outer_parts = spread(scalars(z), tie(outer_sum, outgoing).reshape(4, -1, width))
    outer_parts = ring_send(outer_parts, shift_z)
    incoming = lax.all_to_all(
        outgoing.reshape(all_count, slots, width),
        ("batch", "seq"),
        split_axis=0,
        concat_axis=0,
        tiled=True,
    ).reshape(all_slots, width)
    outer_parts[0] = tie(outer_parts[0], *rest_parts)
    piece = piece_rows(inner_blocks, outer_parts, result)
    gathered = lax.all_gather(piece, "batch", axis=0, tiled=False)
    rest_parts[0] = tie(rest_parts[0], piece)
    rest_parts = ring_send(ring_add(scalars(z), rest_parts), shift_z)
    grad_table = table_grad(fetch[None, :], incoming, table_rows)
    rest_parts = [p.reshape(4, -1, HALF) for p in rest_parts]
    rest_parts[0] = tie(rest_parts[0], grad_table)
    rest_parts = ring_send(ring_add(scalars(y), rest_parts), shift_y)
    rest = sum_copies(rest_parts, lax.axis_size("batch"))
    rest = lax.all_to_all(rest, "batch", split_axis=0, concat_axis=0, tiled=True)
    grad_query, grad_key, grad_value, grad_positions, vectors = finish_rest(rest)
    grad_outer, grad_inner, grad_output, grad_pooler, pooler_bias_grad = finish_ff(
        scalars(z), gathered
    )

    share = width // 4
    mine = lax.dynamic_slice_in_dim(vectors[:8], z * share, share, 1)
    ff = inner_weight.shape[1]
    inner_bias_sum = lax.dynamic_slice_in_dim(vectors[8:12].reshape(-1), z * ff // 4, ff // 4, 0)
    pooler_bias_sum = lax.dynamic_slice_in_dim(pooler_bias_grad[0], z * share, share, 0)
    return (
        hidden_out,
        pooled,
        grad_table,
        grad_positions,
        grad_query,
        grad_key,
        grad_value,
        mine[0],
        mine[1],
        grad_output,
        mine[2],
        mine[3],
        mine[4],
        grad_inner,
        inner_bias_sum,
        grad_outer,
        mine[5],
        mine[6],
        mine[7],
        grad_pooler,
        pooler_bias_sum,
    )


def solution(mesh):
    in_specs = (
        P("batch", "seq"),
        P("batch"),
        P(("batch", "seq"), None),
        P("seq", None),
        P(),
        P(),
        P(),
        P(),
        P(),
        P(),
        P(),
        P(),
        P(),
        P(),
        P(),
        P(),
        P(),
        P(),
        P(),
        P(),
        P(),
        P("batch", "seq", None),
        P("batch", "seq"),
    )
    out_specs = (
        P("batch", "seq", None),
        P("batch", "seq"),
        P(("batch", "seq"), None),
        P("seq", None),
        P("seq", None),
        P("seq", None),
        P("seq", None),
        P("seq"),
        P("seq"),
        P("seq", None),
        P("seq"),
        P("seq"),
        P("seq"),
        P("seq", None),
        P("seq"),
        P("seq", None),
        P("seq"),
        P("seq"),
        P("seq"),
        P("seq", None),
        P("seq"),
    )
    return jax.shard_map(
        per_device, mesh=mesh, in_specs=in_specs, out_specs=out_specs, check_vma=False
    )
```

```python
import functools
import jax
import jax.numpy as jnp
from jax import lax
from jax.experimental import pallas as pl
from jax.experimental.pallas import tpu as pltpu
from jax.sharding import PartitionSpec as P

F32 = jnp.float32
LOW = jnp.bfloat16
EPSILON = 1e-12
MASKED = -1000000000.0
HEAD_DIM = 64
VMEM = 56 * 1024 * 1024
HALF = 384
SHARE = 0.02


def nn(a, b):
    return lax.dot_general(a, b, (((1,), (0,)), ((), ())), preferred_element_type=F32)


def nt(a, b):
    return lax.dot_general(a, b, (((1,), (1,)), ((), ())), preferred_element_type=F32)


def struct(shape, dtype):
    return jax.ShapeDtypeStruct(shape, dtype)


def whole(shape):
    zeros = (0,) * len(shape)
    return pl.BlockSpec(shape, lambda *_: zeros, pipeline_mode=pl.Buffered(1))


def cost(flops, size):
    return pl.CostEstimate(
        flops=int(flops * SHARE), bytes_accessed=int(size * SHARE), transcendentals=0
    )


def params(**kw):
    return pltpu.CompilerParams(vmem_limit_bytes=VMEM, **kw)


def attn_fwd_kernel(
    x0, x1, x2, x3, wq, wk, wv, bq, bv, live, x_o, q_o, k_o, v_o, e_o, inv_o, mt_o, mixed_o, x
):
    scale = HEAD_DIM ** (-0.5)
    n = x0.shape[0]

    @pl.when(pl.program_id(0) == 0)
    def _():
        for m, part in enumerate((x0, x1, x2, x3)):
            x[m * n : m * n + n, :] = part[...]
            x_o[m * n : m * n + n, :] = part[...]

    q = ((nn(x[...], wq[...]) + bq[...].astype(F32)) * scale).astype(LOW)
    q_o[...] = q
    k = nn(x[...], wk[...]).astype(LOW)
    k_o[...] = k
    v = nn(x[...], wv[...]) + bv[...].astype(F32)
    v_o[...] = v.astype(LOW)
    keep = live[...] > 0.0
    lane = lax.broadcasted_iota(jnp.int32, (1, 128), 1)
    for pair in range(q.shape[1] // 128):
        cols = slice(128 * pair, 128 * pair + 128)
        q2, k2 = q[:, cols], k[:, cols]
        vt = v[:, cols].T.astype(LOW)
        parts = []
        for h in range(2):
            kz = jnp.where((lane // 64) == h, k2, jnp.zeros((), LOW))
            s = nt(kz, q2)
            s = jnp.where(keep, s, MASKED)
            e = jnp.exp(s - jnp.max(s, axis=0, keepdims=True))
            inv = 1.0 / jnp.sum(e, axis=0, keepdims=True)
            eb = e.astype(LOW)
            e_o[2 * pair + h] = eb
            inv_o[2 * pair + h] = inv
            parts.append(nn(vt[64 * h : 64 * h + 64], eb) * inv)
        mt = jnp.concatenate(parts, axis=0)
        mt_o[cols, :] = mt.astype(LOW)
        mixed_o[:, cols] = mt.T.astype(LOW)


def attn_fwd(parts, wq, wk, wv, bq, bv, live, group=256):
    n, d = parts[0].shape
    s = 4 * n
    hg = group // HEAD_DIM
    col = pl.BlockSpec((s, group), lambda h: (0, h))
    wcol = pl.BlockSpec((d, group), lambda h: (0, h))
    brow = pl.BlockSpec((1, group), lambda h: (0, h))
    heads = d // HEAD_DIM
    return pl.pallas_call(
        attn_fwd_kernel,
        grid=(d // group,),
        in_specs=[whole((n, d))] * 4 + [wcol, wcol, wcol, brow, brow, whole((s, 1))],
        out_specs=[
            whole((s, d)),
            col,
            col,
            col,
            pl.BlockSpec((hg, s, s), lambda h: (h, 0, 0)),
            pl.BlockSpec((hg, 1, s), lambda h: (h, 0, 0)),
            pl.BlockSpec((group, s), lambda h: (h, 0)),
            col,
        ],
        out_shape=[
            struct((s, d), LOW),
            struct((s, d), LOW),
            struct((s, d), LOW),
            struct((s, d), LOW),
            struct((heads, s, s), LOW),
            struct((heads, 1, s), F32),
            struct((d, s), LOW),
            struct((s, d), LOW),
        ],
        scratch_shapes=[pltpu.VMEM((s, d), LOW)],
        compiler_params=params(),
        cost_estimate=cost(6 * s * d * d + 4 * s * s * 256 * heads, 16e6),
        name="attention_forward",
    )(*parts, wq, wk, wv, bq, bv, live)


def attn_bwd_heads(al, wo, q, k, v, e_i, inv_i, mt_i, dm, dq, dk, dv):
    step = pl.program_id(0)

    @pl.when(step == 0)
    def _():
        dm[...] = nt(al[...], wo[...]).astype(LOW)

    lane = lax.broadcasted_iota(jnp.int32, (1, 128), 1)
    cols = pl.ds(pl.multiple_of(step * 128, 128), 128)
    q2, k2, v2 = q[...], k[...], v[...]
    dmt = dm[:, cols].astype(F32).T
    kt = k2.astype(F32).T.astype(LOW)
    prod = dmt * mt_i[...].astype(F32)
    inv2 = [inv_i[h] for h in range(2)]
    dots = jnp.concatenate([dmt[64 * h : 64 * h + 64] * inv2[h] for h in range(2)], axis=0)
    dot_low = dots.astype(LOW)
    dout = dots.T.astype(LOW)
    dqt, dk2, dv2 = [], [], []
    for h in range(2):
        mine = (lane // 64) == h
        e = e_i[h]
        delta = jnp.sum(prod[64 * h : 64 * h + 64], axis=0, keepdims=True) * inv2[h]
        vz = jnp.where(mine, v2, jnp.zeros((), LOW))
        dp = nn(vz, dot_low)
        ds = (e.astype(F32) * (dp - delta)).astype(LOW)
        dv2.append(nn(e, dout))
        dk2.append(nn(ds, q2))
        dqt.append(nn(kt[64 * h : 64 * h + 64], ds))
    first = lane < 64
    dv[:, cols] = jnp.where(first, dv2[0], dv2[1]).astype(LOW)
    dk[:, cols] = jnp.where(first, dk2[0], dk2[1]).astype(LOW)
    dq[:, cols] = jnp.concatenate(dqt, axis=0).T.astype(LOW)


def embed_part(dq, dk, dv, wq, wk, wv, rows):
    return (
        nt(dq[rows, :], wq[...]) * HEAD_DIM ** (-0.5) + nt(dk[rows, :], wk[...]) + nt(dv[rows, :], wv[...])
    )


def attn_bwd_kernel(
    place, al, wo, q, k, v, e_i, inv_i, mt_i, wq_a, wk_a, wv_a, x_a, base_a, mixed_a,
    pool, vec1, vec2, ib, p0, p1, p2, p3, send, keep,
    dm, dq, dk, dv, wq, wk, wv, x, base, mixed, eg, sems
):
    pairs = ((wq_a, wq), (wk_a, wk), (wv_a, wv), (x_a, x), (base_a, base), (mixed_a, mixed))
    loads = [pltpu.make_async_copy(a, b, sems.at[i]) for i, (a, b) in enumerate(pairs)]

    @pl.when(pl.program_id(0) == 0)
    def _():
        for load in loads:
            load.start()

    attn_bwd_heads(al, wo, q, k, v, e_i, inv_i, mt_i, dm, dq, dk, dv)

    @pl.when(pl.program_id(0) == pl.num_programs(0) - 1)
    def _():
        for load in loads:
            load.wait()
        scale = HEAD_DIM ** (-0.5)
        s, d = base.shape
        n, share = s // 4, d // 4
        core = place[1]

        def put(owner, at, values):
            for c in range(2):

                @pl.when(core == c)
                def _():
                    out = keep if owner == c else send
                    for z in range(4):
                        out[z, at, :] = values(z)

        pieces = ((x, dq, scale), (x, dk, 1.0), (x, dv, 1.0), (mixed, al, 1.0))
        for i, (left, right, factor) in enumerate(pieces):
            weight = (tn(left[...], right[...]) * factor).astype(LOW)
            start = share * (i % 2)
            put(i // 2, slice(start, start + share), lambda z: weight[share * z : share * z + share])
        for m, part in enumerate((p0, p1, p2, p3)):
            at = slice(m * n, m * n + n)
            value = (base[at, :] + embed_part(dq, dk, dv, wq, wk, wv, at)).astype(LOW)
            eg[m] = value
            part[n : n + 16, :] = pool[...]
            part[0:n, :] = value
        put(0, slice(2 * share, 2 * share + n), lambda z: eg[(place[0] + 4 - z) % 4])
        vectors = [
            jnp.sum(dq[...].astype(F32), axis=0, keepdims=True) * scale,
            jnp.sum(dv[...].astype(F32), axis=0, keepdims=True),
            vec1[2:3, :],
            vec1[0:1, :],
            vec1[1:2, :],
            vec2[2:3, :],
            vec2[0:1, :],
            vec2[1:2, :],
        ]
        vectors += [ib[f] for f in range(4)] + [jnp.zeros((n - 12, d), F32)]
        vectors = jnp.concatenate(vectors, axis=0).astype(LOW)
        put(1, slice(2 * share, 2 * share + n), lambda z: vectors)


def attn_bwd(place, al, wo, q, k, v, e, inv, mt, wq, wk, wv, x, base, mixed, pool, vec1, vec2, ib):
    s, d = q.shape
    steps = d // 128
    heads = d // HEAD_DIM
    col = pl.BlockSpec((s, 128), lambda h, p: (0, h))
    small = [whole(pool.shape), whole(vec1.shape), whole(vec2.shape), whole(ib.shape)]
    ins = [
        whole((s, d)),
        whole((d, d)),
        col,
        col,
        col,
        pl.BlockSpec((2, s, s), lambda h, p: (h, 0, 0)),
        pl.BlockSpec((2, 1, s), lambda h, p: (h, 0, 0)),
        pl.BlockSpec((128, s), lambda h, p: (h, 0)),
    ]
    shapes = [((s // 4 + 16, d), LOW)] * 4 + [((4, d // 2 + s // 4, d), LOW)] * 2
    return pl.pallas_call(
        attn_bwd_kernel,
        grid_spec=prefetch(
            1,
            (steps,),
            ins + [pl.BlockSpec(memory_space=pl.ANY)] * 6 + small,
            [whole(shape) for shape, _ in shapes],
            [pltpu.VMEM((s, d), LOW)] * 4
            + [pltpu.VMEM((d, d), LOW)] * 3
            + [pltpu.VMEM((s, d), LOW), pltpu.VMEM((s, d), F32), pltpu.VMEM((s, d), LOW)]
            + [pltpu.VMEM((4, s // 4, d), LOW), pltpu.SemaphoreType.DMA((6,))],
        ),
        out_shape=[struct(*one) for one in shapes],
        compiler_params=params(),
        cost_estimate=cost(14 * s * d * d + 8 * s * s * 256 * heads, 28e6),
        name="attention_backward",
    )(place, al, wo, q, k, v, e, inv, mt, wq, wk, wv, x, base, mixed, pool, vec1, vec2, ib)


def normalize(values):
    center = values - jnp.mean(values, axis=-1, keepdims=True)
    root = lax.rsqrt(jnp.mean(center * center, axis=-1, keepdims=True) + EPSILON)
    return center * root, root


def normalize_back(upstream, normed, root, gain):
    scaled = upstream * gain
    plain = jnp.mean(scaled, axis=-1, keepdims=True)
    crossed = jnp.mean(scaled * normed, axis=-1, keepdims=True)
    return root * (scaled - plain - normed * crossed)


def gelu_pair(v):
    cdf = lax.erf(v * 0.7071067811865476) * 0.5 + 0.5
    bell = jnp.exp(v * v * -0.5)
    return v * cdf, cdf + v * (bell * 0.3989422804014327)


def ff_kernel(
    row0, mixed, wo, bo, x, g1, s1, w1, b1, w2, b2, g2, s2, wp, bp, u0, u1, u2, u3,
    lhs_o, rhs_o, t0, t1, t2, t3, pool_o, al_o, fb_o, vec1_o, vec2_o, ib_o,
    w1s, w2s, wps, ups, gp, normed1, acc, sb, sems, *, chunk
):
    s, d = x.shape
    blocks = w1s.shape[0]
    ol_o, hid_o = lhs_o.at[0], lhs_o.at[1]
    act_o, il_o = rhs_o.at[0], rhs_o.at[1]
    n = s // 4
    per = chunk // n
    outs = (t0, t1, t2, t3)
    chunks = [slice(r, r + chunk) for r in range(0, s, chunk)]

    def load1(f):
        return pltpu.make_async_copy(w1.at[:, pl.ds(f * d, d)], w1s.at[f], sems.at[f])

    def load2(f):
        return pltpu.make_async_copy(w2.at[pl.ds(f * d, d), :], w2s.at[f], sems.at[blocks + f])

    loads = [pltpu.make_async_copy(wp, wps, sems.at[2 * blocks])]
    for m, part in enumerate((u0, u1, u2, u3)):
        loads.append(pltpu.make_async_copy(part, ups.at[m], sems.at[2 * blocks + 1 + m]))
    for f in range(blocks):
        load1(f).start()
        load2(f).start()
    for load in loads:
        load.start()

    roots1 = []
    for rows in chunks:
        val = nn(mixed[rows, :], wo[...]) + bo[...].astype(F32) + x[rows, :].astype(F32)
        normed, root = normalize(val)
        roots1.append(root)
        normed1[rows, :] = normed
        h = (normed * g1[...].astype(F32) + s1[...].astype(F32)).astype(LOW)
        hid_o[rows, :] = h
        acc[rows, :] = h.astype(F32) + b2[...].astype(F32)

    def forward(f, carry):
        load1(f).wait()
        load2(f).wait()
        for rows in chunks:
            pre = nn(hid_o[rows, :], w1s[f]) + b1[f].astype(F32)
            act, slope = gelu_pair(pre)
            act = act.astype(LOW)
            act_o[f, rows, :] = act
            gp[f, rows, :] = slope.astype(LOW)
            acc[rows, :] += nn(act, w2s[f])
        return carry

    lax.fori_loop(0, blocks, forward, 0)
    for load in loads:
        load.wait()

    gain = g2[...].astype(F32)
    roots2 = []
    for k, rows in enumerate(chunks):
        normed, root = normalize(acc[rows, :])
        roots2.append(root)
        res = (normed * gain + s2[...].astype(F32)).astype(LOW)
        al_o[rows, :] = res
        for j in range(per):
            outs[k * per + j][...] = res[j * n : j * n + n, :]
        acc[rows, :] = normed
    cls = al_o[pl.ds(pl.multiple_of(row0[0], 128), 16), :]
    pooled = jnp.tanh(nn(cls, wps[...]) + bp[...].astype(F32))
    pull = 0.0
    for m in range(4):
        terms = ups[m, n : n + 16, :].astype(F32)
        terms = jnp.broadcast_to(terms[0:1] + terms[1:2], (8, d))
        pull = pull + pltpu.roll(terms, ((row0[2] + 4 - m) % 4) * (d // 4), 1)
    pre = pull[:1] * (1.0 - pooled * pooled)
    cls_grad = nt(pre.astype(LOW), wps[...])[:1]
    high = pooled[:1].astype(LOW).astype(F32)
    pool = [cls[:1].astype(F32), pre[:1], high, pooled[:1] - high, jnp.zeros((12, d), F32)]
    pool_o[...] = jnp.concatenate(pool, axis=0).astype(LOW)
    gs, ss, bs = 0.0, 0.0, 0.0
    for k, rows in enumerate(chunks):
        ids = lax.broadcasted_iota(jnp.int32, (chunk, 1), 0) + rows.start
        up = jnp.concatenate([ups[k * per + j, 0:n, :] for j in range(per)], axis=0).astype(F32)
        upstream = up + jnp.where(ids == row0[0], cls_grad, 0.0)
        normed = acc[rows, :]
        back = normalize_back(upstream, normed, roots2[k], gain)
        sb[rows, :] = back
        low = back.astype(LOW)
        ol_o[rows, :] = low
        gs = gs + jnp.sum(upstream * normed, axis=0, keepdims=True)
        ss = ss + jnp.sum(upstream, axis=0, keepdims=True)
        bs = bs + jnp.sum(low.astype(F32), axis=0, keepdims=True)
    live = row0[1].astype(F32)
    vec2_o[0:1, :] = gs * live
    vec2_o[1:2, :] = ss * live
    vec2_o[2:3, :] = bs * live

    def backward(f, carry):
        bias = 0.0
        for rows in chunks:
            low = (nt(ol_o[rows, :], w2s[f]) * gp[f, rows, :].astype(F32)).astype(LOW)
            il_o[f, rows, :] = low
            bias = bias + jnp.sum(low.astype(F32), axis=0, keepdims=True)
            sb[rows, :] += nt(low, w1s[f])
        ib_o[f] = bias
        return carry

    lax.fori_loop(0, blocks, backward, 0)
    gain = g1[...].astype(F32)
    gs, ss, bs = 0.0, 0.0, 0.0
    for k, rows in enumerate(chunks):
        upstream = sb[rows, :]
        normed = normed1[rows, :]
        back = normalize_back(upstream, normed, roots1[k], gain)
        fb_o[rows, :] = back
        low = back.astype(LOW)
        al_o[rows, :] = low
        gs = gs + jnp.sum(upstream * normed, axis=0, keepdims=True)
        ss = ss + jnp.sum(upstream, axis=0, keepdims=True)
        bs = bs + jnp.sum(low.astype(F32), axis=0, keepdims=True)
    vec1_o[0:1, :] = gs
    vec1_o[1:2, :] = ss
    vec1_o[2:3, :] = bs


def feed_forward(row0, mixed, wo, bo, x, g1, s1, w1, b1, w2, b2, g2, s2, wp, bp, ups, chunk=256):
    s, d = x.shape
    ff = w1.shape[1]
    blocks = ff // d
    full, row = whole((s, d)), whole((1, d))
    away = pl.BlockSpec(memory_space=pl.ANY)
    part = (s // 4 + 16, d)
    return pl.pallas_call(
        functools.partial(ff_kernel, chunk=chunk),
        grid_spec=prefetch(
            1,
            (1,),
            [full, whole((d, d)), row, full, row, row, away, whole((blocks, 1, d)), away, row, row, row]
            + [away, row]
            + [away] * 4,
            [whole((2, s, d)), whole((2, blocks, s, d))]
            + [whole((s // 4, d))] * 4
            + [whole((16, d)), full, full, whole((8, d)), whole((8, d)), whole((blocks, 1, d))],
            [
                pltpu.VMEM((blocks, d, d), LOW),
                pltpu.VMEM((blocks, d, d), LOW),
                pltpu.VMEM((d, d), LOW),
                pltpu.VMEM((4,) + part, LOW),
                pltpu.VMEM((blocks, s, d), LOW),
                pltpu.VMEM((s, d), F32),
                pltpu.VMEM((s, d), F32),
                pltpu.VMEM((s, d), F32),
                pltpu.SemaphoreType.DMA((2 * blocks + 5,)),
            ],
        ),
        out_shape=[struct((2, s, d), LOW), struct((2, blocks, s, d), LOW)]
        + [struct((s // 4, d), LOW)] * 4
        + [
            struct((16, d), LOW),
            struct((s, d), LOW),
            struct((s, d), F32),
            struct((8, d), F32),
            struct((8, d), F32),
            struct((blocks, 1, d), F32),
        ],
        compiler_params=params(),
        cost_estimate=cost(2 * s * d * d + 8 * s * d * ff, 30e6),
        name="feed_forward",
    )(row0, mixed, wo, bo, x, g1, s1, w1, b1.reshape(blocks, 1, d), w2, b2, g2, s2, wp, bp, *ups)


def tn(a, b):
    return lax.dot_general(a, b, (((0,), (0,)), ((), ())), preferred_element_type=F32)


def prefetch(count, grid, in_specs, out_specs, scratch=()):
    return pltpu.PrefetchScalarGridSpec(
        num_scalar_prefetch=count,
        grid=grid,
        in_specs=in_specs,
        out_specs=out_specs,
        scratch_shapes=list(scratch),
    )


def index_kernel(ids, req_o, col_o, row_o, *, rows, slots):
    count, n = ids.shape
    owners = req_o.shape[0]
    owner = ((ids[...].astype(F32) + 0.5) * (1.0 / rows)).astype(jnp.int32)
    local = ids[...] - owner * rows + 1
    flat = [owner.astype(F32), (local // 64).astype(F32), (local % 64).astype(F32)]
    flat = jnp.concatenate(flat + [jnp.zeros((16 - 3 * count, n), F32)], axis=0)
    cols = flat.T
    lane = lax.broadcasted_iota(jnp.int32, (n, owners), 1).astype(F32)
    before = lax.broadcasted_iota(jnp.int32, (n, n), 1) < lax.broadcasted_iota(jnp.int32, (n, n), 0)
    before = jnp.where(before, 1.0, 0.0).astype(LOW)
    seen = jnp.zeros((1, owners), F32)
    high, low, places = 0.0, 0.0, []
    slot_lane = lax.broadcasted_iota(jnp.int32, (n, 128), 1).astype(F32)
    for s in range(count):
        hot = jnp.where(lane == cols[:, s : s + 1], 1.0, 0.0)
        hot_low = hot.astype(LOW)
        within = jnp.sum((nn(before, hot_low) + seen) * hot, axis=1, keepdims=True)
        seen = seen + jnp.sum(hot, axis=0, keepdims=True)
        place = cols[:, s : s + 1] * slots + within
        places.append(place)
        here = slot_lane == within
        put_high = jnp.where(here, cols[:, count + s : count + s + 1], 0.0).astype(LOW)
        put_low = jnp.where(here, cols[:, 2 * count + s : 2 * count + s + 1], 0.0).astype(LOW)
        high = high + tn(hot_low, put_high)
        low = low + tn(hot_low, put_low)
    req_o[...] = (high * 64.0 + low).astype(jnp.int32)[:, :slots] - 1
    places.append(jnp.full((n, 1), -1.0, F32))
    table = jnp.concatenate([jnp.broadcast_to(p, (n, 8)) for p in places], axis=1)
    table = jnp.concatenate([table, jnp.zeros((n, 128 - table.shape[1]), F32)], axis=1)
    turned = table.T.astype(jnp.int32)
    for s in range(count + 1):
        col_o[s] = places[s].astype(jnp.int32)
        row_o[s] = turned[8 * s : 8 * s + 1, :]


def index_requests(ids, rows, owners, slots):
    count, n = ids.shape
    return pl.pallas_call(
        functools.partial(index_kernel, rows=rows, slots=slots),
        grid=(1,),
        in_specs=[whole((count, n))],
        out_specs=[whole((owners, slots)), whole((count + 1, n, 1)), whole((count + 1, 1, n))],
        out_shape=[
            struct((owners, slots), jnp.int32),
            struct((count + 1, n, 1), jnp.int32),
            struct((count + 1, 1, n), jnp.int32),
        ],
        compiler_params=params(),
        cost_estimate=cost(0, 1e6),
        name="index_requests",
    )(ids)


def gather_kernel(fetch, table, out, acc, *, rows):
    step = pl.program_id(0)
    last = pl.num_programs(0) - 1
    blk = table.shape[0]
    ids = lax.broadcasted_iota(jnp.int32, (1, blk), 1) + step * blk
    hot = jnp.where(ids == fetch[...], 1.0, 0.0).astype(LOW)

    def add(block):
        part = nn(hot, block)

        @pl.when(step == 0)
        def _():
            acc[...] = part

        @pl.when(step > 0)
        def _():
            acc[...] += part

    @pl.when(step < last)
    def _():
        add(table[...])

    @pl.when(step == last)
    def _():
        ids_col = lax.broadcasted_iota(jnp.int32, (blk, 1), 0) + step * blk
        add(jnp.where(ids_col < rows, table[...], jnp.zeros((), LOW)))
        out[...] = acc[...].astype(LOW)


def gather_rows(fetch, table, blk=1024):
    slots = fetch.shape[0]
    rows, d = table.shape
    return pl.pallas_call(
        functools.partial(gather_kernel, rows=rows),
        grid=(pl.cdiv(rows, blk),),
        in_specs=[whole((slots, 1)), pl.BlockSpec((blk, d), lambda i: (i, 0))],
        out_specs=whole((slots, d)),
        out_shape=struct((slots, d), LOW),
        scratch_shapes=[pltpu.VMEM((slots, d), F32)],
        compiler_params=params(),
        cost_estimate=cost(2 * slots * rows * d, 8e6),
        name="gather_rows",
    )(fetch, table)


def embed_kernel(place, slot, replies, pos, o0, o1, o2, o3):
    ids = lax.broadcasted_iota(jnp.int32, (1, replies.shape[0]), 1)
    for m, out in enumerate((o0, o1, o2, o3)):
        sent = (place[0] + m) % 4
        hot = jnp.where(ids == slot[sent], 1.0, 0.0).astype(LOW)
        live = jnp.where(sent < 3, 1.0, 0.0)
        out[...] = ((nn(hot, replies[...]) + pos[...].astype(F32)) * live).astype(LOW)


def embed_parts(place, slot, replies, pos):
    slots, d = replies.shape
    n = pos.shape[0]
    out = pl.BlockSpec((n, d), lambda i, p: (0, 0))
    return pl.pallas_call(
        embed_kernel,
        grid_spec=prefetch(
            1,
            (1,),
            [whole((4, n, 1)), whole((slots, d)), whole((n, d))],
            [out] * 4,
        ),
        out_shape=[struct((n, d), LOW)] * 4,
        compiler_params=params(),
        cost_estimate=cost(2 * slots * 4 * n * d, 3e6),
        name="embed_parts",
    )(place, slot, replies, pos)


def outgoing_kernel(place, slot, p0, p1, p2, p3, out):
    ids = lax.broadcasted_iota(jnp.int32, (out.shape[0], 1), 0)
    total = 0.0
    for m, part in enumerate((p0, p1, p2, p3)):
        sent = (place[0] + m) % 4
        hot = jnp.where(ids == slot[sent], 1.0, 0.0).astype(LOW)
        total = total + nn(hot, part[...])
    out[...] = total.astype(LOW)


def outgoing_rows(place, slot, parts, slots):
    n = slot.shape[2]
    d = parts[0].shape[1]
    return pl.pallas_call(
        outgoing_kernel,
        grid_spec=prefetch(
            1, (1,), [whole((4, 1, n))] + [whole((n, d))] * 4, whole((slots, d))
        ),
        out_shape=struct((slots, d), LOW),
        compiler_params=params(),
        cost_estimate=cost(2 * slots * 4 * n * d, 3e6),
        name="outgoing_rows",
    )(place, slot, *parts)


def table_kernel(fetch, incoming, out):
    blk = out.shape[0]
    ids = lax.broadcasted_iota(jnp.int32, (blk, 1), 0) + pl.program_id(0) * blk
    out[...] = nn(jnp.where(ids == fetch[...], 1.0, 0.0).astype(LOW), incoming[...])


def table_grad(fetch, incoming, rows, blk=1024):
    slots, d = incoming.shape
    return pl.pallas_call(
        table_kernel,
        grid=(pl.cdiv(rows, blk),),
        in_specs=[whole((1, slots)), whole((slots, d))],
        out_specs=pl.BlockSpec((blk, d), lambda i: (i, 0)),
        out_shape=struct((rows, d), F32),
        compiler_params=params(),
        cost_estimate=cost(2 * slots * rows * d, 13e6),
        name="table_gradient",
    )(fetch, incoming)


def unpermute_kernel(place, p0, p1, p2, p3, out):
    for m, part in enumerate((p0, p1, p2, p3)):
        sent = (place[0] + m) % 4

        @pl.when(sent < 3)
        def _():
            out[sent] = part[...]


def unpermute(place, parts, n):
    d = parts[0].shape[1]
    return pl.pallas_call(
        unpermute_kernel,
        grid_spec=prefetch(1, (1,), [whole((n, d))] * 4, whole((3, n, d))),
        out_shape=struct((3, n, d), parts[0].dtype),
        compiler_params=params(),
        cost_estimate=cost(0, 2e6),
        name="unpermute",
    )(place, *parts)


def ff_send_kernel(which, left, right, out):
    out[0] = tn(left[0], right[0, 0]).astype(LOW)


def ff_specs(s, d):
    return [
        pl.BlockSpec((1, s, d), lambda f, w: (w[0], 0, 0)),
        pl.BlockSpec((1, 1, s, d), lambda f, w: (w[0], f, 0, 0)),
    ]


def ff_send(which, left, right):
    _, blocks, s, d = right.shape
    return pl.pallas_call(
        ff_send_kernel,
        grid_spec=prefetch(
            1, (blocks,), ff_specs(s, d), pl.BlockSpec((1, d, d), lambda f, w: (f, 0, 0))
        ),
        out_shape=struct((blocks, d, d), LOW),
        compiler_params=params(),
        cost_estimate=cost(2 * blocks * s * d * d, 9e6),
        name="ff_send",
    )(which, left, right)


def ff_keep_kernel(place, left, right, got, o0, o1, o2, o3, acc):
    f = pl.program_id(0)
    total = tn(left[0], right[0, 0]) + got[0].astype(F32)
    acc[f] = total.astype(LOW).reshape(acc.shape[1:])

    @pl.when(f == pl.num_programs(0) - 1)
    def _():
        for m, out in enumerate((o0, o1, o2, o3)):
            index = (place[1] + m) % 4

            @pl.when(place[0] == 0)
            def _():
                for z in range(4):
                    out[z] = acc[z, index]

            @pl.when(place[0] == 1)
            def _():
                out[...] = acc[index]


def ff_keep(place, left, right, got):
    _, blocks, s, d = right.shape
    shape = (4, d // 4, d)
    return pl.pallas_call(
        ff_keep_kernel,
        grid_spec=prefetch(
            1,
            (blocks,),
            ff_specs(s, d) + [pl.BlockSpec((1, d, d), lambda f, w: (f, 0, 0))],
            [whole(shape)] * 4,
            [pltpu.VMEM((blocks,) + shape, LOW)],
        ),
        out_shape=[struct(shape, LOW)] * 4,
        compiler_params=params(),
        cost_estimate=cost(2 * blocks * s * d * d, 14e6),
        name="ff_keep",
    )(place, left, right, got)


def core_add_kernel(place, own, got, o0, o1, o2, o3):
    rows = o0.shape[1]
    for m, out in enumerate((o0, o1, o2, o3)):
        at = pl.ds(pl.multiple_of((place[0] + m) % 4 * rows, rows), rows)
        out[...] = (own[:, at, :].astype(F32) + got[:, at, :].astype(F32)).astype(LOW)


def core_add(place, own, got):
    out = (4, own.shape[1] // 4, own.shape[2])
    return pl.pallas_call(
        core_add_kernel,
        grid_spec=prefetch(1, (1,), [whole(own.shape)] * 2, [whole(out)] * 4),
        out_shape=[struct(out, LOW)] * 4,
        compiler_params=params(),
        cost_estimate=cost(0, 9e6),
        name="core_add",
    )(place, own, got)


def add4(a, b, c, d):
    return a[...].astype(F32) + b[...].astype(F32) + c[...].astype(F32) + d[...].astype(F32)


def ring_add_kernel(place, p0, p1, p2, p3, o0, o1, o2, o3, acc):
    acc[...] = add4(p0, p1, p2, p3)
    rows = o0.shape[1]
    for m, out in enumerate((o0, o1, o2, o3)):
        at = pl.ds(pl.multiple_of((place[0] + m) % 4 * rows, rows), rows)
        out[...] = acc[:, at, :].astype(LOW)


def ring_add(place, parts):
    shape = parts[0].shape
    out = (4, shape[1] // 4, shape[2])
    return pl.pallas_call(
        ring_add_kernel,
        grid_spec=prefetch(
            1, (1,), [whole(shape)] * 4, [whole(out)] * 4, [pltpu.VMEM(shape, F32)]
        ),
        out_shape=[struct(out, LOW)] * 4,
        compiler_params=params(),
        cost_estimate=cost(0, 6e6),
        name="ring_add",
    )(place, *parts)


def join_kernel(place, a0, a1, a2, a3, b0, b1, b2, b3, o0, o1, o2, o3, acc):
    acc[:, 0:48, :] = add4(a0, a1, a2, a3)
    acc[:, 48:80, :] = add4(b0, b1, b2, b3)
    for m, out in enumerate((o0, o1, o2, o3)):
        out[...] = acc[(place[0] + m) % 4].astype(LOW)


def join(place, first, second):
    d = first[0].shape[2]
    return pl.pallas_call(
        join_kernel,
        grid_spec=prefetch(
            1,
            (1,),
            [whole(first[0].shape)] * 4 + [whole(second[0].shape)] * 4,
            [whole((80, d))] * 4,
            [pltpu.VMEM((4, 80, d), F32)],
        ),
        out_shape=[struct((80, d), LOW)] * 4,
        compiler_params=params(),
        cost_estimate=cost(0, 4e6),
        name="join",
    )(place, *first, *second)


def piece_kernel(f0, f1, f2, f3, r0, r1, r2, r3, out):
    pool = [part[...].astype(F32)[0:2] for part in (r0, r1, r2, r3)]
    pool.append(jnp.zeros((8, out.shape[1]), F32))
    out[...] = jnp.concatenate([add4(f0, f1, f2, f3)] + pool, axis=0).astype(LOW)


def piece_rows(parts, pool):
    d = parts[0].shape[1]
    return pl.pallas_call(
        piece_kernel,
        grid=(1,),
        in_specs=[whole(p.shape) for p in parts]
        + [pl.BlockSpec((16, d), lambda i: (8, 0)) for p in pool],
        out_specs=whole((96, d)),
        out_shape=struct((96, d), LOW),
        compiler_params=params(),
        cost_estimate=cost(0, 1e6),
        name="piece_rows",
    )(*parts, *pool)


def order_kernel(place, p0, p1, p2, p3, out):
    for m, part in enumerate((p0, p1, p2, p3)):
        out[(place[0] + 4 - m) % 4] = part[...]


def order(place, parts):
    shape = parts[0].shape
    return pl.pallas_call(
        order_kernel,
        grid_spec=prefetch(1, (1,), [whole(shape)] * 4, whole((4,) + shape)),
        out_shape=struct((4,) + shape, LOW),
        compiler_params=params(),
        cost_estimate=cost(0, 3e6),
        name="order",
    )(place, *parts)


def finish_kernel(
    place, own, got, outer_o, inner_o, q_o, k_o, v_o, out_o, pos_o, vec_o, pw_o, pb_o, acc
):
    d = outer_o.shape[0]

    def fill(zero, one):
        pool = []
        for i in range(4):
            for k in range(4):
                at = 96 * k
                r = 192 * i + 48 * k
                acc[r : r + 48, :] = zero[i, at : at + 48, :].astype(F32)
                cols = slice(d * i, d * i + d)
                inner_o[48 * k : 48 * k + 48, cols] = one[i, at : at + 48, :].astype(F32)
                r = 128 * i + 32 * k
                first = zero[i, at + 48 : at + 80, :].astype(F32)
                second = one[i, at + 48 : at + 80, :].astype(F32)
                if r < 192:
                    q_o[r : r + 32, :] = first
                    v_o[r : r + 32, :] = second
                elif r < 384:
                    k_o[r - 192 : r - 160, :] = first
                    out_o[r - 192 : r - 160, :] = second
                else:
                    pos_o[r - 384 : r - 352, :] = first
                    if r == 384:
                        vec_o[...] = second[0:16]
                pool.append(zero[i, at + 80 : at + 96, :].astype(F32)[0:8])
                pool.append(one[i, at + 80 : at + 96, :].astype(F32)[0:8])
        outer_o[...] = acc[...].T
        pool = jnp.concatenate(pool, axis=0)
        even = lax.broadcasted_iota(jnp.int32, (pool.shape[0], 1), 0) % 2 == 0
        below = jnp.concatenate([pool[1:], pool[:1]], axis=0)
        acc[...] = tn(jnp.where(even, pool, 0.0).astype(LOW), below.astype(LOW))
        pb_o[...] = jnp.sum(jnp.where(even, 0.0, pool), axis=0, keepdims=True)

    @pl.when(place[0] == 0)
    def _():
        fill(own, got)

    @pl.when(place[0] == 1)
    def _():
        fill(got, own)

    pw_o[...] = acc[pl.ds(pl.multiple_of(place[1] * (d // 4), d // 4), d // 4), :]


def finish(place, own, got):
    d = own.shape[2]
    share = d // 4
    shapes = [(d, d), (share, 4 * d)] + [(share, d)] * 4 + [(128, d), (16, d), (share, d), (1, d)]
    return pl.pallas_call(
        finish_kernel,
        grid_spec=prefetch(
            1,
            (1,),
            [whole(own.shape)] * 2,
            [whole(s) for s in shapes],
            [pltpu.VMEM((d, d), F32)],
        ),
        out_shape=[struct(s, F32) for s in shapes],
        compiler_params=params(),
        cost_estimate=cost(0, 14e6),
        name="finish",
    )(place, own, got)


def pooled_kernel(place, p0, p1, p2, p3, out):
    for m, part in enumerate((p0, p1, p2, p3)):
        two = part[...].astype(F32)
        row = two[2:3] + two[3:4]
        out[(place[0] + m) % 4] = pltpu.roll(
            jnp.broadcast_to(row, (8, row.shape[1])), row.shape[1] - 192 * place[0], 1
        )


def pooled_rows(place, parts):
    d = parts[0].shape[1]
    below = pl.BlockSpec((16, d), lambda i, p: (8, 0))
    return pl.pallas_call(
        pooled_kernel,
        grid_spec=prefetch(1, (1,), [below] * 4, whole((4, 8, d))),
        out_shape=struct((4, 8, d), F32),
        compiler_params=params(),
        name="pooled_rows",
    )(place, *parts)


def shift_pairs(step, axes):
    pairs = []
    for y in range(4):
        for x in range(4):
            for c in range(2):
                to = (y, (x + step) % 4) if axes[c] == "x" else ((y + step) % 4, x)
                pairs.append(((y * 4 + x) * 2 + c, (to[0] * 4 + to[1]) * 2 + c))
    return pairs


def shift_first(array, step):
    return lax.ppermute(array, "batch", shift_pairs(step, "xy"))


def shift_second(array, step):
    return lax.ppermute(array, "batch", shift_pairs(step, "yx"))


def shift_z(array, step):
    return lax.ppermute(array, "seq", [(z, (z + step) % 4) for z in range(4)])


def swap_core(array):
    return lax.ppermute(array, "batch", [(i, i ^ 1) for i in range(32)])


def ring_send(parts, shift):
    return [parts[0], shift(parts[1], 1), shift(parts[2], 2), shift(parts[3], 3)]


def to_sentence(parts):
    out = [parts[0]]
    for step in (1, 2, 3):
        pairs = [(z, (z + step) % 4) for z in range(4) if (z + step) % 4 < 3]
        out.append(lax.ppermute(parts[step], "seq", pairs))
    return out


def from_sentence(parts):
    out = [parts[0]]
    for step in (1, 2, 3):
        pairs = [((z + step) % 4, z) for z in range(4) if (z + step) % 4 < 3]
        out.append(lax.ppermute(parts[step], "seq", pairs))
    return out


def tie(array, *after):
    return lax.optimization_barrier((array,) + after)[0]


def per_device(
    token_ids,
    lengths,
    word_table,
    positions,
    query_weight,
    key_weight,
    value_weight,
    query_bias,
    value_bias,
    output_weight,
    output_bias,
    first_gain,
    first_shift,
    inner_weight,
    inner_bias,
    outer_weight,
    outer_bias,
    second_gain,
    second_shift,
    pooler_weight,
    pooler_bias,
    out_grad,
    pooled_grad,
):
    num_sent, local_len = token_ids.shape
    table_rows, width = word_table.shape
    all_count = lax.axis_size("seq") * lax.axis_size("batch")
    z = lax.axis_index("seq")
    batch_place = lax.axis_index("batch")
    core = batch_place % 2
    x = (batch_place // 2) % 4
    y = batch_place // 8

    first = jnp.where(core == 0, x, y)
    second = jnp.where(core == 0, y, x)

    def scalars(*values):
        return jnp.stack([jnp.asarray(v, jnp.int32) for v in values])

    slots = 2 * num_sent * local_len // all_count
    all_slots = slots * all_count
    requests, slot_cols, slot_rows = index_requests(token_ids, table_rows, all_count, slots)
    arrived = lax.all_to_all(requests, ("batch", "seq"), split_axis=0, concat_axis=0, tiled=True)
    fetch = arrived.reshape(-1)
    found = gather_rows(fetch[:, None], word_table)
    replies = lax.all_to_all(
        found.reshape(all_count, slots, width),
        ("batch", "seq"),
        split_axis=0,
        concat_axis=0,
        tiled=True,
    ).reshape(all_slots, width)
    live = (z < 3).astype(jnp.int32)
    sentence = jnp.minimum(z, 2)

    def row(vector):
        return vector.reshape(1, -1)

    vectors = (
        query_bias,
        value_bias,
        output_bias,
        first_gain,
        first_shift,
        inner_bias,
        outer_bias,
        second_gain,
        second_shift,
        pooler_bias,
    )
    block_of = (z - jnp.arange(4, dtype=jnp.int32)) % 4
    place_of = block_of[:, None] * local_len + jnp.arange(local_len, dtype=jnp.int32)[None, :]
    live_keys = (place_of.reshape(-1, 1) < lengths[sentence]).astype(F32)

    high = pooled_grad.astype(LOW)
    terms = jnp.stack([high, (pooled_grad - high.astype(F32)).astype(LOW)], axis=1)
    terms = jnp.pad(terms, ((0, 0), (0, 14), (0, width - terms.shape[2])))
    cotangents = jnp.concatenate([out_grad, terms], axis=1)
    early = [live_keys] + [row(v) for v in vectors]
    cotangents, *early = lax.optimization_barrier([cotangents] + early)
    live_keys, q_bias, v_bias, o_bias, gain1, shift1, in_bias, out_bias, gain2, shift2, pool_bias = early
    ups = [
        lax.dynamic_index_in_dim(cotangents, jnp.minimum((z + m) % 4, 2), 0, keepdims=False)
        for m in range(4)
    ]
    ups = to_sentence([jnp.where(z < 3, ups[0], jnp.zeros((), LOW))] + ups[1:])
    replies, *ups = lax.optimization_barrier([replies] + ups)
    embeds = to_sentence(embed_parts(scalars(z), slot_cols, replies, positions))

    embed, query, key, value, expo, inverse, mixed_t, mixed = attn_fwd(
        embeds, query_weight, key_weight, value_weight, q_bias, v_bias, live_keys
    )
    (
        left,
        right,
        *result,
        pool,
        attention_low,
        first_back,
        vec1,
        vec2,
        inner_bias_grad,
    ) = feed_forward(
        scalars(sentence * local_len, live, z),
        mixed,
        output_weight,
        o_bias,
        embed,
        gain1,
        shift1,
        inner_weight,
        in_bias,
        outer_weight,
        out_bias,
        gain2,
        shift2,
        pooler_weight,
        pool_bias,
        ups,
    )

    ff_other = ff_send(scalars(1 - core), left, right)
    ff_parts = ff_keep(scalars(core, first), left, right, swap_core(ff_other))
    attention_low = tie(attention_low, ff_parts[0])
    ff_parts = ring_send(ff_parts, shift_first)
    *embed_grad, rest_other, rest_own = attn_bwd(
        scalars(z, core),
        attention_low,
        output_weight,
        query,
        key,
        value,
        expo,
        inverse,
        mixed_t,
        query_weight,
        key_weight,
        value_weight,
        embed,
        first_back,
        mixed,
        pool,
        vec1,
        vec2,
        inner_bias_grad,
    )
    embed_grad, rest_other, rest_own, ff_parts = lax.optimization_barrier(
        (embed_grad, rest_other, rest_own, ff_parts)
    )

    returned = from_sentence(embed_grad)
    rest_parts = core_add(scalars(first), rest_own, swap_core(rest_other))
    ff_parts[0] = tie(ff_parts[0], rest_parts[0])
    rest_parts = ring_send(rest_parts, shift_first)
    ff_parts = ring_add(scalars(second), ff_parts)
    returned[0] = tie(returned[0], ff_parts[0])
    outgoing = outgoing_rows(scalars(z), slot_rows, returned, all_slots)
    ff_parts = ring_send(ff_parts, shift_second)
    incoming = lax.all_to_all(
        outgoing.reshape(all_count, slots, width),
        ("batch", "seq"),
        split_axis=0,
        concat_axis=0,
        tiled=True,
    ).reshape(all_slots, width)
    rest_parts[0] = tie(rest_parts[0], outgoing)
    rest_parts = ring_send(ring_add(scalars(second), rest_parts), shift_second)
    rest_parts[0] = tie(rest_parts[0], incoming)
    parts = ring_send(join(scalars(z), ff_parts, rest_parts), shift_z)
    piece = piece_rows(parts, returned)
    incoming = tie(incoming, piece)
    pieces = [piece] + [shift_second(piece, m) for m in (1, 2, 3)]
    grad_table = table_grad(fetch[None, :], incoming, table_rows)
    pieces[0] = tie(pieces[0], grad_table)
    block = order(scalars(second), pieces).reshape(-1, width)
    result[0] = tie(result[0], block)
    blocks = [block] + [shift_first(block, m) for m in (1, 2, 3)]
    result = from_sentence(result)
    pooled = pooled_rows(scalars(z), [tie(returned[0], block)] + returned[1:])
    pooled = pooled[:num_sent, 0, : width // 4]
    blocks[0] = tie(blocks[0], pooled)
    whole_own = order(scalars(first), blocks)
    whole_other = swap_core(whole_own)
    result[0] = tie(result[0], whole_own)
    hidden_out = unpermute(scalars(z), result, local_len)
    (
        grad_outer,
        grad_inner,
        grad_query,
        grad_key,
        grad_value,
        grad_output,
        grad_positions,
        vectors,
        grad_pooler,
        pooler_bias_grad,
    ) = finish(scalars(core, z), tie(whole_own, hidden_out), whole_other)

    share = width // 4
    mine = lax.dynamic_slice_in_dim(vectors[:8], z * share, share, 1)
    ff = inner_weight.shape[1]
    inner_bias_sum = lax.dynamic_slice_in_dim(vectors[8:12].reshape(-1), z * ff // 4, ff // 4, 0)
    pooler_bias_sum = lax.dynamic_slice_in_dim(pooler_bias_grad[0], z * share, share, 0)
    return (
        hidden_out,
        pooled,
        grad_table,
        grad_positions,
        grad_query,
        grad_key,
        grad_value,
        mine[0],
        mine[1],
        grad_output,
        mine[2],
        mine[3],
        mine[4],
        grad_inner,
        inner_bias_sum,
        grad_outer,
        mine[5],
        mine[6],
        mine[7],
        grad_pooler,
        pooler_bias_sum,
    )


def solution(mesh):
    in_specs = (
        P("batch", "seq"),
        P("batch"),
        P(("batch", "seq"), None),
        P("seq", None),
        P(),
        P(),
        P(),
        P(),
        P(),
        P(),
        P(),
        P(),
        P(),
        P(),
        P(),
        P(),
        P(),
        P(),
        P(),
        P(),
        P(),
        P("batch", "seq", None),
        P("batch", "seq"),
    )
    out_specs = (
        P("batch", "seq", None),
        P("batch", "seq"),
        P(("batch", "seq"), None),
        P("seq", None),
        P("seq", None),
        P("seq", None),
        P("seq", None),
        P("seq"),
        P("seq"),
        P("seq", None),
        P("seq"),
        P("seq"),
        P("seq"),
        P("seq", None),
        P("seq"),
        P("seq", None),
        P("seq"),
        P("seq"),
        P("seq"),
        P("seq", None),
        P("seq"),
    )
    return jax.shard_map(
        per_device, mesh=mesh, in_specs=in_specs, out_specs=out_specs, check_vma=False
    )
```

```python
import functools
import jax
import jax.numpy as jnp
from jax import lax
from jax.experimental import pallas as pl
from jax.experimental.pallas import tpu as pltpu
from jax.sharding import PartitionSpec as P

F32 = jnp.float32
LOW = jnp.bfloat16
EPSILON = 1e-12
MASKED = -1000000000.0
HEAD_DIM = 64
VMEM = 63 * 1024 * 1024
HALF = 384
SHARE = 0.02


def nn(a, b):
    return lax.dot_general(a, b, (((1,), (0,)), ((), ())), preferred_element_type=F32)


def nt(a, b):
    return lax.dot_general(a, b, (((1,), (1,)), ((), ())), preferred_element_type=F32)


def struct(shape, dtype):
    return jax.ShapeDtypeStruct(shape, dtype)


def whole(shape):
    zeros = (0,) * len(shape)
    return pl.BlockSpec(shape, lambda *_: zeros, pipeline_mode=pl.Buffered(1))


def cost(flops, size):
    return pl.CostEstimate(
        flops=int(flops * SHARE), bytes_accessed=int(size * SHARE), transcendentals=0
    )


def params(**kw):
    return pltpu.CompilerParams(vmem_limit_bytes=VMEM, **kw)


def attn_fwd_kernel(
    x0, x1, x2, x3, wq, wk, wv, bq, bv, live, x_o, q_o, k_o, v_o, e_o, inv_o, mt_o, mixed_o, x
):
    scale = HEAD_DIM ** (-0.5)
    n = x0.shape[0]

    @pl.when(pl.program_id(0) == 0)
    def _():
        for m, part in enumerate((x0, x1, x2, x3)):
            x[m * n : m * n + n, :] = part[...]
            x_o[m * n : m * n + n, :] = part[...]

    q = ((nn(x[...], wq[...]) + bq[...].astype(F32)) * scale).astype(LOW)
    q_o[...] = q
    k = nn(x[...], wk[...]).astype(LOW)
    k_o[...] = k
    v = nn(x[...], wv[...]) + bv[...].astype(F32)
    v_o[...] = v.astype(LOW)
    keep = live[...] > 0.0
    lane = lax.broadcasted_iota(jnp.int32, (1, 128), 1)
    for pair in range(q.shape[1] // 128):
        cols = slice(128 * pair, 128 * pair + 128)
        q2, k2 = q[:, cols], k[:, cols]
        vt = v[:, cols].T.astype(LOW)
        parts = []
        for h in range(2):
            kz = jnp.where((lane // 64) == h, k2, jnp.zeros((), LOW))
            s = nt(kz, q2)
            s = jnp.where(keep, s, MASKED)
            e = jnp.exp(s - jnp.max(s, axis=0, keepdims=True))
            inv = 1.0 / jnp.sum(e, axis=0, keepdims=True)
            eb = e.astype(LOW)
            e_o[2 * pair + h] = eb
            inv_o[2 * pair + h] = inv
            parts.append(nn(vt[64 * h : 64 * h + 64], eb) * inv)
        mt = jnp.concatenate(parts, axis=0)
        mt_o[cols, :] = mt.astype(LOW)
        mixed_o[:, cols] = mt.T.astype(LOW)


def attn_fwd(parts, wq, wk, wv, bq, bv, live, group=256):
    s, d = live.shape[0], wq.shape[0]
    n = s // 4
    hg = group // HEAD_DIM
    col = pl.BlockSpec((s, group), lambda h: (0, h))
    wcol = pl.BlockSpec((d, group), lambda h: (0, h))
    brow = pl.BlockSpec((1, group), lambda h: (0, h))
    heads = d // HEAD_DIM
    return pl.pallas_call(
        attn_fwd_kernel,
        grid=(d // group,),
        in_specs=[pl.BlockSpec((n, d), lambda h: (0, 0))] * 4 + [wcol, wcol, wcol, brow, brow, whole((s, 1))],
        out_specs=[
            whole((s, d)),
            col,
            col,
            col,
            pl.BlockSpec((hg, s, s), lambda h: (h, 0, 0)),
            pl.BlockSpec((hg, 1, s), lambda h: (h, 0, 0)),
            pl.BlockSpec((group, s), lambda h: (h, 0)),
            col,
        ],
        out_shape=[
            struct((s, d), LOW),
            struct((s, d), LOW),
            struct((s, d), LOW),
            struct((s, d), LOW),
            struct((heads, s, s), LOW),
            struct((heads, 1, s), F32),
            struct((d, s), LOW),
            struct((s, d), LOW),
        ],
        scratch_shapes=[pltpu.VMEM((s, d), LOW)],
        compiler_params=params(),
        cost_estimate=cost(6 * s * d * d + 4 * s * s * 256 * heads, 16e6),
        name="attention_forward",
    )(*parts, wq, wk, wv, bq, bv, live)


def attn_bwd_heads(al, wo, q, k, v, e_i, inv_i, mt_i, dm, dq, dk, dv):
    step = pl.program_id(0)

    @pl.when(step == 0)
    def _():
        dm[...] = nt(al[...], wo[...]).astype(LOW)

    lane = lax.broadcasted_iota(jnp.int32, (1, 128), 1)
    cols = pl.ds(pl.multiple_of(step * 128, 128), 128)
    q2, k2, v2 = q[...], k[...], v[...]
    dmt = dm[:, cols].astype(F32).T
    kt = k2.astype(F32).T.astype(LOW)
    prod = dmt * mt_i[...].astype(F32)
    inv2 = [inv_i[h] for h in range(2)]
    dots = jnp.concatenate([dmt[64 * h : 64 * h + 64] * inv2[h] for h in range(2)], axis=0)
    dot_low = dots.astype(LOW)
    dout = dots.T.astype(LOW)
    dqt, dk2, dv2 = [], [], []
    for h in range(2):
        mine = (lane // 64) == h
        e = e_i[h]
        delta = jnp.sum(prod[64 * h : 64 * h + 64], axis=0, keepdims=True) * inv2[h]
        vz = jnp.where(mine, v2, jnp.zeros((), LOW))
        dp = nn(vz, dot_low)
        ds = (e.astype(F32) * (dp - delta)).astype(LOW)
        dv2.append(nn(e, dout))
        dk2.append(nn(ds, q2))
        dqt.append(nn(kt[64 * h : 64 * h + 64], ds))
    first = lane < 64
    dv[:, cols] = jnp.where(first, dv2[0], dv2[1]).astype(LOW)
    dk[:, cols] = jnp.where(first, dk2[0], dk2[1]).astype(LOW)
    dq[:, cols] = jnp.concatenate(dqt, axis=0).T.astype(LOW)


def embed_part(dq, dk, dv, wq, wk, wv, rows):
    return (
        nt(dq[rows, :], wq[...]) * HEAD_DIM ** (-0.5) + nt(dk[rows, :], wk[...]) + nt(dv[rows, :], wv[...])
    )


def attn_bwd_kernel(
    place, al, wo, q, k, v, e_i, inv_i, mt_i, wq_a, wk_a, wv_a, x_a, base_a, mixed_a,
    res0, res1, res2, res3, pool, vec1, vec2, ib, p0, p1, p2, p3, send, keep,
    dm, dq, dk, dv, wq, wk, wv, x, base, mixed, eg, sems
):
    pairs = ((wq_a, wq), (wk_a, wk), (wv_a, wv), (x_a, x), (base_a, base), (mixed_a, mixed))
    loads = [pltpu.make_async_copy(a, b, sems.at[i]) for i, (a, b) in enumerate(pairs)]

    @pl.when(pl.program_id(0) == 0)
    def _():
        for load in loads:
            load.start()

    attn_bwd_heads(al, wo, q, k, v, e_i, inv_i, mt_i, dm, dq, dk, dv)

    @pl.when(pl.program_id(0) == pl.num_programs(0) - 1)
    def _():
        for load in loads:
            load.wait()
        scale = HEAD_DIM ** (-0.5)
        s, d = base.shape
        n, share = s // 4, d // 4
        core = place[1]

        def put(owner, at, values):
            for c in range(2):

                @pl.when(core == c)
                def _():
                    out = keep if owner == c else send
                    for z in range(4):
                        out[z, at, :] = values(z)

        pieces = ((x, dq, scale), (x, dk, 1.0), (x, dv, 1.0), (mixed, al, 1.0))
        for i, (left, right, factor) in enumerate(pieces):
            weight = (tn(left[...], right[...]) * factor).astype(LOW)
            start = share * (i % 2)
            put(i // 2, slice(start, start + share), lambda z: weight[share * z : share * z + share])
        for m, part in enumerate((p0, p1, p2, p3)):
            at = slice(m * n, m * n + n)
            value = (base[at, :] + embed_part(dq, dk, dv, wq, wk, wv, at)).astype(LOW)
            eg[m] = value
            part[0:n, :] = value
            part[n : 2 * n, :] = (res0, res1, res2, res3)[m][...]
            part[2 * n : 2 * n + 16, :] = pool[...]
        put(0, slice(2 * share, 2 * share + n), lambda z: eg[(place[0] + 4 - z) % 4])
        vectors = [
            jnp.sum(dq[...].astype(F32), axis=0, keepdims=True) * scale,
            jnp.sum(dv[...].astype(F32), axis=0, keepdims=True),
            vec1[2:3, :],
            vec1[0:1, :],
            vec1[1:2, :],
            vec2[2:3, :],
            vec2[0:1, :],
            vec2[1:2, :],
        ]
        vectors += [ib[f] for f in range(4)] + [jnp.zeros((n - 12, d), F32)]
        vectors = jnp.concatenate(vectors, axis=0).astype(LOW)
        put(1, slice(2 * share, 2 * share + n), lambda z: vectors)


def attn_bwd(place, al, wo, q, k, v, e, inv, mt, wq, wk, wv, x, base, mixed, res, pool, vec1, vec2, ib):
    s, d = q.shape
    steps = d // 128
    heads = d // HEAD_DIM
    col = pl.BlockSpec((s, 128), lambda h, p: (0, h))
    small = [whole(part.shape) for part in res]
    small += [whole(pool.shape), whole(vec1.shape), whole(vec2.shape), whole(ib.shape)]
    ins = [
        whole((s, d)),
        whole((d, d)),
        col,
        col,
        col,
        pl.BlockSpec((2, s, s), lambda h, p: (h, 0, 0)),
        pl.BlockSpec((2, 1, s), lambda h, p: (h, 0, 0)),
        pl.BlockSpec((128, s), lambda h, p: (h, 0)),
    ]
    shapes = [((s // 2 + 16, d), LOW)] * 4 + [((4, d // 2 + s // 4, d), LOW)] * 2
    return pl.pallas_call(
        attn_bwd_kernel,
        grid_spec=prefetch(
            1,
            (steps,),
            ins + [pl.BlockSpec(memory_space=pl.ANY)] * 6 + small,
            [whole(shape) for shape, _ in shapes],
            [pltpu.VMEM((s, d), LOW)] * 4
            + [pltpu.VMEM((d, d), LOW)] * 3
            + [pltpu.VMEM((s, d), LOW), pltpu.VMEM((s, d), F32), pltpu.VMEM((s, d), LOW)]
            + [pltpu.VMEM((4, s // 4, d), LOW), pltpu.SemaphoreType.DMA((6,))],
        ),
        out_shape=[struct(*one) for one in shapes],
        compiler_params=params(),
        cost_estimate=cost(14 * s * d * d + 8 * s * s * 256 * heads, 28e6),
        name="attention_backward",
    )(place, al, wo, q, k, v, e, inv, mt, wq, wk, wv, x, base, mixed, *res, pool, vec1, vec2, ib)


def normalize(values):
    center = values - jnp.mean(values, axis=-1, keepdims=True)
    root = lax.rsqrt(jnp.mean(center * center, axis=-1, keepdims=True) + EPSILON)
    return center * root, root


def normalize_back(upstream, normed, root, gain):
    scaled = upstream * gain
    plain = jnp.mean(scaled, axis=-1, keepdims=True)
    crossed = jnp.mean(scaled * normed, axis=-1, keepdims=True)
    return root * (scaled - plain - normed * crossed)


def gelu_pair(v):
    cdf = lax.erf(v * 0.7071067811865476) * 0.5 + 0.5
    bell = jnp.exp(v * v * -0.5)
    return v * cdf, cdf + v * (bell * 0.3989422804014327)


def ff_kernel(
    row0, mixed, wo, bo, x, g1, s1, w1, b1, w2, b2, g2, s2, wp, bp, u0, u1, u2, u3,
    lhs_o, rhs_o, t0, t1, t2, t3, pool_o, al_o, fb_o, vec1_o, vec2_o, ib_o,
    w1s, w2s, wps, ups, gp, normed1, acc, sb, sems, *, chunk
):
    s, d = x.shape
    blocks = w1s.shape[0]
    ol_o, hid_o = lhs_o.at[0], lhs_o.at[1]
    act_o, il_o = rhs_o.at[0], rhs_o.at[1]
    n = s // 4
    per = chunk // n
    outs = (t0, t1, t2, t3)
    chunks = [slice(r, r + chunk) for r in range(0, s, chunk)]

    def load1(f):
        return pltpu.make_async_copy(w1.at[:, pl.ds(f * d, d)], w1s.at[f], sems.at[f])

    def load2(f):
        return pltpu.make_async_copy(w2.at[pl.ds(f * d, d), :], w2s.at[f], sems.at[blocks + f])

    loads = [pltpu.make_async_copy(wp, wps, sems.at[2 * blocks])]
    for m, part in enumerate((u0, u1, u2, u3)):
        rows = part.at[pl.ds(n, n + 16), :]
        loads.append(pltpu.make_async_copy(rows, ups.at[m], sems.at[2 * blocks + 1 + m]))
    for f in range(blocks):
        load1(f).start()
        load2(f).start()
    for load in loads:
        load.start()

    roots1 = []
    for rows in chunks:
        val = nn(mixed[rows, :], wo[...]) + bo[...].astype(F32) + x[rows, :].astype(F32)
        normed, root = normalize(val)
        roots1.append(root)
        normed1[rows, :] = normed
        h = (normed * g1[...].astype(F32) + s1[...].astype(F32)).astype(LOW)
        hid_o[rows, :] = h
        acc[rows, :] = h.astype(F32) + b2[...].astype(F32)

    def forward(f, carry):
        load1(f).wait()
        load2(f).wait()
        for rows in chunks:
            pre = nn(hid_o[rows, :], w1s[f]) + b1[f].astype(F32)
            act, slope = gelu_pair(pre)
            act = act.astype(LOW)
            act_o[f, rows, :] = act
            gp[f, rows, :] = slope.astype(LOW)
            acc[rows, :] += nn(act, w2s[f])
        return carry

    lax.fori_loop(0, blocks, forward, 0)
    for load in loads:
        load.wait()

    gain = g2[...].astype(F32)
    roots2 = []
    for k, rows in enumerate(chunks):
        normed, root = normalize(acc[rows, :])
        roots2.append(root)
        res = (normed * gain + s2[...].astype(F32)).astype(LOW)
        al_o[rows, :] = res
        for j in range(per):
            outs[k * per + j][...] = res[j * n : j * n + n, :]
        acc[rows, :] = normed
    cls = al_o[pl.ds(pl.multiple_of(row0[0], 128), 16), :]
    pooled = jnp.tanh(nn(cls, wps[...]) + bp[...].astype(F32))
    pull = 0.0
    for m in range(4):
        terms = ups[m, n : n + 16, :].astype(F32)
        terms = jnp.broadcast_to(terms[0:1] + terms[1:2], (8, d))
        pull = pull + pltpu.roll(terms, ((row0[2] + 4 - m) % 4) * (d // 4), 1)
    pre = pull[:1] * (1.0 - pooled * pooled)
    cls_grad = nt(pre.astype(LOW), wps[...])[:1]
    high = pooled[:1].astype(LOW).astype(F32)
    pool = [cls[:1].astype(F32), pre[:1], high, pooled[:1] - high, jnp.zeros((12, d), F32)]
    pool_o[...] = jnp.concatenate(pool, axis=0).astype(LOW)
    gs, ss, bs = 0.0, 0.0, 0.0
    for k, rows in enumerate(chunks):
        ids = lax.broadcasted_iota(jnp.int32, (chunk, 1), 0) + rows.start
        up = jnp.concatenate([ups[k * per + j, 0:n, :] for j in range(per)], axis=0).astype(F32)
        upstream = up + jnp.where(ids == row0[0], cls_grad, 0.0)
        normed = acc[rows, :]
        back = normalize_back(upstream, normed, roots2[k], gain)
        sb[rows, :] = back
        low = back.astype(LOW)
        ol_o[rows, :] = low
        gs = gs + jnp.sum(upstream * normed, axis=0, keepdims=True)
        ss = ss + jnp.sum(upstream, axis=0, keepdims=True)
        bs = bs + jnp.sum(low.astype(F32), axis=0, keepdims=True)
    live = row0[1].astype(F32)
    vec2_o[0:1, :] = gs * live
    vec2_o[1:2, :] = ss * live
    vec2_o[2:3, :] = bs * live

    def backward(f, carry):
        bias = 0.0
        for rows in chunks:
            low = (nt(ol_o[rows, :], w2s[f]) * gp[f, rows, :].astype(F32)).astype(LOW)
            il_o[f, rows, :] = low
            bias = bias + jnp.sum(low.astype(F32), axis=0, keepdims=True)
            sb[rows, :] += nt(low, w1s[f])
        ib_o[f] = bias
        return carry

    lax.fori_loop(0, blocks, backward, 0)
    gain = g1[...].astype(F32)
    gs, ss, bs = 0.0, 0.0, 0.0
    for k, rows in enumerate(chunks):
        upstream = sb[rows, :]
        normed = normed1[rows, :]
        back = normalize_back(upstream, normed, roots1[k], gain)
        fb_o[rows, :] = back
        low = back.astype(LOW)
        al_o[rows, :] = low
        gs = gs + jnp.sum(upstream * normed, axis=0, keepdims=True)
        ss = ss + jnp.sum(upstream, axis=0, keepdims=True)
        bs = bs + jnp.sum(low.astype(F32), axis=0, keepdims=True)
    vec1_o[0:1, :] = gs
    vec1_o[1:2, :] = ss
    vec1_o[2:3, :] = bs


def feed_forward(row0, mixed, wo, bo, x, g1, s1, w1, b1, w2, b2, g2, s2, wp, bp, ups, chunk=256):
    s, d = x.shape
    ff = w1.shape[1]
    blocks = ff // d
    full, row = whole((s, d)), whole((1, d))
    away = pl.BlockSpec(memory_space=pl.ANY)
    part = (s // 4 + 16, d)
    return pl.pallas_call(
        functools.partial(ff_kernel, chunk=chunk),
        grid_spec=prefetch(
            1,
            (1,),
            [full, whole((d, d)), row, full, row, row, away, whole((blocks, 1, d)), away, row, row, row]
            + [away, row]
            + [away] * 4,
            [whole((2, s, d)), whole((2, blocks, s, d))]
            + [whole((s // 4, d))] * 4
            + [whole((16, d)), full, full, whole((8, d)), whole((8, d)), whole((blocks, 1, d))],
            [
                pltpu.VMEM((blocks, d, d), LOW),
                pltpu.VMEM((blocks, d, d), LOW),
                pltpu.VMEM((d, d), LOW),
                pltpu.VMEM((4,) + part, LOW),
                pltpu.VMEM((blocks, s, d), LOW),
                pltpu.VMEM((s, d), F32),
                pltpu.VMEM((s, d), F32),
                pltpu.VMEM((s, d), F32),
                pltpu.SemaphoreType.DMA((2 * blocks + 5,)),
            ],
        ),
        out_shape=[struct((2, s, d), LOW), struct((2, blocks, s, d), LOW)]
        + [struct((s // 4, d), LOW)] * 4
        + [
            struct((16, d), LOW),
            struct((s, d), LOW),
            struct((s, d), F32),
            struct((8, d), F32),
            struct((8, d), F32),
            struct((blocks, 1, d), F32),
        ],
        compiler_params=params(),
        cost_estimate=cost(2 * s * d * d + 8 * s * d * ff, 30e6),
        name="feed_forward",
    )(row0, mixed, wo, bo, x, g1, s1, w1, b1.reshape(blocks, 1, d), w2, b2, g2, s2, wp, bp, *ups)


def tn(a, b):
    return lax.dot_general(a, b, (((0,), (0,)), ((), ())), preferred_element_type=F32)


def prefetch(count, grid, in_specs, out_specs, scratch=()):
    return pltpu.PrefetchScalarGridSpec(
        num_scalar_prefetch=count,
        grid=grid,
        in_specs=in_specs,
        out_specs=out_specs,
        scratch_shapes=list(scratch),
    )


def index_kernel(ids, req_o, col_o, row_o, *, rows, slots):
    count, n = ids.shape
    owners = req_o.shape[0]
    owner = ((ids[...].astype(F32) + 0.5) * (1.0 / rows)).astype(jnp.int32)
    local = ids[...] - owner * rows + 1
    flat = [owner.astype(F32), (local // 64).astype(F32), (local % 64).astype(F32)]
    flat = jnp.concatenate(flat + [jnp.zeros((16 - 3 * count, n), F32)], axis=0)
    cols = flat.T
    lane = lax.broadcasted_iota(jnp.int32, (n, owners), 1).astype(F32)
    before = lax.broadcasted_iota(jnp.int32, (n, n), 1) < lax.broadcasted_iota(jnp.int32, (n, n), 0)
    before = jnp.where(before, 1.0, 0.0).astype(LOW)
    seen = jnp.zeros((1, owners), F32)
    high, low, places = 0.0, 0.0, []
    slot_lane = lax.broadcasted_iota(jnp.int32, (n, 128), 1).astype(F32)
    for s in range(count):
        hot = jnp.where(lane == cols[:, s : s + 1], 1.0, 0.0)
        hot_low = hot.astype(LOW)
        within = jnp.sum((nn(before, hot_low) + seen) * hot, axis=1, keepdims=True)
        seen = seen + jnp.sum(hot, axis=0, keepdims=True)
        place = cols[:, s : s + 1] * slots + within
        places.append(place)
        here = slot_lane == within
        put_high = jnp.where(here, cols[:, count + s : count + s + 1], 0.0).astype(LOW)
        put_low = jnp.where(here, cols[:, 2 * count + s : 2 * count + s + 1], 0.0).astype(LOW)
        high = high + tn(hot_low, put_high)
        low = low + tn(hot_low, put_low)
    req_o[...] = (high * 64.0 + low).astype(jnp.int32)[:, :slots] - 1
    places.append(jnp.full((n, 1), -1.0, F32))
    table = jnp.concatenate([jnp.broadcast_to(p, (n, 8)) for p in places], axis=1)
    table = jnp.concatenate([table, jnp.zeros((n, 128 - table.shape[1]), F32)], axis=1)
    turned = table.T.astype(jnp.int32)
    for s in range(count + 1):
        col_o[s] = places[s].astype(jnp.int32)
        row_o[s] = turned[8 * s : 8 * s + 1, :]


def index_requests(ids, rows, owners, slots):
    count, n = ids.shape
    return pl.pallas_call(
        functools.partial(index_kernel, rows=rows, slots=slots),
        grid=(1,),
        in_specs=[whole((count, n))],
        out_specs=[whole((owners, slots)), whole((count + 1, n, 1)), whole((count + 1, 1, n))],
        out_shape=[
            struct((owners, slots), jnp.int32),
            struct((count + 1, n, 1), jnp.int32),
            struct((count + 1, 1, n), jnp.int32),
        ],
        compiler_params=params(),
        cost_estimate=cost(0, 1e6),
        name="index_requests",
    )(ids)


def gather_kernel(fetch, table, out, acc, *, rows):
    step = pl.program_id(0)
    last = pl.num_programs(0) - 1
    blk = table.shape[0]
    ids = lax.broadcasted_iota(jnp.int32, (1, blk), 1) + step * blk
    hot = jnp.where(ids == fetch[...], 1.0, 0.0).astype(LOW)

    def add(block):
        part = nn(hot, block)

        @pl.when(step == 0)
        def _():
            acc[...] = part

        @pl.when(step > 0)
        def _():
            acc[...] += part

    @pl.when(step < last)
    def _():
        add(table[...])

    @pl.when(step == last)
    def _():
        ids_col = lax.broadcasted_iota(jnp.int32, (blk, 1), 0) + step * blk
        add(jnp.where(ids_col < rows, table[...], jnp.zeros((), LOW)))
        out[...] = acc[...].astype(LOW)


def gather_rows(fetch, table, blk=1024):
    slots = fetch.shape[0]
    rows, d = table.shape
    return pl.pallas_call(
        functools.partial(gather_kernel, rows=rows),
        grid=(pl.cdiv(rows, blk),),
        in_specs=[whole((slots, 1)), pl.BlockSpec((blk, d), lambda i: (i, 0))],
        out_specs=whole((slots, d)),
        out_shape=struct((slots, d), LOW),
        scratch_shapes=[pltpu.VMEM((slots, d), F32)],
        compiler_params=params(),
        cost_estimate=cost(2 * slots * rows * d, 8e6),
        name="gather_rows",
    )(fetch, table)


def embed_kernel(place, slot, replies, pos, grads, terms, o0, o1, o2, o3):
    n = pos.shape[0]
    ids = lax.broadcasted_iota(jnp.int32, (1, replies.shape[0]), 1)
    for m, out in enumerate((o0, o1, o2, o3)):
        sent = (place[0] + m) % 4
        here = jnp.minimum(sent, 2)
        hot = jnp.where(ids == slot[sent], 1.0, 0.0).astype(LOW)
        live = jnp.where(sent < 3, 1.0, 0.0)
        out[0:n, :] = ((nn(hot, replies[...]) + pos[...].astype(F32)) * live).astype(LOW)
        out[n : 2 * n, :] = (grads[here].astype(F32) * live).astype(LOW)
        out[2 * n : 2 * n + 16, :] = (terms[here].astype(F32) * live).astype(LOW)


def embed_parts(place, slot, replies, pos, grads, terms):
    slots, d = replies.shape
    n = pos.shape[0]
    out = (2 * n + 16, d)
    return pl.pallas_call(
        embed_kernel,
        grid_spec=prefetch(
            1,
            (1,),
            [whole((4, n, 1)), whole((slots, d)), whole((n, d))]
            + [whole(grads.shape), whole(terms.shape)],
            [whole(out)] * 4,
        ),
        out_shape=[struct(out, LOW)] * 4,
        compiler_params=params(),
        cost_estimate=cost(2 * slots * 4 * n * d, 3e6),
        name="embed_parts",
    )(place, slot, replies, pos, grads, terms)


def outgoing_kernel(place, slot, p0, p1, p2, p3, out):
    ids = lax.broadcasted_iota(jnp.int32, (out.shape[0], 1), 0)
    total = 0.0
    for m, part in enumerate((p0, p1, p2, p3)):
        sent = (place[0] + m) % 4
        hot = jnp.where(ids == slot[sent], 1.0, 0.0).astype(LOW)
        total = total + nn(hot, part[...])
    out[...] = total.astype(LOW)


def outgoing_rows(place, slot, parts, slots):
    n = slot.shape[2]
    d = parts[0].shape[1]
    return pl.pallas_call(
        outgoing_kernel,
        grid_spec=prefetch(
            1,
            (1,),
            [whole((4, 1, n))] + [pl.BlockSpec((n, d), lambda i, p: (0, 0))] * 4,
            whole((slots, d)),
        ),
        out_shape=struct((slots, d), LOW),
        compiler_params=params(),
        cost_estimate=cost(2 * slots * 4 * n * d, 3e6),
        name="outgoing_rows",
    )(place, slot, *parts)


def table_kernel(fetch, incoming, out):
    blk = out.shape[0]
    ids = lax.broadcasted_iota(jnp.int32, (blk, 1), 0) + pl.program_id(0) * blk
    out[...] = nn(jnp.where(ids == fetch[...], 1.0, 0.0).astype(LOW), incoming[...])


def table_grad(fetch, incoming, rows, blk=1024):
    slots, d = incoming.shape
    return pl.pallas_call(
        table_kernel,
        grid=(pl.cdiv(rows, blk),),
        in_specs=[whole((1, slots)), whole((slots, d))],
        out_specs=pl.BlockSpec((blk, d), lambda i: (i, 0)),
        out_shape=struct((rows, d), F32),
        compiler_params=params(),
        cost_estimate=cost(2 * slots * rows * d, 13e6),
        name="table_gradient",
    )(fetch, incoming)


def unpermute_kernel(place, p0, p1, p2, p3, out):
    for m, part in enumerate((p0, p1, p2, p3)):
        sent = (place[0] + m) % 4

        @pl.when(sent < 3)
        def _():
            out[sent] = part[...]


def unpermute(place, parts, n):
    d = parts[0].shape[1]
    return pl.pallas_call(
        unpermute_kernel,
        grid_spec=prefetch(
            1, (1,), [pl.BlockSpec((n, d), lambda i, p: (1, 0))] * 4, whole((3, n, d))
        ),
        out_shape=struct((3, n, d), parts[0].dtype),
        compiler_params=params(),
        cost_estimate=cost(0, 2e6),
        name="unpermute",
    )(place, *parts)


def ff_send_kernel(which, left, right, out):
    out[0] = tn(left[0], right[0, 0]).astype(LOW)


def ff_specs(s, d):
    return [
        pl.BlockSpec((1, s, d), lambda f, w: (w[0], 0, 0)),
        pl.BlockSpec((1, 1, s, d), lambda f, w: (w[0], f, 0, 0)),
    ]


def ff_send(which, left, right):
    _, blocks, s, d = right.shape
    return pl.pallas_call(
        ff_send_kernel,
        grid_spec=prefetch(
            1, (blocks,), ff_specs(s, d), pl.BlockSpec((1, d, d), lambda f, w: (f, 0, 0))
        ),
        out_shape=struct((blocks, d, d), LOW),
        compiler_params=params(),
        cost_estimate=cost(2 * blocks * s * d * d, 9e6),
        name="ff_send",
    )(which, left, right)


def ff_keep_kernel(place, left, right, got, o0, o1, o2, o3, acc):
    f = pl.program_id(0)
    total = tn(left[0], right[0, 0]) + got[0].astype(F32)
    acc[f] = total.astype(LOW).reshape(acc.shape[1:])

    @pl.when(f == pl.num_programs(0) - 1)
    def _():
        for m, out in enumerate((o0, o1, o2, o3)):
            index = (place[1] + m) % 4

            @pl.when(place[0] == 0)
            def _():
                for z in range(4):
                    out[z] = acc[z, index]

            @pl.when(place[0] == 1)
            def _():
                out[...] = acc[index]


def ff_keep(place, left, right, got):
    _, blocks, s, d = right.shape
    shape = (4, d // 4, d)
    return pl.pallas_call(
        ff_keep_kernel,
        grid_spec=prefetch(
            1,
            (blocks,),
            ff_specs(s, d) + [pl.BlockSpec((1, d, d), lambda f, w: (f, 0, 0))],
            [whole(shape)] * 4,
            [pltpu.VMEM((blocks,) + shape, LOW)],
        ),
        out_shape=[struct(shape, LOW)] * 4,
        compiler_params=params(),
        cost_estimate=cost(2 * blocks * s * d * d, 14e6),
        name="ff_keep",
    )(place, left, right, got)


def core_add_kernel(place, own, got, o0, o1, o2, o3):
    rows = o0.shape[1]
    for m, out in enumerate((o0, o1, o2, o3)):
        at = pl.ds(pl.multiple_of((place[0] + m) % 4 * rows, rows), rows)
        out[...] = (own[:, at, :].astype(F32) + got[:, at, :].astype(F32)).astype(LOW)


def core_add(place, own, got):
    out = (4, own.shape[1] // 4, own.shape[2])
    return pl.pallas_call(
        core_add_kernel,
        grid_spec=prefetch(1, (1,), [whole(own.shape)] * 2, [whole(out)] * 4),
        out_shape=[struct(out, LOW)] * 4,
        compiler_params=params(),
        cost_estimate=cost(0, 9e6),
        name="core_add",
    )(place, own, got)


def add4(a, b, c, d):
    return a[...].astype(F32) + b[...].astype(F32) + c[...].astype(F32) + d[...].astype(F32)


def ring_add_kernel(place, p0, p1, p2, p3, o0, o1, o2, o3, acc):
    acc[...] = add4(p0, p1, p2, p3)
    rows = o0.shape[1]
    for m, out in enumerate((o0, o1, o2, o3)):
        at = pl.ds(pl.multiple_of((place[0] + m) % 4 * rows, rows), rows)
        out[...] = acc[:, at, :].astype(LOW)


def ring_add(place, parts):
    shape = parts[0].shape
    out = (4, shape[1] // 4, shape[2])
    return pl.pallas_call(
        ring_add_kernel,
        grid_spec=prefetch(
            1, (1,), [whole(shape)] * 4, [whole(out)] * 4, [pltpu.VMEM(shape, F32)]
        ),
        out_shape=[struct(out, LOW)] * 4,
        compiler_params=params(),
        cost_estimate=cost(0, 6e6),
        name="ring_add",
    )(place, *parts)


def join_kernel(place, a0, a1, a2, a3, b0, b1, b2, b3, o0, o1, o2, o3, acc):
    acc[:, 0:48, :] = add4(a0, a1, a2, a3)
    acc[:, 48:80, :] = add4(b0, b1, b2, b3)
    for m, out in enumerate((o0, o1, o2, o3)):
        out[...] = acc[(place[0] + m) % 4].astype(LOW)


def join(place, first, second):
    d = first[0].shape[2]
    return pl.pallas_call(
        join_kernel,
        grid_spec=prefetch(
            1,
            (1,),
            [whole(first[0].shape)] * 4 + [whole(second[0].shape)] * 4,
            [whole((80, d))] * 4,
            [pltpu.VMEM((4, 80, d), F32)],
        ),
        out_shape=[struct((80, d), LOW)] * 4,
        compiler_params=params(),
        cost_estimate=cost(0, 4e6),
        name="join",
    )(place, *first, *second)


def piece_kernel(f0, f1, f2, f3, r0, r1, r2, r3, out):
    pool = [part[...].astype(F32)[0:2] for part in (r0, r1, r2, r3)]
    pool.append(jnp.zeros((8, out.shape[1]), F32))
    out[...] = jnp.concatenate([add4(f0, f1, f2, f3)] + pool, axis=0).astype(LOW)


def piece_rows(parts, pool):
    d = parts[0].shape[1]
    return pl.pallas_call(
        piece_kernel,
        grid=(1,),
        in_specs=[whole(p.shape) for p in parts]
        + [pl.BlockSpec((16, d), lambda i: (16, 0)) for p in pool],
        out_specs=whole((96, d)),
        out_shape=struct((96, d), LOW),
        compiler_params=params(),
        cost_estimate=cost(0, 1e6),
        name="piece_rows",
    )(*parts, *pool)


def order_kernel(place, p0, p1, p2, p3, out):
    for m, part in enumerate((p0, p1, p2, p3)):
        out[(place[0] + 4 - m) % 4] = part[...]


def order(place, parts):
    shape = parts[0].shape
    return pl.pallas_call(
        order_kernel,
        grid_spec=prefetch(1, (1,), [whole(shape)] * 4, whole((4,) + shape)),
        out_shape=struct((4,) + shape, LOW),
        compiler_params=params(),
        cost_estimate=cost(0, 3e6),
        name="order",
    )(place, *parts)


def finish_kernel(
    place, own, got, outer_o, inner_o, q_o, k_o, v_o, out_o, pos_o, vec_o, pw_o, pb_o, acc
):
    d = outer_o.shape[0]

    def fill(zero, one):
        pool = []
        for i in range(4):
            for k in range(4):
                at = 96 * k
                r = 192 * i + 48 * k
                acc[r : r + 48, :] = zero[i, at : at + 48, :].astype(F32)
                cols = slice(d * i, d * i + d)
                inner_o[48 * k : 48 * k + 48, cols] = one[i, at : at + 48, :].astype(F32)
                r = 128 * i + 32 * k
                first = zero[i, at + 48 : at + 80, :].astype(F32)
                second = one[i, at + 48 : at + 80, :].astype(F32)
                if r < 192:
                    q_o[r : r + 32, :] = first
                    v_o[r : r + 32, :] = second
                elif r < 384:
                    k_o[r - 192 : r - 160, :] = first
                    out_o[r - 192 : r - 160, :] = second
                else:
                    pos_o[r - 384 : r - 352, :] = first
                    if r == 384:
                        vec_o[...] = second[0:16]
                pool.append(zero[i, at + 80 : at + 96, :].astype(F32)[0:8])
                pool.append(one[i, at + 80 : at + 96, :].astype(F32)[0:8])
        outer_o[...] = acc[...].T
        pool = jnp.concatenate(pool, axis=0)
        even = lax.broadcasted_iota(jnp.int32, (pool.shape[0], 1), 0) % 2 == 0
        below = jnp.concatenate([pool[1:], pool[:1]], axis=0)
        acc[...] = tn(jnp.where(even, pool, 0.0).astype(LOW), below.astype(LOW))
        pb_o[...] = jnp.sum(jnp.where(even, 0.0, pool), axis=0, keepdims=True)

    @pl.when(place[0] == 0)
    def _():
        fill(own, got)

    @pl.when(place[0] == 1)
    def _():
        fill(got, own)

    pw_o[...] = acc[pl.ds(pl.multiple_of(place[1] * (d // 4), d // 4), d // 4), :]


def finish(place, own, got):
    d = own.shape[2]
    share = d // 4
    shapes = [(d, d), (share, 4 * d)] + [(share, d)] * 4 + [(128, d), (16, d), (share, d), (1, d)]
    return pl.pallas_call(
        finish_kernel,
        grid_spec=prefetch(
            1,
            (1,),
            [whole(own.shape)] * 2,
            [whole(s) for s in shapes],
            [pltpu.VMEM((d, d), F32)],
        ),
        out_shape=[struct(s, F32) for s in shapes],
        compiler_params=params(),
        cost_estimate=cost(0, 14e6),
        name="finish",
    )(place, own, got)


def pooled_kernel(place, p0, p1, p2, p3, out):
    for m, part in enumerate((p0, p1, p2, p3)):
        two = part[...].astype(F32)
        row = two[2:3] + two[3:4]
        out[(place[0] + m) % 4] = pltpu.roll(
            jnp.broadcast_to(row, (8, row.shape[1])), row.shape[1] - 192 * place[0], 1
        )


def pooled_rows(place, parts):
    d = parts[0].shape[1]
    below = pl.BlockSpec((16, d), lambda i, p: (16, 0))
    return pl.pallas_call(
        pooled_kernel,
        grid_spec=prefetch(1, (1,), [below] * 4, whole((4, 8, d))),
        out_shape=struct((4, 8, d), F32),
        compiler_params=params(),
        name="pooled_rows",
    )(place, *parts)


def shift_pairs(step, axes):
    pairs = []
    for y in range(4):
        for x in range(4):
            for c in range(2):
                to = (y, (x + step) % 4) if axes[c] == "x" else ((y + step) % 4, x)
                pairs.append(((y * 4 + x) * 2 + c, (to[0] * 4 + to[1]) * 2 + c))
    return pairs


def shift_first(array, step):
    return lax.ppermute(array, "batch", shift_pairs(step, "xy"))


def shift_second(array, step):
    return lax.ppermute(array, "batch", shift_pairs(step, "yx"))


def shift_z(array, step):
    return lax.ppermute(array, "seq", [(z, (z + step) % 4) for z in range(4)])


def swap_core(array):
    return lax.ppermute(array, "batch", [(i, i ^ 1) for i in range(32)])


def ring_send(parts, shift):
    return [parts[0], shift(parts[1], 1), shift(parts[2], 2), shift(parts[3], 3)]


def to_sentence(parts):
    out = [parts[0]]
    for step in (1, 2, 3):
        pairs = [(z, (z + step) % 4) for z in range(4) if (z + step) % 4 < 3]
        out.append(lax.ppermute(parts[step], "seq", pairs))
    return out


def from_sentence(parts):
    out = [parts[0]]
    for step in (1, 2, 3):
        pairs = [((z + step) % 4, z) for z in range(4) if (z + step) % 4 < 3]
        out.append(lax.ppermute(parts[step], "seq", pairs))
    return out


def tie(array, *after):
    return lax.optimization_barrier((array,) + after)[0]


def per_device(
    token_ids,
    lengths,
    word_table,
    positions,
    query_weight,
    key_weight,
    value_weight,
    query_bias,
    value_bias,
    output_weight,
    output_bias,
    first_gain,
    first_shift,
    inner_weight,
    inner_bias,
    outer_weight,
    outer_bias,
    second_gain,
    second_shift,
    pooler_weight,
    pooler_bias,
    out_grad,
    pooled_grad,
):
    num_sent, local_len = token_ids.shape
    table_rows, width = word_table.shape
    all_count = lax.axis_size("seq") * lax.axis_size("batch")
    z = lax.axis_index("seq")
    batch_place = lax.axis_index("batch")
    core = batch_place % 2
    x = (batch_place // 2) % 4
    y = batch_place // 8

    first = jnp.where(core == 0, x, y)
    second = jnp.where(core == 0, y, x)

    def scalars(*values):
        return jnp.stack([jnp.asarray(v, jnp.int32) for v in values])

    slots = 2 * num_sent * local_len // all_count
    all_slots = slots * all_count
    requests, slot_cols, slot_rows = index_requests(token_ids, table_rows, all_count, slots)
    arrived = lax.all_to_all(requests, ("batch", "seq"), split_axis=0, concat_axis=0, tiled=True)
    fetch = arrived.reshape(-1)
    found = gather_rows(fetch[:, None], word_table)
    replies = lax.all_to_all(
        found.reshape(all_count, slots, width),
        ("batch", "seq"),
        split_axis=0,
        concat_axis=0,
        tiled=True,
    ).reshape(all_slots, width)
    live = (z < 3).astype(jnp.int32)
    sentence = jnp.minimum(z, 2)

    def row(vector):
        return vector.reshape(1, -1)

    vectors = (
        query_bias,
        value_bias,
        output_bias,
        first_gain,
        first_shift,
        inner_bias,
        outer_bias,
        second_gain,
        second_shift,
        pooler_bias,
    )
    block_of = (z - jnp.arange(4, dtype=jnp.int32)) % 4
    place_of = block_of[:, None] * local_len + jnp.arange(local_len, dtype=jnp.int32)[None, :]
    live_keys = (place_of.reshape(-1, 1) < lengths[sentence]).astype(F32)

    high = pooled_grad.astype(LOW)
    terms = jnp.stack([high, (pooled_grad - high.astype(F32)).astype(LOW)], axis=1)
    terms = jnp.pad(terms, ((0, 0), (0, 14), (0, width - terms.shape[2])))
    early = [live_keys, terms] + [row(v) for v in vectors]
    replies, *early = lax.optimization_barrier([replies] + early)
    live_keys, terms = early[:2]
    q_bias, v_bias, o_bias, gain1, shift1, in_bias, out_bias, gain2, shift2, pool_bias = early[2:]
    embeds = to_sentence(
        embed_parts(scalars(z), slot_cols, replies, positions, out_grad, terms)
    )

    embed, query, key, value, expo, inverse, mixed_t, mixed = attn_fwd(
        embeds, query_weight, key_weight, value_weight, q_bias, v_bias, live_keys
    )
    (
        left,
        right,
        *result,
        pool,
        attention_low,
        first_back,
        vec1,
        vec2,
        inner_bias_grad,
    ) = feed_forward(
        scalars(sentence * local_len, live, z),
        mixed,
        output_weight,
        o_bias,
        embed,
        gain1,
        shift1,
        inner_weight,
        in_bias,
        outer_weight,
        out_bias,
        gain2,
        shift2,
        pooler_weight,
        pool_bias,
        embeds,
    )

    ff_other = ff_send(scalars(1 - core), left, right)
    ff_parts = ff_keep(scalars(core, first), left, right, swap_core(ff_other))
    attention_low = tie(attention_low, ff_parts[0])
    ff_parts = ring_send(ff_parts, shift_first)
    *embed_grad, rest_other, rest_own = attn_bwd(
        scalars(z, core),
        attention_low,
        output_weight,
        query,
        key,
        value,
        expo,
        inverse,
        mixed_t,
        query_weight,
        key_weight,
        value_weight,
        embed,
        first_back,
        mixed,
        result,
        pool,
        vec1,
        vec2,
        inner_bias_grad,
    )
    embed_grad, rest_other, rest_own, ff_parts = lax.optimization_barrier(
        (embed_grad, rest_other, rest_own, ff_parts)
    )

    returned = from_sentence(embed_grad)
    rest_parts = core_add(scalars(first), rest_own, swap_core(rest_other))
    ff_parts[0] = tie(ff_parts[0], rest_parts[0])
    rest_parts = ring_send(rest_parts, shift_first)
    ff_parts = ring_add(scalars(second), ff_parts)
    rest_parts[0] = tie(rest_parts[0], ff_parts[0])
    ff_parts = ring_send(ff_parts, shift_second)
    rest_parts = ring_add(scalars(second), rest_parts)
    returned[0] = tie(returned[0], rest_parts[0])
    outgoing = outgoing_rows(scalars(z), slot_rows, returned, all_slots)
    outgoing = outgoing.reshape(all_count, slots, width)
    rest_parts = ring_send(rest_parts, shift_second)
    rest_parts[0] = tie(rest_parts[0], outgoing)
    parts = ring_send(join(scalars(z), ff_parts, rest_parts), shift_z)
    piece = piece_rows(parts, returned)
    pieces = [piece] + [shift_second(piece, m) for m in (1, 2, 3)]
    pooled = pooled_rows(scalars(z), [tie(returned[0], piece)] + returned[1:])
    pooled = pooled[:num_sent, 0, : width // 4]
    hidden_out = unpermute(scalars(z), [tie(returned[0], piece)] + returned[1:], local_len)
    pieces[0] = tie(pieces[0], pooled, hidden_out)
    block = order(scalars(second), pieces).reshape(-1, width)
    blocks = [block] + [shift_first(block, m) for m in (1, 2, 3)]
    incoming = lax.all_to_all(
        tie(outgoing, block),
        ("batch", "seq"),
        split_axis=0,
        concat_axis=0,
        tiled=True,
    ).reshape(all_slots, width)
    grad_table = table_grad(fetch[None, :], incoming, table_rows)
    blocks[0] = tie(blocks[0], incoming)
    whole_own = order(scalars(first), blocks)
    incoming = tie(incoming, whole_own)
    whole_other = swap_core(whole_own)
    grad_table = table_grad(fetch[None, :], incoming, table_rows)
    whole_other = tie(whole_other, grad_table)
    (
        grad_outer,
        grad_inner,
        grad_query,
        grad_key,
        grad_value,
        grad_output,
        grad_positions,
        vectors,
        grad_pooler,
        pooler_bias_grad,
    ) = finish(scalars(core, z), whole_own, whole_other)

    share = width // 4
    mine = lax.dynamic_slice_in_dim(vectors[:8], z * share, share, 1)
    ff = inner_weight.shape[1]
    inner_bias_sum = lax.dynamic_slice_in_dim(vectors[8:12].reshape(-1), z * ff // 4, ff // 4, 0)
    pooler_bias_sum = lax.dynamic_slice_in_dim(pooler_bias_grad[0], z * share, share, 0)
    return (
        hidden_out,
        pooled,
        grad_table,
        grad_positions,
        grad_query,
        grad_key,
        grad_value,
        mine[0],
        mine[1],
        grad_output,
        mine[2],
        mine[3],
        mine[4],
        grad_inner,
        inner_bias_sum,
        grad_outer,
        mine[5],
        mine[6],
        mine[7],
        grad_pooler,
        pooler_bias_sum,
    )


def solution(mesh):
    in_specs = (
        P("batch", "seq"),
        P("batch"),
        P(("batch", "seq"), None),
        P("seq", None),
        P(),
        P(),
        P(),
        P(),
        P(),
        P(),
        P(),
        P(),
        P(),
        P(),
        P(),
        P(),
        P(),
        P(),
        P(),
        P(),
        P(),
        P("batch", "seq", None),
        P("batch", "seq"),
    )
    out_specs = (
        P("batch", "seq", None),
        P("batch", "seq"),
        P(("batch", "seq"), None),
        P("seq", None),
        P("seq", None),
        P("seq", None),
        P("seq", None),
        P("seq"),
        P("seq"),
        P("seq", None),
        P("seq"),
        P("seq"),
        P("seq"),
        P("seq", None),
        P("seq"),
        P("seq", None),
        P("seq"),
        P("seq"),
        P("seq"),
        P("seq", None),
        P("seq"),
    )
    return jax.shard_map(
        per_device, mesh=mesh, in_specs=in_specs, out_specs=out_specs, check_vma=False
    )
```

```python
import functools
import jax
import jax.numpy as jnp
from jax import lax
from jax.experimental import pallas as pl
from jax.experimental.pallas import tpu as pltpu
from jax.sharding import PartitionSpec as P

F32 = jnp.float32
LOW = jnp.bfloat16
EPSILON = 1e-12
MASKED = -1000000000.0
HEAD_DIM = 64
VMEM = 63 * 1024 * 1024
HALF = 384
SHARE = 0.02


def nn(a, b):
    return lax.dot_general(a, b, (((1,), (0,)), ((), ())), preferred_element_type=F32)


def nt(a, b):
    return lax.dot_general(a, b, (((1,), (1,)), ((), ())), preferred_element_type=F32)


def struct(shape, dtype):
    return jax.ShapeDtypeStruct(shape, dtype)


def whole(shape):
    zeros = (0,) * len(shape)
    return pl.BlockSpec(shape, lambda *_: zeros, pipeline_mode=pl.Buffered(1))


def cost(flops, size):
    return pl.CostEstimate(
        flops=int(flops * SHARE), bytes_accessed=int(size * SHARE), transcendentals=0
    )


def params(**kw):
    return pltpu.CompilerParams(vmem_limit_bytes=VMEM, **kw)


def attn_fwd_kernel(
    x0, x1, x2, x3, wq, wk, wv, bq, bv, live, x_o, q_o, k_o, v_o, e_o, inv_o, mt_o, mixed_o, x
):
    scale = HEAD_DIM ** (-0.5)
    n = x0.shape[0]

    @pl.when(pl.program_id(0) == 0)
    def _():
        for m, part in enumerate((x0, x1, x2, x3)):
            x[m * n : m * n + n, :] = part[...]
            x_o[m * n : m * n + n, :] = part[...]

    q = ((nn(x[...], wq[...]) + bq[...].astype(F32)) * scale).astype(LOW)
    q_o[...] = q
    k = nn(x[...], wk[...]).astype(LOW)
    k_o[...] = k
    v = nn(x[...], wv[...]) + bv[...].astype(F32)
    v_o[...] = v.astype(LOW)
    keep = live[...] > 0.0
    lane = lax.broadcasted_iota(jnp.int32, (1, 128), 1)
    for pair in range(q.shape[1] // 128):
        cols = slice(128 * pair, 128 * pair + 128)
        q2, k2 = q[:, cols], k[:, cols]
        vt = v[:, cols].T.astype(LOW)
        parts = []
        for h in range(2):
            kz = jnp.where((lane // 64) == h, k2, jnp.zeros((), LOW))
            s = nt(kz, q2)
            s = jnp.where(keep, s, MASKED)
            e = jnp.exp(s - jnp.max(s, axis=0, keepdims=True))
            inv = 1.0 / jnp.sum(e, axis=0, keepdims=True)
            eb = e.astype(LOW)
            e_o[2 * pair + h] = eb
            inv_o[2 * pair + h] = inv
            parts.append(nn(vt[64 * h : 64 * h + 64], eb) * inv)
        mt = jnp.concatenate(parts, axis=0)
        mt_o[cols, :] = mt.astype(LOW)
        mixed_o[:, cols] = mt.T.astype(LOW)


def attn_fwd(parts, wq, wk, wv, bq, bv, live, group=256):
    s, d = live.shape[0], wq.shape[0]
    n = s // 4
    hg = group // HEAD_DIM
    col = pl.BlockSpec((s, group), lambda h: (0, h))
    wcol = pl.BlockSpec((d, group), lambda h: (0, h))
    brow = pl.BlockSpec((1, group), lambda h: (0, h))
    heads = d // HEAD_DIM
    return pl.pallas_call(
        attn_fwd_kernel,
        grid=(d // group,),
        in_specs=[pl.BlockSpec((n, d), lambda h: (0, 0))] * 4 + [wcol, wcol, wcol, brow, brow, whole((s, 1))],
        out_specs=[
            whole((s, d)),
            col,
            col,
            col,
            pl.BlockSpec((hg, s, s), lambda h: (h, 0, 0)),
            pl.BlockSpec((hg, 1, s), lambda h: (h, 0, 0)),
            pl.BlockSpec((group, s), lambda h: (h, 0)),
            col,
        ],
        out_shape=[
            struct((s, d), LOW),
            struct((s, d), LOW),
            struct((s, d), LOW),
            struct((s, d), LOW),
            struct((heads, s, s), LOW),
            struct((heads, 1, s), F32),
            struct((d, s), LOW),
            struct((s, d), LOW),
        ],
        scratch_shapes=[pltpu.VMEM((s, d), LOW)],
        compiler_params=params(),
        cost_estimate=cost(6 * s * d * d + 4 * s * s * 256 * heads, 16e6),
        name="attention_forward",
    )(*parts, wq, wk, wv, bq, bv, live)


def attn_bwd_heads(al, wo, q, k, v, e_i, inv_i, mt_i, dm, dq, dk, dv):
    step = pl.program_id(0)

    @pl.when(step == 0)
    def _():
        dm[...] = nt(al[...], wo[...]).astype(LOW)

    lane = lax.broadcasted_iota(jnp.int32, (1, 128), 1)
    cols = pl.ds(pl.multiple_of(step * 128, 128), 128)
    q2, k2, v2 = q[...], k[...], v[...]
    dmt = dm[:, cols].astype(F32).T
    kt = k2.astype(F32).T.astype(LOW)
    prod = dmt * mt_i[...].astype(F32)
    inv2 = [inv_i[h] for h in range(2)]
    dots = jnp.concatenate([dmt[64 * h : 64 * h + 64] * inv2[h] for h in range(2)], axis=0)
    dot_low = dots.astype(LOW)
    dout = dots.T.astype(LOW)
    dqt, dk2, dv2 = [], [], []
    for h in range(2):
        mine = (lane // 64) == h
        e = e_i[h]
        delta = jnp.sum(prod[64 * h : 64 * h + 64], axis=0, keepdims=True) * inv2[h]
        vz = jnp.where(mine, v2, jnp.zeros((), LOW))
        dp = nn(vz, dot_low)
        ds = (e.astype(F32) * (dp - delta)).astype(LOW)
        dv2.append(nn(e, dout))
        dk2.append(nn(ds, q2))
        dqt.append(nn(kt[64 * h : 64 * h + 64], ds))
    first = lane < 64
    dv[:, cols] = jnp.where(first, dv2[0], dv2[1]).astype(LOW)
    dk[:, cols] = jnp.where(first, dk2[0], dk2[1]).astype(LOW)
    dq[:, cols] = jnp.concatenate(dqt, axis=0).T.astype(LOW)


def embed_part(dq, dk, dv, wq, wk, wv, rows):
    return (
        nt(dq[rows, :], wq[...]) * HEAD_DIM ** (-0.5) + nt(dk[rows, :], wk[...]) + nt(dv[rows, :], wv[...])
    )


def attn_bwd_kernel(
    place, al, wo, q, k, v, e_i, inv_i, mt_i, wq_a, wk_a, wv_a, x_a, base_a, mixed_a,
    res0, res1, res2, res3, pool, vec1, vec2, ib, p0, p1, p2, p3, send, keep,
    dm, dq, dk, dv, wq, wk, wv, x, base, mixed, eg, sems
):
    pairs = ((wq_a, wq), (wk_a, wk), (wv_a, wv), (x_a, x), (base_a, base), (mixed_a, mixed))
    loads = [pltpu.make_async_copy(a, b, sems.at[i]) for i, (a, b) in enumerate(pairs)]

    @pl.when(pl.program_id(0) == 0)
    def _():
        for load in loads:
            load.start()

    attn_bwd_heads(al, wo, q, k, v, e_i, inv_i, mt_i, dm, dq, dk, dv)

    @pl.when(pl.program_id(0) == pl.num_programs(0) - 1)
    def _():
        for load in loads:
            load.wait()
        scale = HEAD_DIM ** (-0.5)
        s, d = base.shape
        n, share = s // 4, d // 4
        core = place[1]

        def put(owner, at, values):
            for c in range(2):

                @pl.when(core == c)
                def _():
                    out = keep if owner == c else send
                    for z in range(4):
                        out[z, at, :] = values(z)

        pieces = ((x, dq, scale), (x, dk, 1.0), (x, dv, 1.0), (mixed, al, 1.0))
        for i, (left, right, factor) in enumerate(pieces):
            weight = (tn(left[...], right[...]) * factor).astype(LOW)
            start = share * (i % 2)
            put(i // 2, slice(start, start + share), lambda z: weight[share * z : share * z + share])
        for m, part in enumerate((p0, p1, p2, p3)):
            at = slice(m * n, m * n + n)
            value = (base[at, :] + embed_part(dq, dk, dv, wq, wk, wv, at)).astype(LOW)
            eg[m] = value
            part[0:n, :] = value
            part[n : 2 * n, :] = (res0, res1, res2, res3)[m][...]
            part[2 * n : 2 * n + 16, :] = pool[...]
        put(0, slice(2 * share, 2 * share + n), lambda z: eg[(place[0] + 4 - z) % 4])
        vectors = [
            jnp.sum(dq[...].astype(F32), axis=0, keepdims=True) * scale,
            jnp.sum(dv[...].astype(F32), axis=0, keepdims=True),
            vec1[2:3, :],
            vec1[0:1, :],
            vec1[1:2, :],
            vec2[2:3, :],
            vec2[0:1, :],
            vec2[1:2, :],
        ]
        vectors += [ib[f] for f in range(4)] + [jnp.zeros((n - 12, d), F32)]
        vectors = jnp.concatenate(vectors, axis=0).astype(LOW)
        put(1, slice(2 * share, 2 * share + n), lambda z: vectors)


def attn_bwd(place, al, wo, q, k, v, e, inv, mt, wq, wk, wv, x, base, mixed, res, pool, vec1, vec2, ib):
    s, d = q.shape
    steps = d // 128
    heads = d // HEAD_DIM
    col = pl.BlockSpec((s, 128), lambda h, p: (0, h))
    small = [whole(part.shape) for part in res]
    small += [whole(pool.shape), whole(vec1.shape), whole(vec2.shape), whole(ib.shape)]
    ins = [
        whole((s, d)),
        whole((d, d)),
        col,
        col,
        col,
        pl.BlockSpec((2, s, s), lambda h, p: (h, 0, 0)),
        pl.BlockSpec((2, 1, s), lambda h, p: (h, 0, 0)),
        pl.BlockSpec((128, s), lambda h, p: (h, 0)),
    ]
    shapes = [((s // 2 + 16, d), LOW)] * 4 + [((4, d // 2 + s // 4, d), LOW)] * 2
    return pl.pallas_call(
        attn_bwd_kernel,
        grid_spec=prefetch(
            1,
            (steps,),
            ins + [pl.BlockSpec(memory_space=pl.ANY)] * 6 + small,
            [whole(shape) for shape, _ in shapes],
            [pltpu.VMEM((s, d), LOW)] * 4
            + [pltpu.VMEM((d, d), LOW)] * 3
            + [pltpu.VMEM((s, d), LOW), pltpu.VMEM((s, d), F32), pltpu.VMEM((s, d), LOW)]
            + [pltpu.VMEM((4, s // 4, d), LOW), pltpu.SemaphoreType.DMA((6,))],
        ),
        out_shape=[struct(*one) for one in shapes],
        compiler_params=params(),
        cost_estimate=cost(14 * s * d * d + 8 * s * s * 256 * heads, 28e6),
        name="attention_backward",
    )(place, al, wo, q, k, v, e, inv, mt, wq, wk, wv, x, base, mixed, *res, pool, vec1, vec2, ib)


def normalize(values):
    center = values - jnp.mean(values, axis=-1, keepdims=True)
    root = lax.rsqrt(jnp.mean(center * center, axis=-1, keepdims=True) + EPSILON)
    return center * root, root


def normalize_back(upstream, normed, root, gain):
    scaled = upstream * gain
    plain = jnp.mean(scaled, axis=-1, keepdims=True)
    crossed = jnp.mean(scaled * normed, axis=-1, keepdims=True)
    return root * (scaled - plain - normed * crossed)


def gelu_pair(v):
    cdf = lax.erf(v * 0.7071067811865476) * 0.5 + 0.5
    bell = jnp.exp(v * v * -0.5)
    return v * cdf, cdf + v * (bell * 0.3989422804014327)


def ff_kernel(
    row0, mixed, wo, bo, x, g1, s1, w1, b1, w2, b2, g2, s2, wp, bp, u0, u1, u2, u3,
    lhs_o, rhs_o, t0, t1, t2, t3, pool_o, al_o, fb_o, vec1_o, vec2_o, ib_o,
    w1s, w2s, wps, ups, gp, normed1, acc, sb, sems, *, chunk
):
    s, d = x.shape
    blocks = w1s.shape[0]
    ol_o, hid_o = lhs_o.at[0], lhs_o.at[1]
    act_o, il_o = rhs_o.at[0], rhs_o.at[1]
    n = s // 4
    per = chunk // n
    outs = (t0, t1, t2, t3)
    chunks = [slice(r, r + chunk) for r in range(0, s, chunk)]

    def load1(f):
        return pltpu.make_async_copy(w1.at[:, pl.ds(f * d, d)], w1s.at[f], sems.at[f])

    def load2(f):
        return pltpu.make_async_copy(w2.at[pl.ds(f * d, d), :], w2s.at[f], sems.at[blocks + f])

    loads = [pltpu.make_async_copy(wp, wps, sems.at[2 * blocks])]
    for m, part in enumerate((u0, u1, u2, u3)):
        loads.append(pltpu.make_async_copy(part, ups.at[m], sems.at[2 * blocks + 1 + m]))
    for f in range(blocks):
        load1(f).start()
        load2(f).start()
    for load in loads:
        load.start()

    roots1 = []
    for rows in chunks:
        val = nn(mixed[rows, :], wo[...]) + bo[...].astype(F32) + x[rows, :].astype(F32)
        normed, root = normalize(val)
        roots1.append(root)
        normed1[rows, :] = normed
        h = (normed * g1[...].astype(F32) + s1[...].astype(F32)).astype(LOW)
        hid_o[rows, :] = h
        acc[rows, :] = h.astype(F32) + b2[...].astype(F32)

    def forward(f, carry):
        load1(f).wait()
        load2(f).wait()
        for rows in chunks:
            pre = nn(hid_o[rows, :], w1s[f]) + b1[f].astype(F32)
            act, slope = gelu_pair(pre)
            act = act.astype(LOW)
            act_o[f, rows, :] = act
            gp[f, rows, :] = slope.astype(LOW)
            acc[rows, :] += nn(act, w2s[f])
        return carry

    lax.fori_loop(0, blocks, forward, 0)
    for load in loads:
        load.wait()

    gain = g2[...].astype(F32)
    roots2 = []
    for k, rows in enumerate(chunks):
        normed, root = normalize(acc[rows, :])
        roots2.append(root)
        res = (normed * gain + s2[...].astype(F32)).astype(LOW)
        al_o[rows, :] = res
        for j in range(per):
            outs[k * per + j][...] = res[j * n : j * n + n, :]
        acc[rows, :] = normed
    cls = al_o[pl.ds(pl.multiple_of(row0[0], 128), 16), :]
    pooled = jnp.tanh(nn(cls, wps[...]) + bp[...].astype(F32))
    pull = 0.0
    for m in range(4):
        terms = ups[m, n : n + 16, :].astype(F32)
        terms = jnp.broadcast_to(terms[0:1] + terms[1:2], (8, d))
        pull = pull + pltpu.roll(terms, ((row0[2] + 4 - m) % 4) * (d // 4), 1)
    pre = pull[:1] * (1.0 - pooled * pooled)
    cls_grad = nt(pre.astype(LOW), wps[...])[:1]
    high = pooled[:1].astype(LOW).astype(F32)
    pool = [cls[:1].astype(F32), pre[:1], high, pooled[:1] - high, jnp.zeros((12, d), F32)]
    pool_o[...] = jnp.concatenate(pool, axis=0).astype(LOW)
    gs, ss, bs = 0.0, 0.0, 0.0
    for k, rows in enumerate(chunks):
        ids = lax.broadcasted_iota(jnp.int32, (chunk, 1), 0) + rows.start
        up = jnp.concatenate([ups[k * per + j, 0:n, :] for j in range(per)], axis=0).astype(F32)
        upstream = up + jnp.where(ids == row0[0], cls_grad, 0.0)
        normed = acc[rows, :]
        back = normalize_back(upstream, normed, roots2[k], gain)
        sb[rows, :] = back
        low = back.astype(LOW)
        ol_o[rows, :] = low
        gs = gs + jnp.sum(upstream * normed, axis=0, keepdims=True)
        ss = ss + jnp.sum(upstream, axis=0, keepdims=True)
        bs = bs + jnp.sum(low.astype(F32), axis=0, keepdims=True)
    live = row0[1].astype(F32)
    vec2_o[0:1, :] = gs * live
    vec2_o[1:2, :] = ss * live
    vec2_o[2:3, :] = bs * live

    def backward(f, carry):
        bias = 0.0
        for rows in chunks:
            low = (nt(ol_o[rows, :], w2s[f]) * gp[f, rows, :].astype(F32)).astype(LOW)
            il_o[f, rows, :] = low
            bias = bias + jnp.sum(low.astype(F32), axis=0, keepdims=True)
            sb[rows, :] += nt(low, w1s[f])
        ib_o[f] = bias
        return carry

    lax.fori_loop(0, blocks, backward, 0)
    gain = g1[...].astype(F32)
    gs, ss, bs = 0.0, 0.0, 0.0
    for k, rows in enumerate(chunks):
        upstream = sb[rows, :]
        normed = normed1[rows, :]
        back = normalize_back(upstream, normed, roots1[k], gain)
        fb_o[rows, :] = back
        low = back.astype(LOW)
        al_o[rows, :] = low
        gs = gs + jnp.sum(upstream * normed, axis=0, keepdims=True)
        ss = ss + jnp.sum(upstream, axis=0, keepdims=True)
        bs = bs + jnp.sum(low.astype(F32), axis=0, keepdims=True)
    vec1_o[0:1, :] = gs
    vec1_o[1:2, :] = ss
    vec1_o[2:3, :] = bs


def feed_forward(row0, mixed, wo, bo, x, g1, s1, w1, b1, w2, b2, g2, s2, wp, bp, ups, chunk=256):
    s, d = x.shape
    ff = w1.shape[1]
    blocks = ff // d
    full, row = whole((s, d)), whole((1, d))
    away = pl.BlockSpec(memory_space=pl.ANY)
    part = (s // 4 + 16, d)
    return pl.pallas_call(
        functools.partial(ff_kernel, chunk=chunk),
        grid_spec=prefetch(
            1,
            (1,),
            [full, whole((d, d)), row, full, row, row, away, whole((blocks, 1, d)), away, row, row, row]
            + [away, row]
            + [away] * 4,
            [whole((2, s, d)), whole((2, blocks, s, d))]
            + [whole((s // 4, d))] * 4
            + [whole((16, d)), full, full, whole((8, d)), whole((8, d)), whole((blocks, 1, d))],
            [
                pltpu.VMEM((blocks, d, d), LOW),
                pltpu.VMEM((blocks, d, d), LOW),
                pltpu.VMEM((d, d), LOW),
                pltpu.VMEM((4,) + part, LOW),
                pltpu.VMEM((blocks, s, d), LOW),
                pltpu.VMEM((s, d), F32),
                pltpu.VMEM((s, d), F32),
                pltpu.VMEM((s, d), F32),
                pltpu.SemaphoreType.DMA((2 * blocks + 5,)),
            ],
        ),
        out_shape=[struct((2, s, d), LOW), struct((2, blocks, s, d), LOW)]
        + [struct((s // 4, d), LOW)] * 4
        + [
            struct((16, d), LOW),
            struct((s, d), LOW),
            struct((s, d), F32),
            struct((8, d), F32),
            struct((8, d), F32),
            struct((blocks, 1, d), F32),
        ],
        compiler_params=params(),
        cost_estimate=cost(2 * s * d * d + 8 * s * d * ff, 30e6),
        name="feed_forward",
    )(row0, mixed, wo, bo, x, g1, s1, w1, b1.reshape(blocks, 1, d), w2, b2, g2, s2, wp, bp, *ups)


def tn(a, b):
    return lax.dot_general(a, b, (((0,), (0,)), ((), ())), preferred_element_type=F32)


def prefetch(count, grid, in_specs, out_specs, scratch=()):
    return pltpu.PrefetchScalarGridSpec(
        num_scalar_prefetch=count,
        grid=grid,
        in_specs=in_specs,
        out_specs=out_specs,
        scratch_shapes=list(scratch),
    )


def index_kernel(ids, req_o, col_o, row_o, *, rows, slots):
    count, n = ids.shape
    owners = req_o.shape[0]
    owner = ((ids[...].astype(F32) + 0.5) * (1.0 / rows)).astype(jnp.int32)
    local = ids[...] - owner * rows + 1
    flat = [owner.astype(F32), (local // 64).astype(F32), (local % 64).astype(F32)]
    flat = jnp.concatenate(flat + [jnp.zeros((16 - 3 * count, n), F32)], axis=0)
    cols = flat.T
    lane = lax.broadcasted_iota(jnp.int32, (n, owners), 1).astype(F32)
    before = lax.broadcasted_iota(jnp.int32, (n, n), 1) < lax.broadcasted_iota(jnp.int32, (n, n), 0)
    before = jnp.where(before, 1.0, 0.0).astype(LOW)
    seen = jnp.zeros((1, owners), F32)
    high, low, places = 0.0, 0.0, []
    slot_lane = lax.broadcasted_iota(jnp.int32, (n, 128), 1).astype(F32)
    for s in range(count):
        hot = jnp.where(lane == cols[:, s : s + 1], 1.0, 0.0)
        hot_low = hot.astype(LOW)
        within = jnp.sum((nn(before, hot_low) + seen) * hot, axis=1, keepdims=True)
        seen = seen + jnp.sum(hot, axis=0, keepdims=True)
        place = cols[:, s : s + 1] * slots + within
        places.append(place)
        here = slot_lane == within
        put_high = jnp.where(here, cols[:, count + s : count + s + 1], 0.0).astype(LOW)
        put_low = jnp.where(here, cols[:, 2 * count + s : 2 * count + s + 1], 0.0).astype(LOW)
        high = high + tn(hot_low, put_high)
        low = low + tn(hot_low, put_low)
    req_o[...] = (high * 64.0 + low).astype(jnp.int32)[:, :slots] - 1
    places.append(jnp.full((n, 1), -1.0, F32))
    table = jnp.concatenate([jnp.broadcast_to(p, (n, 8)) for p in places], axis=1)
    table = jnp.concatenate([table, jnp.zeros((n, 128 - table.shape[1]), F32)], axis=1)
    turned = table.T.astype(jnp.int32)
    for s in range(count + 1):
        col_o[s] = places[s].astype(jnp.int32)
        row_o[s] = turned[8 * s : 8 * s + 1, :]


def index_requests(ids, rows, owners, slots):
    count, n = ids.shape
    return pl.pallas_call(
        functools.partial(index_kernel, rows=rows, slots=slots),
        grid=(1,),
        in_specs=[whole((count, n))],
        out_specs=[whole((owners, slots)), whole((count + 1, n, 1)), whole((count + 1, 1, n))],
        out_shape=[
            struct((owners, slots), jnp.int32),
            struct((count + 1, n, 1), jnp.int32),
            struct((count + 1, 1, n), jnp.int32),
        ],
        compiler_params=params(),
        cost_estimate=cost(0, 1e6),
        name="index_requests",
    )(ids)


def gather_kernel(fetch, table, out, acc, *, rows):
    step = pl.program_id(0)
    last = pl.num_programs(0) - 1
    blk = table.shape[0]
    ids = lax.broadcasted_iota(jnp.int32, (1, blk), 1) + step * blk
    hot = jnp.where(ids == fetch[...], 1.0, 0.0).astype(LOW)

    def add(block):
        part = nn(hot, block)

        @pl.when(step == 0)
        def _():
            acc[...] = part

        @pl.when(step > 0)
        def _():
            acc[...] += part

    @pl.when(step < last)
    def _():
        add(table[...])

    @pl.when(step == last)
    def _():
        ids_col = lax.broadcasted_iota(jnp.int32, (blk, 1), 0) + step * blk
        add(jnp.where(ids_col < rows, table[...], jnp.zeros((), LOW)))
        out[...] = acc[...].astype(LOW)


def gather_rows(fetch, table, blk=2048):
    slots = fetch.shape[0]
    rows, d = table.shape
    return pl.pallas_call(
        functools.partial(gather_kernel, rows=rows),
        grid=(pl.cdiv(rows, blk),),
        in_specs=[whole((slots, 1)), pl.BlockSpec((blk, d), lambda i: (i, 0))],
        out_specs=whole((slots, d)),
        out_shape=struct((slots, d), LOW),
        scratch_shapes=[pltpu.VMEM((slots, d), F32)],
        compiler_params=params(),
        cost_estimate=cost(2 * slots * rows * d, 8e6),
        name="gather_rows",
    )(fetch, table)


def embed_kernel(place, slot, replies, pos, o0, o1, o2, o3):
    ids = lax.broadcasted_iota(jnp.int32, (1, replies.shape[0]), 1)
    for m, out in enumerate((o0, o1, o2, o3)):
        sent = (place[0] + m) % 4
        hot = jnp.where(ids == slot[sent], 1.0, 0.0).astype(LOW)
        live = jnp.where(sent < 3, 1.0, 0.0)
        out[...] = ((nn(hot, replies[...]) + pos[...].astype(F32)) * live).astype(LOW)


def embed_parts(place, slot, replies, pos):
    slots, d = replies.shape
    n = pos.shape[0]
    return pl.pallas_call(
        embed_kernel,
        grid_spec=prefetch(
            1,
            (1,),
            [whole((4, n, 1)), whole((slots, d)), whole((n, d))],
            [whole((n, d))] * 4,
        ),
        out_shape=[struct((n, d), LOW)] * 4,
        compiler_params=params(),
        cost_estimate=cost(2 * slots * 4 * n * d, 3e6),
        name="embed_parts",
    )(place, slot, replies, pos)


def cotangent_kernel(place, grads, terms, o0, o1, o2, o3):
    n = grads.shape[1]
    for m, out in enumerate((o0, o1, o2, o3)):
        sent = (place[0] + m) % 4
        here = jnp.minimum(sent, 2)
        live = jnp.where(sent < 3, 1.0, 0.0)
        out[0:n, :] = (grads[here].astype(F32) * live).astype(LOW)
        out[n : n + 16, :] = (terms[here].astype(F32) * live).astype(LOW)


def cotangent_parts(place, grads, terms):
    _, n, d = grads.shape
    return pl.pallas_call(
        cotangent_kernel,
        grid_spec=prefetch(
            1, (1,), [whole(grads.shape), whole(terms.shape)], [whole((n + 16, d))] * 4
        ),
        out_shape=[struct((n + 16, d), LOW)] * 4,
        compiler_params=params(),
        cost_estimate=cost(0, 2e6),
        name="cotangent_parts",
    )(place, grads, terms)


def outgoing_kernel(place, slot, p0, p1, p2, p3, out):
    ids = lax.broadcasted_iota(jnp.int32, (out.shape[0], 1), 0)
    total = 0.0
    for m, part in enumerate((p0, p1, p2, p3)):
        sent = (place[0] + m) % 4
        hot = jnp.where(ids == slot[sent], 1.0, 0.0).astype(LOW)
        total = total + nn(hot, part[...])
    out[...] = total.astype(LOW)


def outgoing_rows(place, slot, parts, slots):
    n = slot.shape[2]
    d = parts[0].shape[1]
    return pl.pallas_call(
        outgoing_kernel,
        grid_spec=prefetch(
            1,
            (1,),
            [whole((4, 1, n))] + [pl.BlockSpec((n, d), lambda i, p: (0, 0))] * 4,
            whole((slots, d)),
        ),
        out_shape=struct((slots, d), LOW),
        compiler_params=params(),
        cost_estimate=cost(2 * slots * 4 * n * d, 3e6),
        name="outgoing_rows",
    )(place, slot, *parts)


def table_kernel(fetch, incoming, out):
    blk = out.shape[0]
    ids = lax.broadcasted_iota(jnp.int32, (blk, 1), 0) + pl.program_id(0) * blk
    out[...] = nn(jnp.where(ids == fetch[...], 1.0, 0.0).astype(LOW), incoming[...])


def table_grad(fetch, incoming, rows, blk=1024):
    slots, d = incoming.shape
    return pl.pallas_call(
        table_kernel,
        grid=(pl.cdiv(rows, blk),),
        in_specs=[whole((1, slots)), whole((slots, d))],
        out_specs=pl.BlockSpec((blk, d), lambda i: (i, 0)),
        out_shape=struct((rows, d), F32),
        compiler_params=params(),
        cost_estimate=cost(2 * slots * rows * d, 13e6),
        name="table_gradient",
    )(fetch, incoming)


def unpermute_kernel(place, p0, p1, p2, p3, out):
    for m, part in enumerate((p0, p1, p2, p3)):
        sent = (place[0] + m) % 4

        @pl.when(sent < 3)
        def _():
            out[sent] = part[...]


def unpermute(place, parts, n):
    d = parts[0].shape[1]
    return pl.pallas_call(
        unpermute_kernel,
        grid_spec=prefetch(
            1, (1,), [pl.BlockSpec((n, d), lambda i, p: (1, 0))] * 4, whole((3, n, d))
        ),
        out_shape=struct((3, n, d), parts[0].dtype),
        compiler_params=params(),
        cost_estimate=cost(0, 2e6),
        name="unpermute",
    )(place, *parts)


def ff_send_kernel(which, left, right, out):
    out[0] = tn(left[0], right[0, 0]).astype(LOW)


def ff_specs(s, d):
    return [
        pl.BlockSpec((1, s, d), lambda f, w: (w[0], 0, 0)),
        pl.BlockSpec((1, 1, s, d), lambda f, w: (w[0], f, 0, 0)),
    ]


def ff_send(which, left, right):
    _, blocks, s, d = right.shape
    return pl.pallas_call(
        ff_send_kernel,
        grid_spec=prefetch(
            1, (blocks,), ff_specs(s, d), pl.BlockSpec((1, d, d), lambda f, w: (f, 0, 0))
        ),
        out_shape=struct((blocks, d, d), LOW),
        compiler_params=params(),
        cost_estimate=cost(2 * blocks * s * d * d, 9e6),
        name="ff_send",
    )(which, left, right)


def ff_keep_kernel(place, left, right, got, o0, o1, o2, o3, acc):
    f = pl.program_id(0)
    total = tn(left[0], right[0, 0]) + got[0].astype(F32)
    acc[f] = total.astype(LOW).reshape(acc.shape[1:])

    @pl.when(f == pl.num_programs(0) - 1)
    def _():
        for m, out in enumerate((o0, o1, o2, o3)):
            index = (place[1] + m) % 4

            @pl.when(place[0] == 0)
            def _():
                for z in range(4):
                    out[z] = acc[z, index]

            @pl.when(place[0] == 1)
            def _():
                out[...] = acc[index]


def ff_keep(place, left, right, got):
    _, blocks, s, d = right.shape
    shape = (4, d // 4, d)
    return pl.pallas_call(
        ff_keep_kernel,
        grid_spec=prefetch(
            1,
            (blocks,),
            ff_specs(s, d) + [pl.BlockSpec((1, d, d), lambda f, w: (f, 0, 0))],
            [whole(shape)] * 4,
            [pltpu.VMEM((blocks,) + shape, LOW)],
        ),
        out_shape=[struct(shape, LOW)] * 4,
        compiler_params=params(),
        cost_estimate=cost(2 * blocks * s * d * d, 14e6),
        name="ff_keep",
    )(place, left, right, got)


def core_add_kernel(place, own, got, o0, o1, o2, o3):
    rows = o0.shape[1]
    for m, out in enumerate((o0, o1, o2, o3)):
        at = pl.ds(pl.multiple_of((place[0] + m) % 4 * rows, rows), rows)
        out[...] = (own[:, at, :].astype(F32) + got[:, at, :].astype(F32)).astype(LOW)


def core_add(place, own, got):
    out = (4, own.shape[1] // 4, own.shape[2])
    return pl.pallas_call(
        core_add_kernel,
        grid_spec=prefetch(1, (1,), [whole(own.shape)] * 2, [whole(out)] * 4),
        out_shape=[struct(out, LOW)] * 4,
        compiler_params=params(),
        cost_estimate=cost(0, 9e6),
        name="core_add",
    )(place, own, got)


def add4(a, b, c, d):
    return a[...].astype(F32) + b[...].astype(F32) + c[...].astype(F32) + d[...].astype(F32)


def ring_add_kernel(place, p0, p1, p2, p3, o0, o1, o2, o3, acc):
    acc[...] = add4(p0, p1, p2, p3)
    rows = o0.shape[1]
    for m, out in enumerate((o0, o1, o2, o3)):
        at = pl.ds(pl.multiple_of((place[0] + m) % 4 * rows, rows), rows)
        out[...] = acc[:, at, :].astype(LOW)


def ring_add(place, parts):
    shape = parts[0].shape
    out = (4, shape[1] // 4, shape[2])
    return pl.pallas_call(
        ring_add_kernel,
        grid_spec=prefetch(
            1, (1,), [whole(shape)] * 4, [whole(out)] * 4, [pltpu.VMEM(shape, F32)]
        ),
        out_shape=[struct(out, LOW)] * 4,
        compiler_params=params(),
        cost_estimate=cost(0, 6e6),
        name="ring_add",
    )(place, *parts)


def join_kernel(place, a0, a1, a2, a3, b0, b1, b2, b3, o0, o1, o2, o3, acc):
    acc[:, 0:48, :] = add4(a0, a1, a2, a3)
    acc[:, 48:80, :] = add4(b0, b1, b2, b3)
    for m, out in enumerate((o0, o1, o2, o3)):
        out[...] = acc[(place[0] + m) % 4].astype(LOW)


def join(place, first, second):
    d = first[0].shape[2]
    return pl.pallas_call(
        join_kernel,
        grid_spec=prefetch(
            1,
            (1,),
            [whole(first[0].shape)] * 4 + [whole(second[0].shape)] * 4,
            [whole((80, d))] * 4,
            [pltpu.VMEM((4, 80, d), F32)],
        ),
        out_shape=[struct((80, d), LOW)] * 4,
        compiler_params=params(),
        cost_estimate=cost(0, 4e6),
        name="join",
    )(place, *first, *second)


def piece_kernel(f0, f1, f2, f3, r0, r1, r2, r3, out):
    pool = [part[...].astype(F32)[0:2] for part in (r0, r1, r2, r3)]
    pool.append(jnp.zeros((8, out.shape[1]), F32))
    out[...] = jnp.concatenate([add4(f0, f1, f2, f3)] + pool, axis=0).astype(LOW)


def piece_rows(parts, pool):
    d = parts[0].shape[1]
    return pl.pallas_call(
        piece_kernel,
        grid=(1,),
        in_specs=[whole(p.shape) for p in parts]
        + [pl.BlockSpec((16, d), lambda i: (16, 0)) for p in pool],
        out_specs=whole((96, d)),
        out_shape=struct((96, d), LOW),
        compiler_params=params(),
        cost_estimate=cost(0, 1e6),
        name="piece_rows",
    )(*parts, *pool)


def order_kernel(place, p0, p1, p2, p3, out):
    for m, part in enumerate((p0, p1, p2, p3)):
        out[(place[0] + 4 - m) % 4] = part[...]


def order(place, parts):
    shape = parts[0].shape
    return pl.pallas_call(
        order_kernel,
        grid_spec=prefetch(1, (1,), [whole(shape)] * 4, whole((4,) + shape)),
        out_shape=struct((4,) + shape, LOW),
        compiler_params=params(),
        cost_estimate=cost(0, 3e6),
        name="order",
    )(place, *parts)


def finish_kernel(
    place, own, got, outer_o, inner_o, q_o, k_o, v_o, out_o, pos_o, vec_o, ib_o, pw_o, pb_o, acc, vec
):
    d = outer_o.shape[0]
    share = d // 4

    def mine(rows):
        return pltpu.roll(rows, d - share * place[1], 1)[:, 0:share]

    def fill(zero, one):
        pool = []
        for i in range(4):
            for k in range(4):
                at = 96 * k
                r = 192 * i + 48 * k
                acc[r : r + 48, :] = zero[i, at : at + 48, :].astype(F32)
                cols = slice(d * i, d * i + d)
                inner_o[48 * k : 48 * k + 48, cols] = one[i, at : at + 48, :].astype(F32)
                r = 128 * i + 32 * k
                first = zero[i, at + 48 : at + 80, :].astype(F32)
                second = one[i, at + 48 : at + 80, :].astype(F32)
                if r < 192:
                    q_o[r : r + 32, :] = first
                    v_o[r : r + 32, :] = second
                elif r < 384:
                    k_o[r - 192 : r - 160, :] = first
                    out_o[r - 192 : r - 160, :] = second
                else:
                    pos_o[r - 384 : r - 352, :] = first
                    if r == 384:
                        vec[...] = second[0:16]
                pool.append(zero[i, at + 80 : at + 96, :].astype(F32)[0:8])
                pool.append(one[i, at + 80 : at + 96, :].astype(F32)[0:8])
        outer_o[...] = acc[...].T
        pool = jnp.concatenate(pool, axis=0)
        even = lax.broadcasted_iota(jnp.int32, (pool.shape[0], 1), 0) % 2 == 0
        below = jnp.concatenate([pool[1:], pool[:1]], axis=0)
        acc[...] = tn(jnp.where(even, pool, 0.0).astype(LOW), below.astype(LOW))
        bias = jnp.sum(jnp.where(even, 0.0, pool), axis=0, keepdims=True)
        pb_o[...] = mine(jnp.broadcast_to(bias, (8, d)))[0:1]

    @pl.when(place[0] == 0)
    def _():
        fill(own, got)

    @pl.when(place[0] == 1)
    def _():
        fill(got, own)

    pw_o[...] = acc[pl.ds(pl.multiple_of(place[1] * share, share), share), :]
    vec_o[...] = mine(vec[0:8, :])
    ib_o[...] = vec[pl.ds(8 + place[1], 1), :]


def finish(place, own, got):
    d = own.shape[2]
    share = d // 4
    shapes = [(d, d), (share, 4 * d)] + [(share, d)] * 4 + [(128, d), (8, share), (1, d)]
    shapes += [(share, d), (1, share)]
    return pl.pallas_call(
        finish_kernel,
        grid_spec=prefetch(
            1,
            (1,),
            [whole(own.shape)] * 2,
            [whole(s) for s in shapes],
            [pltpu.VMEM((d, d), F32), pltpu.VMEM((16, d), F32)],
        ),
        out_shape=[struct(s, F32) for s in shapes],
        compiler_params=params(),
        cost_estimate=cost(0, 14e6),
        name="finish",
    )(place, own, got)


def pooled_kernel(place, p0, p1, p2, p3, out):
    for m, part in enumerate((p0, p1, p2, p3)):
        two = part[...].astype(F32)
        row = two[2:3] + two[3:4]
        out[(place[0] + m) % 4] = pltpu.roll(
            jnp.broadcast_to(row, (8, row.shape[1])), row.shape[1] - 192 * place[0], 1
        )


def pooled_rows(place, parts):
    d = parts[0].shape[1]
    below = pl.BlockSpec((16, d), lambda i, p: (16, 0))
    return pl.pallas_call(
        pooled_kernel,
        grid_spec=prefetch(1, (1,), [below] * 4, whole((4, 8, d))),
        out_shape=struct((4, 8, d), F32),
        compiler_params=params(),
        name="pooled_rows",
    )(place, *parts)


def shift_pairs(step, axes):
    pairs = []
    for y in range(4):
        for x in range(4):
            for c in range(2):
                to = (y, (x + step) % 4) if axes[c] == "x" else ((y + step) % 4, x)
                pairs.append(((y * 4 + x) * 2 + c, (to[0] * 4 + to[1]) * 2 + c))
    return pairs


def shift_first(array, step):
    return lax.ppermute(array, "batch", shift_pairs(step, "xy"))


def shift_second(array, step):
    return lax.ppermute(array, "batch", shift_pairs(step, "yx"))


def shift_z(array, step):
    return lax.ppermute(array, "seq", [(z, (z + step) % 4) for z in range(4)])


def swap_core(array):
    return lax.ppermute(array, "batch", [(i, i ^ 1) for i in range(32)])


def ring_send(parts, shift):
    return [parts[0], shift(parts[1], 1), shift(parts[2], 2), shift(parts[3], 3)]


def to_sentence(parts):
    out = [parts[0]]
    for step in (1, 2, 3):
        pairs = [(z, (z + step) % 4) for z in range(4) if (z + step) % 4 < 3]
        out.append(lax.ppermute(parts[step], "seq", pairs))
    return out


def from_sentence(parts):
    out = [parts[0]]
    for step in (1, 2, 3):
        pairs = [((z + step) % 4, z) for z in range(4) if (z + step) % 4 < 3]
        out.append(lax.ppermute(parts[step], "seq", pairs))
    return out


def tie(array, *after):
    return lax.optimization_barrier((array,) + after)[0]


def per_device(
    token_ids,
    lengths,
    word_table,
    positions,
    query_weight,
    key_weight,
    value_weight,
    query_bias,
    value_bias,
    output_weight,
    output_bias,
    first_gain,
    first_shift,
    inner_weight,
    inner_bias,
    outer_weight,
    outer_bias,
    second_gain,
    second_shift,
    pooler_weight,
    pooler_bias,
    out_grad,
    pooled_grad,
):
    num_sent, local_len = token_ids.shape
    table_rows, width = word_table.shape
    all_count = lax.axis_size("seq") * lax.axis_size("batch")
    z = lax.axis_index("seq")
    batch_place = lax.axis_index("batch")
    core = batch_place % 2
    x = (batch_place // 2) % 4
    y = batch_place // 8

    first = jnp.where(core == 0, x, y)
    second = jnp.where(core == 0, y, x)

    def scalars(*values):
        return jnp.stack([jnp.asarray(v, jnp.int32) for v in values])

    slots = 2 * num_sent * local_len // all_count
    all_slots = slots * all_count
    requests, slot_cols, slot_rows = index_requests(token_ids, table_rows, all_count, slots)
    arrived = lax.all_to_all(requests, ("batch", "seq"), split_axis=0, concat_axis=0, tiled=True)
    fetch = arrived.reshape(-1)
    found = gather_rows(fetch[:, None], word_table)
    replies = lax.all_to_all(
        found.reshape(all_count, slots, width),
        ("batch", "seq"),
        split_axis=0,
        concat_axis=0,
        tiled=True,
    ).reshape(all_slots, width)
    live = (z < 3).astype(jnp.int32)
    sentence = jnp.minimum(z, 2)

    def row(vector):
        return vector.reshape(1, -1)

    vectors = (
        query_bias,
        value_bias,
        output_bias,
        first_gain,
        first_shift,
        inner_bias,
        outer_bias,
        second_gain,
        second_shift,
        pooler_bias,
    )
    block_of = (z - jnp.arange(4, dtype=jnp.int32)) % 4
    place_of = block_of[:, None] * local_len + jnp.arange(local_len, dtype=jnp.int32)[None, :]
    live_keys = (place_of.reshape(-1, 1) < lengths[sentence]).astype(F32)

    high = pooled_grad.astype(LOW)
    terms = jnp.stack([high, (pooled_grad - high.astype(F32)).astype(LOW)], axis=1)
    terms = jnp.pad(terms, ((0, 0), (0, 14), (0, width - terms.shape[2])))
    early = [live_keys] + [row(v) for v in vectors]
    terms, *early = lax.optimization_barrier([terms] + early)
    live_keys, q_bias, v_bias, o_bias, gain1, shift1, in_bias, out_bias, gain2, shift2, pool_bias = early
    ups = to_sentence(cotangent_parts(scalars(z), out_grad, terms))
    parts = embed_parts(scalars(z), slot_cols, replies, positions)
    parts, ups = lax.optimization_barrier((parts, ups))
    embeds = to_sentence(parts)

    embed, query, key, value, expo, inverse, mixed_t, mixed = attn_fwd(
        embeds, query_weight, key_weight, value_weight, q_bias, v_bias, live_keys
    )
    (
        left,
        right,
        *result,
        pool,
        attention_low,
        first_back,
        vec1,
        vec2,
        inner_bias_grad,
    ) = feed_forward(
        scalars(sentence * local_len, live, z),
        mixed,
        output_weight,
        o_bias,
        embed,
        gain1,
        shift1,
        inner_weight,
        in_bias,
        outer_weight,
        out_bias,
        gain2,
        shift2,
        pooler_weight,
        pool_bias,
        ups,
    )

    ff_other = ff_send(scalars(1 - core), left, right)
    ff_parts = ff_keep(scalars(core, first), left, right, swap_core(ff_other))
    attention_low = tie(attention_low, ff_parts[0])
    ff_parts = ring_send(ff_parts, shift_first)
    *embed_grad, rest_other, rest_own = attn_bwd(
        scalars(z, core),
        attention_low,
        output_weight,
        query,
        key,
        value,
        expo,
        inverse,
        mixed_t,
        query_weight,
        key_weight,
        value_weight,
        embed,
        first_back,
        mixed,
        result,
        pool,
        vec1,
        vec2,
        inner_bias_grad,
    )
    embed_grad, rest_other, rest_own, ff_parts = lax.optimization_barrier(
        (embed_grad, rest_other, rest_own, ff_parts)
    )

    returned = from_sentence(embed_grad)
    ff_parts = list(ring_add(scalars(second), ff_parts))
    rest_own = tie(rest_own, ff_parts[0])
    rest_parts = core_add(scalars(first), rest_own, swap_core(rest_other))
    ff_parts[0] = tie(ff_parts[0], rest_parts[0])
    rest_parts = ring_send(rest_parts, shift_first)
    ff_parts = ring_send(ff_parts, shift_second)
    rest_parts = ring_add(scalars(second), rest_parts)
    returned[0] = tie(returned[0], rest_parts[0])
    outgoing = outgoing_rows(scalars(z), slot_rows, returned, all_slots)
    outgoing = outgoing.reshape(all_count, slots, width)
    rest_parts = ring_send(rest_parts, shift_second)
    rest_parts[0] = tie(rest_parts[0], outgoing)
    parts = ring_send(join(scalars(z), ff_parts, rest_parts), shift_z)
    piece = piece_rows(parts, returned)
    pieces = [piece] + [shift_second(piece, m) for m in (1, 2, 3)]
    block = order(scalars(second), pieces).reshape(-1, width)
    blocks = [block] + [shift_first(block, m) for m in (1, 2, 3)]
    incoming = lax.all_to_all(
        tie(outgoing, block), ("batch", "seq"), split_axis=0, concat_axis=0, tiled=True
    ).reshape(all_slots, width)
    returned[0] = tie(returned[0], block)
    pooled = pooled_rows(scalars(z), returned)[:num_sent, 0, : width // 4]
    hidden_out = unpermute(scalars(z), returned, local_len)
    incoming = tie(incoming, pooled, hidden_out)
    grad_table = table_grad(fetch[None, :], incoming, table_rows)
    blocks[0] = tie(blocks[0], grad_table)
    whole_own = order(scalars(first), blocks)
    whole_other = swap_core(whole_own)
    (
        grad_outer,
        grad_inner,
        grad_query,
        grad_key,
        grad_value,
        grad_output,
        grad_positions,
        mine,
        inner_bias_sum,
        grad_pooler,
        pooler_bias_sum,
    ) = finish(scalars(core, z), whole_own, whole_other)

    return (
        hidden_out,
        pooled,
        grad_table,
        grad_positions,
        grad_query,
        grad_key,
        grad_value,
        mine[0],
        mine[1],
        grad_output,
        mine[2],
        mine[3],
        mine[4],
        grad_inner,
        inner_bias_sum[0],
        grad_outer,
        mine[5],
        mine[6],
        mine[7],
        grad_pooler,
        pooler_bias_sum[0],
    )


def solution(mesh):
    in_specs = (
        P("batch", "seq"),
        P("batch"),
        P(("batch", "seq"), None),
        P("seq", None),
        P(),
        P(),
        P(),
        P(),
        P(),
        P(),
        P(),
        P(),
        P(),
        P(),
        P(),
        P(),
        P(),
        P(),
        P(),
        P(),
        P(),
        P("batch", "seq", None),
        P("batch", "seq"),
    )
    out_specs = (
        P("batch", "seq", None),
        P("batch", "seq"),
        P(("batch", "seq"), None),
        P("seq", None),
        P("seq", None),
        P("seq", None),
        P("seq", None),
        P("seq"),
        P("seq"),
        P("seq", None),
        P("seq"),
        P("seq"),
        P("seq"),
        P("seq", None),
        P("seq"),
        P("seq", None),
        P("seq"),
        P("seq"),
        P("seq"),
        P("seq", None),
        P("seq"),
    )
    return jax.shard_map(
        per_device, mesh=mesh, in_specs=in_specs, out_specs=out_specs, check_vma=False
    )
```

```python
import functools
import jax
import jax.numpy as jnp
from jax import lax
from jax.experimental import pallas as pl
from jax.experimental.pallas import tpu as pltpu
from jax.sharding import PartitionSpec as P

F32 = jnp.float32
LOW = jnp.bfloat16
EPSILON = 1e-12
MASKED = -1000000000.0
HEAD_DIM = 64
VMEM = 63 * 1024 * 1024
HALF = 384
SHARE = 0.02


def nn(a, b):
    return lax.dot_general(a, b, (((1,), (0,)), ((), ())), preferred_element_type=F32)


def nt(a, b):
    return lax.dot_general(a, b, (((1,), (1,)), ((), ())), preferred_element_type=F32)


def struct(shape, dtype):
    return jax.ShapeDtypeStruct(shape, dtype)


def whole(shape):
    zeros = (0,) * len(shape)
    return pl.BlockSpec(shape, lambda *_: zeros, pipeline_mode=pl.Buffered(1))


def cost(flops, size):
    return pl.CostEstimate(
        flops=int(flops * SHARE), bytes_accessed=int(size * SHARE), transcendentals=0
    )


def params(**kw):
    return pltpu.CompilerParams(vmem_limit_bytes=VMEM, **kw)


def attn_fwd_kernel(
    x0, x1, x2, x3, wq, wk, wv, bq, bv, live, x_o, q_o, k_o, v_o, e_o, inv_o, mt_o, mixed_o, x
):
    scale = HEAD_DIM ** (-0.5)
    n = x0.shape[0]

    @pl.when(pl.program_id(0) == 0)
    def _():
        for m, part in enumerate((x0, x1, x2, x3)):
            x[m * n : m * n + n, :] = part[...]
            x_o[m * n : m * n + n, :] = part[...]

    q = ((nn(x[...], wq[...]) + bq[...].astype(F32)) * scale).astype(LOW)
    q_o[...] = q
    k = nn(x[...], wk[...]).astype(LOW)
    k_o[...] = k
    v = nn(x[...], wv[...]) + bv[...].astype(F32)
    v_o[...] = v.astype(LOW)
    keep = live[...] > 0.0
    lane = lax.broadcasted_iota(jnp.int32, (1, 128), 1)
    for pair in range(q.shape[1] // 128):
        cols = slice(128 * pair, 128 * pair + 128)
        q2, k2 = q[:, cols], k[:, cols]
        vt = v[:, cols].T.astype(LOW)
        parts = []
        for h in range(2):
            kz = jnp.where((lane // 64) == h, k2, jnp.zeros((), LOW))
            s = nt(kz, q2)
            s = jnp.where(keep, s, MASKED)
            e = jnp.exp(s - jnp.max(s, axis=0, keepdims=True))
            inv = 1.0 / jnp.sum(e, axis=0, keepdims=True)
            eb = e.astype(LOW)
            e_o[2 * pair + h] = eb
            inv_o[2 * pair + h] = inv
            parts.append(nn(vt[64 * h : 64 * h + 64], eb) * inv)
        mt = jnp.concatenate(parts, axis=0)
        mt_o[cols, :] = mt.astype(LOW)
        mixed_o[:, cols] = mt.T.astype(LOW)


def attn_fwd(parts, wq, wk, wv, bq, bv, live, group=256):
    s, d = live.shape[0], wq.shape[0]
    n = s // 4
    hg = group // HEAD_DIM
    col = pl.BlockSpec((s, group), lambda h: (0, h))
    wcol = pl.BlockSpec((d, group), lambda h: (0, h))
    brow = pl.BlockSpec((1, group), lambda h: (0, h))
    heads = d // HEAD_DIM
    return pl.pallas_call(
        attn_fwd_kernel,
        grid=(d // group,),
        in_specs=[pl.BlockSpec((n, d), lambda h: (0, 0))] * 4 + [wcol, wcol, wcol, brow, brow, whole((s, 1))],
        out_specs=[
            whole((s, d)),
            col,
            col,
            col,
            pl.BlockSpec((hg, s, s), lambda h: (h, 0, 0)),
            pl.BlockSpec((hg, 1, s), lambda h: (h, 0, 0)),
            pl.BlockSpec((group, s), lambda h: (h, 0)),
            col,
        ],
        out_shape=[
            struct((s, d), LOW),
            struct((s, d), LOW),
            struct((s, d), LOW),
            struct((s, d), LOW),
            struct((heads, s, s), LOW),
            struct((heads, 1, s), F32),
            struct((d, s), LOW),
            struct((s, d), LOW),
        ],
        scratch_shapes=[pltpu.VMEM((s, d), LOW)],
        compiler_params=params(),
        cost_estimate=cost(6 * s * d * d + 4 * s * s * 256 * heads, 16e6),
        name="attention_forward",
    )(*parts, wq, wk, wv, bq, bv, live)


def attn_bwd_heads(al, wo, q, k, v, e_i, inv_i, mt_i, dm, dq, dk, dv):
    step = pl.program_id(0)

    @pl.when(step == 0)
    def _():
        dm[...] = nt(al[...], wo[...]).astype(LOW)

    lane = lax.broadcasted_iota(jnp.int32, (1, 128), 1)
    cols = pl.ds(pl.multiple_of(step * 128, 128), 128)
    q2, k2, v2 = q[...], k[...], v[...]
    dmt = dm[:, cols].astype(F32).T
    kt = k2.astype(F32).T.astype(LOW)
    prod = dmt * mt_i[...].astype(F32)
    inv2 = [inv_i[h] for h in range(2)]
    dots = jnp.concatenate([dmt[64 * h : 64 * h + 64] * inv2[h] for h in range(2)], axis=0)
    dot_low = dots.astype(LOW)
    dout = dots.T.astype(LOW)
    dqt, dk2, dv2 = [], [], []
    for h in range(2):
        mine = (lane // 64) == h
        e = e_i[h]
        delta = jnp.sum(prod[64 * h : 64 * h + 64], axis=0, keepdims=True) * inv2[h]
        vz = jnp.where(mine, v2, jnp.zeros((), LOW))
        dp = nn(vz, dot_low)
        ds = (e.astype(F32) * (dp - delta)).astype(LOW)
        dv2.append(nn(e, dout))
        dk2.append(nn(ds, q2))
        dqt.append(nn(kt[64 * h : 64 * h + 64], ds))
    first = lane < 64
    dv[:, cols] = jnp.where(first, dv2[0], dv2[1]).astype(LOW)
    dk[:, cols] = jnp.where(first, dk2[0], dk2[1]).astype(LOW)
    dq[:, cols] = jnp.concatenate(dqt, axis=0).T.astype(LOW)


def embed_part(dq, dk, dv, wq, wk, wv, rows):
    return (
        nt(dq[rows, :], wq[...]) * HEAD_DIM ** (-0.5) + nt(dk[rows, :], wk[...]) + nt(dv[rows, :], wv[...])
    )


def attn_bwd_kernel(
    place, al, wo, q, k, v, e_i, inv_i, mt_i, wq_a, wk_a, wv_a, x_a, base_a, mixed_a,
    res0, res1, res2, res3, pool, vec1, vec2, ib, p0, p1, p2, p3, send, keep,
    dm, dq, dk, dv, wq, wk, wv, x, base, mixed, eg, sems
):
    pairs = ((wq_a, wq), (wk_a, wk), (wv_a, wv), (x_a, x), (base_a, base), (mixed_a, mixed))
    loads = [pltpu.make_async_copy(a, b, sems.at[i]) for i, (a, b) in enumerate(pairs)]

    @pl.when(pl.program_id(0) == 0)
    def _():
        for load in loads:
            load.start()

    attn_bwd_heads(al, wo, q, k, v, e_i, inv_i, mt_i, dm, dq, dk, dv)

    @pl.when(pl.program_id(0) == pl.num_programs(0) - 1)
    def _():
        for load in loads:
            load.wait()
        scale = HEAD_DIM ** (-0.5)
        s, d = base.shape
        n, share = s // 4, d // 4
        core = place[1]

        def put(owner, at, values):
            for c in range(2):

                @pl.when(core == c)
                def _():
                    out = keep if owner == c else send
                    for z in range(4):
                        out[z, at, :] = values(z)

        pieces = ((x, dq, scale), (x, dk, 1.0), (x, dv, 1.0), (mixed, al, 1.0))
        for i, (left, right, factor) in enumerate(pieces):
            weight = (tn(left[...], right[...]) * factor).astype(LOW)
            start = share * (i % 2)
            put(i // 2, slice(start, start + share), lambda z: weight[share * z : share * z + share])
        for m, part in enumerate((p0, p1, p2, p3)):
            at = slice(m * n, m * n + n)
            value = (base[at, :] + embed_part(dq, dk, dv, wq, wk, wv, at)).astype(LOW)
            eg[m] = value
            part[0:n, :] = value
            part[n : 2 * n, :] = (res0, res1, res2, res3)[m][...]
            part[2 * n : 2 * n + 16, :] = pool[...]
        put(0, slice(2 * share, 2 * share + n), lambda z: eg[(place[0] + 4 - z) % 4])
        vectors = [
            jnp.sum(dq[...].astype(F32), axis=0, keepdims=True) * scale,
            jnp.sum(dv[...].astype(F32), axis=0, keepdims=True),
            vec1[2:3, :],
            vec1[0:1, :],
            vec1[1:2, :],
            vec2[2:3, :],
            vec2[0:1, :],
            vec2[1:2, :],
        ]
        vectors += [ib[f] for f in range(4)] + [jnp.zeros((n - 12, d), F32)]
        vectors = jnp.concatenate(vectors, axis=0).astype(LOW)
        put(1, slice(2 * share, 2 * share + n), lambda z: vectors)


def attn_bwd(place, al, wo, q, k, v, e, inv, mt, wq, wk, wv, x, base, mixed, res, pool, vec1, vec2, ib):
    s, d = q.shape
    steps = d // 128
    heads = d // HEAD_DIM
    col = pl.BlockSpec((s, 128), lambda h, p: (0, h))
    small = [whole(part.shape) for part in res]
    small += [whole(pool.shape), whole(vec1.shape), whole(vec2.shape), whole(ib.shape)]
    ins = [
        whole((s, d)),
        whole((d, d)),
        col,
        col,
        col,
        pl.BlockSpec((2, s, s), lambda h, p: (h, 0, 0)),
        pl.BlockSpec((2, 1, s), lambda h, p: (h, 0, 0)),
        pl.BlockSpec((128, s), lambda h, p: (h, 0)),
    ]
    shapes = [((s // 2 + 16, d), LOW)] * 4 + [((4, d // 2 + s // 4, d), LOW)] * 2
    return pl.pallas_call(
        attn_bwd_kernel,
        grid_spec=prefetch(
            1,
            (steps,),
            ins + [pl.BlockSpec(memory_space=pl.ANY)] * 6 + small,
            [whole(shape) for shape, _ in shapes],
            [pltpu.VMEM((s, d), LOW)] * 4
            + [pltpu.VMEM((d, d), LOW)] * 3
            + [pltpu.VMEM((s, d), LOW), pltpu.VMEM((s, d), F32), pltpu.VMEM((s, d), LOW)]
            + [pltpu.VMEM((4, s // 4, d), LOW), pltpu.SemaphoreType.DMA((6,))],
        ),
        out_shape=[struct(*one) for one in shapes],
        compiler_params=params(),
        cost_estimate=cost(14 * s * d * d + 8 * s * s * 256 * heads, 28e6),
        name="attention_backward",
    )(place, al, wo, q, k, v, e, inv, mt, wq, wk, wv, x, base, mixed, *res, pool, vec1, vec2, ib)


def normalize(values):
    center = values - jnp.mean(values, axis=-1, keepdims=True)
    root = lax.rsqrt(jnp.mean(center * center, axis=-1, keepdims=True) + EPSILON)
    return center * root, root


def normalize_back(upstream, normed, root, gain):
    scaled = upstream * gain
    plain = jnp.mean(scaled, axis=-1, keepdims=True)
    crossed = jnp.mean(scaled * normed, axis=-1, keepdims=True)
    return root * (scaled - plain - normed * crossed)


def gelu_pair(v):
    cdf = lax.erf(v * 0.7071067811865476) * 0.5 + 0.5
    bell = jnp.exp(v * v * -0.5)
    return v * cdf, cdf + v * (bell * 0.3989422804014327)


def ff_kernel(
    row0, mixed, wo, bo, x, g1, s1, w1, b1, w2, b2, g2, s2, wp, bp, u0, u1, u2, u3,
    lhs_o, rhs_o, t0, t1, t2, t3, pool_o, al_o, fb_o, vec1_o, vec2_o, ib_o,
    w1s, w2s, wps, ups, gp, normed1, acc, sb, sems, *, chunk
):
    s, d = x.shape
    blocks = w1s.shape[0]
    ol_o, hid_o = lhs_o.at[0], lhs_o.at[1]
    act_o, il_o = rhs_o.at[0], rhs_o.at[1]
    n = s // 4
    per = chunk // n
    outs = (t0, t1, t2, t3)
    chunks = [slice(r, r + chunk) for r in range(0, s, chunk)]

    def load1(f):
        return pltpu.make_async_copy(w1.at[:, pl.ds(f * d, d)], w1s.at[f], sems.at[f])

    def load2(f):
        return pltpu.make_async_copy(w2.at[pl.ds(f * d, d), :], w2s.at[f], sems.at[blocks + f])

    loads = [pltpu.make_async_copy(wp, wps, sems.at[2 * blocks])]
    for m, part in enumerate((u0, u1, u2, u3)):
        loads.append(pltpu.make_async_copy(part, ups.at[m], sems.at[2 * blocks + 1 + m]))
    for f in range(blocks):
        load1(f).start()
        load2(f).start()
    for load in loads:
        load.start()

    roots1 = []
    for rows in chunks:
        val = nn(mixed[rows, :], wo[...]) + bo[...].astype(F32) + x[rows, :].astype(F32)
        normed, root = normalize(val)
        roots1.append(root)
        normed1[rows, :] = normed
        h = (normed * g1[...].astype(F32) + s1[...].astype(F32)).astype(LOW)
        hid_o[rows, :] = h
        acc[rows, :] = h.astype(F32) + b2[...].astype(F32)

    def forward(f, carry):
        load1(f).wait()
        load2(f).wait()
        for rows in chunks:
            pre = nn(hid_o[rows, :], w1s[f]) + b1[f].astype(F32)
            act, slope = gelu_pair(pre)
            act = act.astype(LOW)
            act_o[f, rows, :] = act
            gp[f, rows, :] = slope.astype(LOW)
            acc[rows, :] += nn(act, w2s[f])
        return carry

    lax.fori_loop(0, blocks, forward, 0)
    for load in loads:
        load.wait()

    gain = g2[...].astype(F32)
    roots2 = []
    for k, rows in enumerate(chunks):
        normed, root = normalize(acc[rows, :])
        roots2.append(root)
        res = (normed * gain + s2[...].astype(F32)).astype(LOW)
        al_o[rows, :] = res
        for j in range(per):
            outs[k * per + j][...] = res[j * n : j * n + n, :]
        acc[rows, :] = normed
    cls = al_o[pl.ds(pl.multiple_of(row0[0], 128), 16), :]
    pooled = jnp.tanh(nn(cls, wps[...]) + bp[...].astype(F32))
    pull = 0.0
    for m in range(4):
        terms = ups[m, n : n + 16, :].astype(F32)
        terms = jnp.broadcast_to(terms[0:1] + terms[1:2], (8, d))
        pull = pull + pltpu.roll(terms, ((row0[2] + 4 - m) % 4) * (d // 4), 1)
    pre = pull[:1] * (1.0 - pooled * pooled)
    cls_grad = nt(pre.astype(LOW), wps[...])[:1]
    high = pooled[:1].astype(LOW).astype(F32)
    pool = [cls[:1].astype(F32), pre[:1], high, pooled[:1] - high, jnp.zeros((12, d), F32)]
    pool_o[...] = jnp.concatenate(pool, axis=0).astype(LOW)
    gs, ss, bs = 0.0, 0.0, 0.0
    for k, rows in enumerate(chunks):
        ids = lax.broadcasted_iota(jnp.int32, (chunk, 1), 0) + rows.start
        up = jnp.concatenate([ups[k * per + j, 0:n, :] for j in range(per)], axis=0).astype(F32)
        upstream = up + jnp.where(ids == row0[0], cls_grad, 0.0)
        normed = acc[rows, :]
        back = normalize_back(upstream, normed, roots2[k], gain)
        sb[rows, :] = back
        low = back.astype(LOW)
        ol_o[rows, :] = low
        gs = gs + jnp.sum(upstream * normed, axis=0, keepdims=True)
        ss = ss + jnp.sum(upstream, axis=0, keepdims=True)
        bs = bs + jnp.sum(low.astype(F32), axis=0, keepdims=True)
    live = row0[1].astype(F32)
    vec2_o[0:1, :] = gs * live
    vec2_o[1:2, :] = ss * live
    vec2_o[2:3, :] = bs * live

    def backward(f, carry):
        bias = 0.0
        for rows in chunks:
            low = (nt(ol_o[rows, :], w2s[f]) * gp[f, rows, :].astype(F32)).astype(LOW)
            il_o[f, rows, :] = low
            bias = bias + jnp.sum(low.astype(F32), axis=0, keepdims=True)
            sb[rows, :] += nt(low, w1s[f])
        ib_o[f] = bias
        return carry

    lax.fori_loop(0, blocks, backward, 0)
    gain = g1[...].astype(F32)
    gs, ss, bs = 0.0, 0.0, 0.0
    for k, rows in enumerate(chunks):
        upstream = sb[rows, :]
        normed = normed1[rows, :]
        back = normalize_back(upstream, normed, roots1[k], gain)
        fb_o[rows, :] = back
        low = back.astype(LOW)
        al_o[rows, :] = low
        gs = gs + jnp.sum(upstream * normed, axis=0, keepdims=True)
        ss = ss + jnp.sum(upstream, axis=0, keepdims=True)
        bs = bs + jnp.sum(low.astype(F32), axis=0, keepdims=True)
    vec1_o[0:1, :] = gs
    vec1_o[1:2, :] = ss
    vec1_o[2:3, :] = bs


def feed_forward(row0, mixed, wo, bo, x, g1, s1, w1, b1, w2, b2, g2, s2, wp, bp, ups, chunk=256):
    s, d = x.shape
    ff = w1.shape[1]
    blocks = ff // d
    full, row = whole((s, d)), whole((1, d))
    away = pl.BlockSpec(memory_space=pl.ANY)
    part = (s // 4 + 16, d)
    return pl.pallas_call(
        functools.partial(ff_kernel, chunk=chunk),
        grid_spec=prefetch(
            1,
            (1,),
            [full, whole((d, d)), row, full, row, row, away, whole((blocks, 1, d)), away, row, row, row]
            + [away, row]
            + [away] * 4,
            [whole((2, s, d)), whole((2, blocks, s, d))]
            + [whole((s // 4, d))] * 4
            + [whole((16, d)), full, full, whole((8, d)), whole((8, d)), whole((blocks, 1, d))],
            [
                pltpu.VMEM((blocks, d, d), LOW),
                pltpu.VMEM((blocks, d, d), LOW),
                pltpu.VMEM((d, d), LOW),
                pltpu.VMEM((4,) + part, LOW),
                pltpu.VMEM((blocks, s, d), LOW),
                pltpu.VMEM((s, d), F32),
                pltpu.VMEM((s, d), F32),
                pltpu.VMEM((s, d), F32),
                pltpu.SemaphoreType.DMA((2 * blocks + 5,)),
            ],
        ),
        out_shape=[struct((2, s, d), LOW), struct((2, blocks, s, d), LOW)]
        + [struct((s // 4, d), LOW)] * 4
        + [
            struct((16, d), LOW),
            struct((s, d), LOW),
            struct((s, d), F32),
            struct((8, d), F32),
            struct((8, d), F32),
            struct((blocks, 1, d), F32),
        ],
        compiler_params=params(),
        cost_estimate=cost(2 * s * d * d + 8 * s * d * ff, 30e6),
        name="feed_forward",
    )(row0, mixed, wo, bo, x, g1, s1, w1, b1.reshape(blocks, 1, d), w2, b2, g2, s2, wp, bp, *ups)


def tn(a, b):
    return lax.dot_general(a, b, (((0,), (0,)), ((), ())), preferred_element_type=F32)


def prefetch(count, grid, in_specs, out_specs, scratch=()):
    return pltpu.PrefetchScalarGridSpec(
        num_scalar_prefetch=count,
        grid=grid,
        in_specs=in_specs,
        out_specs=out_specs,
        scratch_shapes=list(scratch),
    )


def index_kernel(ids, req_o, col_o, row_o, *, rows, slots):
    count, n = ids.shape
    owners = req_o.shape[0]
    owner = ((ids[...].astype(F32) + 0.5) * (1.0 / rows)).astype(jnp.int32)
    local = ids[...] - owner * rows + 1
    flat = [owner.astype(F32), (local // 64).astype(F32), (local % 64).astype(F32)]
    flat = jnp.concatenate(flat + [jnp.zeros((16 - 3 * count, n), F32)], axis=0)
    cols = flat.T
    lane = lax.broadcasted_iota(jnp.int32, (n, owners), 1).astype(F32)
    before = lax.broadcasted_iota(jnp.int32, (n, n), 1) < lax.broadcasted_iota(jnp.int32, (n, n), 0)
    before = jnp.where(before, 1.0, 0.0).astype(LOW)
    seen = jnp.zeros((1, owners), F32)
    high, low, places = 0.0, 0.0, []
    slot_lane = lax.broadcasted_iota(jnp.int32, (n, 128), 1).astype(F32)
    for s in range(count):
        hot = jnp.where(lane == cols[:, s : s + 1], 1.0, 0.0)
        hot_low = hot.astype(LOW)
        within = jnp.sum((nn(before, hot_low) + seen) * hot, axis=1, keepdims=True)
        seen = seen + jnp.sum(hot, axis=0, keepdims=True)
        place = cols[:, s : s + 1] * slots + within
        places.append(place)
        here = slot_lane == within
        put_high = jnp.where(here, cols[:, count + s : count + s + 1], 0.0).astype(LOW)
        put_low = jnp.where(here, cols[:, 2 * count + s : 2 * count + s + 1], 0.0).astype(LOW)
        high = high + tn(hot_low, put_high)
        low = low + tn(hot_low, put_low)
    req_o[...] = (high * 64.0 + low).astype(jnp.int32)[:, :slots] - 1
    places.append(jnp.full((n, 1), -1.0, F32))
    table = jnp.concatenate([jnp.broadcast_to(p, (n, 8)) for p in places], axis=1)
    table = jnp.concatenate([table, jnp.zeros((n, 128 - table.shape[1]), F32)], axis=1)
    turned = table.T.astype(jnp.int32)
    for s in range(count + 1):
        col_o[s] = places[s].astype(jnp.int32)
        row_o[s] = turned[8 * s : 8 * s + 1, :]


def index_requests(ids, rows, owners, slots):
    count, n = ids.shape
    return pl.pallas_call(
        functools.partial(index_kernel, rows=rows, slots=slots),
        grid=(1,),
        in_specs=[whole((count, n))],
        out_specs=[whole((owners, slots)), whole((count + 1, n, 1)), whole((count + 1, 1, n))],
        out_shape=[
            struct((owners, slots), jnp.int32),
            struct((count + 1, n, 1), jnp.int32),
            struct((count + 1, 1, n), jnp.int32),
        ],
        compiler_params=params(),
        cost_estimate=cost(0, 1e6),
        name="index_requests",
    )(ids)


def gather_kernel(fetch, table, out, acc, *, rows):
    step = pl.program_id(0)
    last = pl.num_programs(0) - 1
    blk = table.shape[0]
    ids = lax.broadcasted_iota(jnp.int32, (1, blk), 1) + step * blk
    hot = jnp.where(ids == fetch[...], 1.0, 0.0).astype(LOW)

    def add(block):
        part = nn(hot, block)

        @pl.when(step == 0)
        def _():
            acc[...] = part

        @pl.when(step > 0)
        def _():
            acc[...] += part

    @pl.when(step < last)
    def _():
        add(table[...])

    @pl.when(step == last)
    def _():
        ids_col = lax.broadcasted_iota(jnp.int32, (blk, 1), 0) + step * blk
        add(jnp.where(ids_col < rows, table[...], jnp.zeros((), LOW)))
        out[...] = acc[...].astype(LOW)


def gather_rows(fetch, table, blk=2048):
    slots = fetch.shape[0]
    rows, d = table.shape
    return pl.pallas_call(
        functools.partial(gather_kernel, rows=rows),
        grid=(pl.cdiv(rows, blk),),
        in_specs=[whole((slots, 1)), pl.BlockSpec((blk, d), lambda i: (i, 0))],
        out_specs=whole((slots, d)),
        out_shape=struct((slots, d), LOW),
        scratch_shapes=[pltpu.VMEM((slots, d), F32)],
        compiler_params=params(),
        cost_estimate=cost(2 * slots * rows * d, 8e6),
        name="gather_rows",
    )(fetch, table)


def embed_kernel(place, slot, replies, pos, o0, o1, o2, o3):
    ids = lax.broadcasted_iota(jnp.int32, (1, replies.shape[0]), 1)
    for m, out in enumerate((o0, o1, o2, o3)):
        sent = (place[0] + m) % 4
        hot = jnp.where(ids == slot[sent], 1.0, 0.0).astype(LOW)
        live = jnp.where(sent < 3, 1.0, 0.0)
        out[...] = ((nn(hot, replies[...]) + pos[...].astype(F32)) * live).astype(LOW)


def embed_parts(place, slot, replies, pos):
    slots, d = replies.shape
    n = pos.shape[0]
    return pl.pallas_call(
        embed_kernel,
        grid_spec=prefetch(
            1,
            (1,),
            [whole((4, n, 1)), whole((slots, d)), whole((n, d))],
            [whole((n, d))] * 4,
        ),
        out_shape=[struct((n, d), LOW)] * 4,
        compiler_params=params(),
        cost_estimate=cost(2 * slots * 4 * n * d, 3e6),
        name="embed_parts",
    )(place, slot, replies, pos)


def cotangent_kernel(place, grads, terms, o0, o1, o2, o3):
    n = grads.shape[1]
    for m, out in enumerate((o0, o1, o2, o3)):
        sent = (place[0] + m) % 4
        here = jnp.minimum(sent, 2)
        live = jnp.where(sent < 3, 1.0, 0.0)
        out[0:n, :] = (grads[here].astype(F32) * live).astype(LOW)
        out[n : n + 16, :] = (terms[here].astype(F32) * live).astype(LOW)


def cotangent_parts(place, grads, terms):
    _, n, d = grads.shape
    return pl.pallas_call(
        cotangent_kernel,
        grid_spec=prefetch(
            1, (1,), [whole(grads.shape), whole(terms.shape)], [whole((n + 16, d))] * 4
        ),
        out_shape=[struct((n + 16, d), LOW)] * 4,
        compiler_params=params(),
        cost_estimate=cost(0, 2e6),
        name="cotangent_parts",
    )(place, grads, terms)


def outgoing_kernel(place, slot, p0, p1, p2, p3, out):
    ids = lax.broadcasted_iota(jnp.int32, (out.shape[0], 1), 0)
    total = 0.0
    for m, part in enumerate((p0, p1, p2, p3)):
        sent = (place[0] + m) % 4
        hot = jnp.where(ids == slot[sent], 1.0, 0.0).astype(LOW)
        total = total + nn(hot, part[...])
    out[...] = total.astype(LOW)


def outgoing_rows(place, slot, parts, slots):
    n = slot.shape[2]
    d = parts[0].shape[1]
    return pl.pallas_call(
        outgoing_kernel,
        grid_spec=prefetch(
            1,
            (1,),
            [whole((4, 1, n))] + [pl.BlockSpec((n, d), lambda i, p: (0, 0))] * 4,
            whole((slots, d)),
        ),
        out_shape=struct((slots, d), LOW),
        compiler_params=params(),
        cost_estimate=cost(2 * slots * 4 * n * d, 3e6),
        name="outgoing_rows",
    )(place, slot, *parts)


def table_kernel(fetch, incoming, out):
    blk = out.shape[0]
    ids = lax.broadcasted_iota(jnp.int32, (blk, 1), 0) + pl.program_id(0) * blk
    out[...] = nn(jnp.where(ids == fetch[...], 1.0, 0.0).astype(LOW), incoming[...])


def table_grad(fetch, incoming, rows, blk=1024):
    slots, d = incoming.shape
    return pl.pallas_call(
        table_kernel,
        grid=(pl.cdiv(rows, blk),),
        in_specs=[whole((1, slots)), whole((slots, d))],
        out_specs=pl.BlockSpec((blk, d), lambda i: (i, 0)),
        out_shape=struct((rows, d), F32),
        compiler_params=params(),
        cost_estimate=cost(2 * slots * rows * d, 13e6),
        name="table_gradient",
    )(fetch, incoming)


def unpermute_kernel(place, p0, p1, p2, p3, out):
    for m, part in enumerate((p0, p1, p2, p3)):
        sent = (place[0] + m) % 4

        @pl.when(sent < 3)
        def _():
            out[sent] = part[...]


def unpermute(place, parts, n):
    d = parts[0].shape[1]
    return pl.pallas_call(
        unpermute_kernel,
        grid_spec=prefetch(
            1, (1,), [pl.BlockSpec((n, d), lambda i, p: (1, 0))] * 4, whole((3, n, d))
        ),
        out_shape=struct((3, n, d), parts[0].dtype),
        compiler_params=params(),
        cost_estimate=cost(0, 2e6),
        name="unpermute",
    )(place, *parts)


def ff_send_kernel(which, left, right, out):
    out[0] = tn(left[0], right[0, 0]).astype(LOW)


def ff_specs(s, d):
    return [
        pl.BlockSpec((1, s, d), lambda f, w: (w[0], 0, 0)),
        pl.BlockSpec((1, 1, s, d), lambda f, w: (w[0], f, 0, 0)),
    ]


def ff_send(which, left, right):
    _, blocks, s, d = right.shape
    return pl.pallas_call(
        ff_send_kernel,
        grid_spec=prefetch(
            1, (blocks,), ff_specs(s, d), pl.BlockSpec((1, d, d), lambda f, w: (f, 0, 0))
        ),
        out_shape=struct((blocks, d, d), LOW),
        compiler_params=params(),
        cost_estimate=cost(2 * blocks * s * d * d, 9e6),
        name="ff_send",
    )(which, left, right)


def ff_keep_kernel(place, left, right, got, o0, o1, o2, o3, acc):
    f = pl.program_id(0)
    total = tn(left[0], right[0, 0]) + got[0].astype(F32)
    acc[f] = total.astype(LOW).reshape(acc.shape[1:])

    @pl.when(f == pl.num_programs(0) - 1)
    def _():
        for m, out in enumerate((o0, o1, o2, o3)):
            index = (place[1] + m) % 4

            @pl.when(place[0] == 0)
            def _():
                for z in range(4):
                    out[z] = acc[z, index]

            @pl.when(place[0] == 1)
            def _():
                out[...] = acc[index]


def ff_keep(place, left, right, got):
    _, blocks, s, d = right.shape
    shape = (4, d // 4, d)
    return pl.pallas_call(
        ff_keep_kernel,
        grid_spec=prefetch(
            1,
            (blocks,),
            ff_specs(s, d) + [pl.BlockSpec((1, d, d), lambda f, w: (f, 0, 0))],
            [whole(shape)] * 4,
            [pltpu.VMEM((blocks,) + shape, LOW)],
        ),
        out_shape=[struct(shape, LOW)] * 4,
        compiler_params=params(),
        cost_estimate=cost(2 * blocks * s * d * d, 14e6),
        name="ff_keep",
    )(place, left, right, got)


def core_add_kernel(place, own, got, o0, o1, o2, o3):
    rows = o0.shape[1]
    for m, out in enumerate((o0, o1, o2, o3)):
        at = pl.ds(pl.multiple_of((place[0] + m) % 4 * rows, rows), rows)
        out[...] = (own[:, at, :].astype(F32) + got[:, at, :].astype(F32)).astype(LOW)


def core_add(place, own, got):
    out = (4, own.shape[1] // 4, own.shape[2])
    return pl.pallas_call(
        core_add_kernel,
        grid_spec=prefetch(1, (1,), [whole(own.shape)] * 2, [whole(out)] * 4),
        out_shape=[struct(out, LOW)] * 4,
        compiler_params=params(),
        cost_estimate=cost(0, 9e6),
        name="core_add",
    )(place, own, got)


def add4(a, b, c, d):
    return a[...].astype(F32) + b[...].astype(F32) + c[...].astype(F32) + d[...].astype(F32)


def ring_add_kernel(place, p0, p1, p2, p3, o0, o1, o2, o3, acc):
    acc[...] = add4(p0, p1, p2, p3)
    rows = o0.shape[1]
    for m, out in enumerate((o0, o1, o2, o3)):
        at = pl.ds(pl.multiple_of((place[0] + m) % 4 * rows, rows), rows)
        out[...] = acc[:, at, :].astype(LOW)


def ring_add(place, parts):
    shape = parts[0].shape
    out = (4, shape[1] // 4, shape[2])
    return pl.pallas_call(
        ring_add_kernel,
        grid_spec=prefetch(
            1, (1,), [whole(shape)] * 4, [whole(out)] * 4, [pltpu.VMEM(shape, F32)]
        ),
        out_shape=[struct(out, LOW)] * 4,
        compiler_params=params(),
        cost_estimate=cost(0, 6e6),
        name="ring_add",
    )(place, *parts)


def join_kernel(place, a0, a1, a2, a3, b0, b1, b2, b3, o0, o1, o2, o3, acc):
    acc[:, 0:48, :] = add4(a0, a1, a2, a3)
    acc[:, 48:80, :] = add4(b0, b1, b2, b3)
    for m, out in enumerate((o0, o1, o2, o3)):
        out[...] = acc[(place[0] + m) % 4].astype(LOW)


def join(place, first, second):
    d = first[0].shape[2]
    return pl.pallas_call(
        join_kernel,
        grid_spec=prefetch(
            1,
            (1,),
            [whole(first[0].shape)] * 4 + [whole(second[0].shape)] * 4,
            [whole((80, d))] * 4,
            [pltpu.VMEM((4, 80, d), F32)],
        ),
        out_shape=[struct((80, d), LOW)] * 4,
        compiler_params=params(),
        cost_estimate=cost(0, 4e6),
        name="join",
    )(place, *first, *second)


def piece_kernel(f0, f1, f2, f3, r0, r1, r2, r3, out):
    pool = [part[...].astype(F32)[0:2] for part in (r0, r1, r2, r3)]
    pool.append(jnp.zeros((8, out.shape[1]), F32))
    out[...] = jnp.concatenate([add4(f0, f1, f2, f3)] + pool, axis=0).astype(LOW)


def piece_rows(parts, pool):
    d = parts[0].shape[1]
    return pl.pallas_call(
        piece_kernel,
        grid=(1,),
        in_specs=[whole(p.shape) for p in parts]
        + [pl.BlockSpec((16, d), lambda i: (16, 0)) for p in pool],
        out_specs=whole((96, d)),
        out_shape=struct((96, d), LOW),
        compiler_params=params(),
        cost_estimate=cost(0, 1e6),
        name="piece_rows",
    )(*parts, *pool)


def order_kernel(place, p0, p1, p2, p3, out):
    for m, part in enumerate((p0, p1, p2, p3)):
        out[(place[0] + 4 - m) % 4] = part[...]


def order(place, parts):
    shape = parts[0].shape
    return pl.pallas_call(
        order_kernel,
        grid_spec=prefetch(1, (1,), [whole(shape)] * 4, whole((4,) + shape)),
        out_shape=struct((4,) + shape, LOW),
        compiler_params=params(),
        cost_estimate=cost(0, 3e6),
        name="order",
    )(place, *parts)


def finish_kernel(
    place, own, got, outer_o, inner_o, q_o, k_o, v_o, out_o, pos_o, vec_o, ib_o, pw_o, pb_o, acc, vec
):
    d = outer_o.shape[0]
    share = d // 4

    def mine(rows):
        return pltpu.roll(rows, d - share * place[1], 1)[:, 0:share]

    def fill(zero, one):
        pool = []
        for i in range(4):
            for k in range(4):
                at = 96 * k
                r = 192 * i + 48 * k
                acc[r : r + 48, :] = zero[i, at : at + 48, :].astype(F32)
                cols = slice(d * i, d * i + d)
                inner_o[48 * k : 48 * k + 48, cols] = one[i, at : at + 48, :].astype(F32)
                r = 128 * i + 32 * k
                first = zero[i, at + 48 : at + 80, :].astype(F32)
                second = one[i, at + 48 : at + 80, :].astype(F32)
                if r < 192:
                    q_o[r : r + 32, :] = first
                    v_o[r : r + 32, :] = second
                elif r < 384:
                    k_o[r - 192 : r - 160, :] = first
                    out_o[r - 192 : r - 160, :] = second
                else:
                    pos_o[r - 384 : r - 352, :] = first
                    if r == 384:
                        vec[...] = second[0:16]
                pool.append(zero[i, at + 80 : at + 96, :].astype(F32)[0:8])
                pool.append(one[i, at + 80 : at + 96, :].astype(F32)[0:8])
        outer_o[...] = acc[...].T
        pool = jnp.concatenate(pool, axis=0)
        even = lax.broadcasted_iota(jnp.int32, (pool.shape[0], 1), 0) % 2 == 0
        below = jnp.concatenate([pool[1:], pool[:1]], axis=0)
        acc[...] = tn(jnp.where(even, pool, 0.0).astype(LOW), below.astype(LOW))
        bias = jnp.sum(jnp.where(even, 0.0, pool), axis=0, keepdims=True)
        pb_o[...] = mine(jnp.broadcast_to(bias, (8, d)))[0:1]

    @pl.when(place[0] == 0)
    def _():
        fill(own, got)

    @pl.when(place[0] == 1)
    def _():
        fill(got, own)

    pw_o[...] = acc[pl.ds(pl.multiple_of(place[1] * share, share), share), :]
    vec_o[...] = mine(vec[0:8, :])
    ib_o[...] = vec[pl.ds(8 + place[1], 1), :]


def finish(place, own, got):
    d = own.shape[2]
    share = d // 4
    shapes = [(d, d), (share, 4 * d)] + [(share, d)] * 4 + [(128, d), (8, share), (1, d)]
    shapes += [(share, d), (1, share)]
    return pl.pallas_call(
        finish_kernel,
        grid_spec=prefetch(
            1,
            (1,),
            [whole(own.shape)] * 2,
            [whole(s) for s in shapes],
            [pltpu.VMEM((d, d), F32), pltpu.VMEM((16, d), F32)],
        ),
        out_shape=[struct(s, F32) for s in shapes],
        compiler_params=params(),
        cost_estimate=cost(0, 14e6),
        name="finish",
    )(place, own, got)


def pooled_kernel(place, p0, p1, p2, p3, out):
    for m, part in enumerate((p0, p1, p2, p3)):
        two = part[...].astype(F32)
        row = two[2:3] + two[3:4]
        out[(place[0] + m) % 4] = pltpu.roll(
            jnp.broadcast_to(row, (8, row.shape[1])), row.shape[1] - 192 * place[0], 1
        )


def pooled_rows(place, parts):
    d = parts[0].shape[1]
    below = pl.BlockSpec((16, d), lambda i, p: (16, 0))
    return pl.pallas_call(
        pooled_kernel,
        grid_spec=prefetch(1, (1,), [below] * 4, whole((4, 8, d))),
        out_shape=struct((4, 8, d), F32),
        compiler_params=params(),
        name="pooled_rows",
    )(place, *parts)


def shift_pairs(step, axes):
    pairs = []
    for y in range(4):
        for x in range(4):
            for c in range(2):
                to = (y, (x + step) % 4) if axes[c] == "x" else ((y + step) % 4, x)
                pairs.append(((y * 4 + x) * 2 + c, (to[0] * 4 + to[1]) * 2 + c))
    return pairs


def shift_first(array, step):
    return lax.ppermute(array, "batch", shift_pairs(step, "xy"))


def shift_second(array, step):
    return lax.ppermute(array, "batch", shift_pairs(step, "yx"))


def shift_z(array, step):
    return lax.ppermute(array, "seq", [(z, (z + step) % 4) for z in range(4)])


def swap_core(array):
    return lax.ppermute(array, "batch", [(i, i ^ 1) for i in range(32)])


def ring_send(parts, shift):
    return [parts[0], shift(parts[1], 1), shift(parts[2], 2), shift(parts[3], 3)]


def to_sentence(parts):
    out = [parts[0]]
    for step in (1, 2, 3):
        pairs = [(z, (z + step) % 4) for z in range(4) if (z + step) % 4 < 3]
        out.append(lax.ppermute(parts[step], "seq", pairs))
    return out


def from_sentence(parts):
    out = [parts[0]]
    for step in (1, 2, 3):
        pairs = [((z + step) % 4, z) for z in range(4) if (z + step) % 4 < 3]
        out.append(lax.ppermute(parts[step], "seq", pairs))
    return out


def tie(array, *after):
    return lax.optimization_barrier((array,) + after)[0]


def per_device(
    token_ids,
    lengths,
    word_table,
    positions,
    query_weight,
    key_weight,
    value_weight,
    query_bias,
    value_bias,
    output_weight,
    output_bias,
    first_gain,
    first_shift,
    inner_weight,
    inner_bias,
    outer_weight,
    outer_bias,
    second_gain,
    second_shift,
    pooler_weight,
    pooler_bias,
    out_grad,
    pooled_grad,
):
    num_sent, local_len = token_ids.shape
    table_rows, width = word_table.shape
    all_count = lax.axis_size("seq") * lax.axis_size("batch")
    z = lax.axis_index("seq")
    batch_place = lax.axis_index("batch")
    core = batch_place % 2
    x = (batch_place // 2) % 4
    y = batch_place // 8

    first = jnp.where(core == 0, x, y)
    second = jnp.where(core == 0, y, x)

    def scalars(*values):
        return jnp.stack([jnp.asarray(v, jnp.int32) for v in values])

    slots = 2 * num_sent * local_len // all_count
    all_slots = slots * all_count
    requests, slot_cols, slot_rows = index_requests(token_ids, table_rows, all_count, slots)
    arrived = lax.all_to_all(requests, ("batch", "seq"), split_axis=0, concat_axis=0, tiled=True)
    fetch = arrived.reshape(-1)
    found = gather_rows(fetch[:, None], word_table)
    replies = lax.all_to_all(
        found.reshape(all_count, slots, width),
        ("batch", "seq"),
        split_axis=0,
        concat_axis=0,
        tiled=True,
    ).reshape(all_slots, width)
    live = (z < 3).astype(jnp.int32)
    sentence = jnp.minimum(z, 2)

    def row(vector):
        return vector.reshape(1, -1)

    vectors = (
        query_bias,
        value_bias,
        output_bias,
        first_gain,
        first_shift,
        inner_bias,
        outer_bias,
        second_gain,
        second_shift,
        pooler_bias,
    )
    block_of = (z - jnp.arange(4, dtype=jnp.int32)) % 4
    place_of = block_of[:, None] * local_len + jnp.arange(local_len, dtype=jnp.int32)[None, :]
    live_keys = (place_of.reshape(-1, 1) < lengths[sentence]).astype(F32)

    high = pooled_grad.astype(LOW)
    terms = jnp.stack([high, (pooled_grad - high.astype(F32)).astype(LOW)], axis=1)
    terms = jnp.pad(terms, ((0, 0), (0, 14), (0, width - terms.shape[2])))
    early = [live_keys] + [row(v) for v in vectors]
    terms, *early = lax.optimization_barrier([terms] + early)
    live_keys, q_bias, v_bias, o_bias, gain1, shift1, in_bias, out_bias, gain2, shift2, pool_bias = early
    ups = to_sentence(cotangent_parts(scalars(z), out_grad, terms))
    parts = embed_parts(scalars(z), slot_cols, replies, positions)
    parts, ups = lax.optimization_barrier((parts, ups))
    embeds = to_sentence(parts)

    embed, query, key, value, expo, inverse, mixed_t, mixed = attn_fwd(
        embeds, query_weight, key_weight, value_weight, q_bias, v_bias, live_keys
    )
    (
        left,
        right,
        *result,
        pool,
        attention_low,
        first_back,
        vec1,
        vec2,
        inner_bias_grad,
    ) = feed_forward(
        scalars(sentence * local_len, live, z),
        mixed,
        output_weight,
        o_bias,
        embed,
        gain1,
        shift1,
        inner_weight,
        in_bias,
        outer_weight,
        out_bias,
        gain2,
        shift2,
        pooler_weight,
        pool_bias,
        ups,
    )

    ff_other = ff_send(scalars(1 - core), left, right)
    ff_parts = ff_keep(scalars(core, first), left, right, swap_core(ff_other))
    attention_low = tie(attention_low, ff_parts[0])
    ff_parts = ring_send(ff_parts, shift_first)
    *embed_grad, rest_other, rest_own = attn_bwd(
        scalars(z, core),
        attention_low,
        output_weight,
        query,
        key,
        value,
        expo,
        inverse,
        mixed_t,
        query_weight,
        key_weight,
        value_weight,
        embed,
        first_back,
        mixed,
        result,
        pool,
        vec1,
        vec2,
        inner_bias_grad,
    )
    embed_grad, rest_other, rest_own, ff_parts = lax.optimization_barrier(
        (embed_grad, rest_other, rest_own, ff_parts)
    )

    returned = from_sentence(embed_grad)
    ff_parts = list(ring_add(scalars(second), ff_parts))
    rest_own = tie(rest_own, ff_parts[0])
    rest_parts = core_add(scalars(first), rest_own, swap_core(rest_other))
    ff_parts[0] = tie(ff_parts[0], rest_parts[0])
    rest_parts = ring_send(rest_parts, shift_first)
    ff_parts = ring_send(ff_parts, shift_second)
    rest_parts = ring_add(scalars(second), rest_parts)
    returned[0] = tie(returned[0], rest_parts[0])
    outgoing = outgoing_rows(scalars(z), slot_rows, returned, all_slots)
    rest_parts = ring_send(rest_parts, shift_second)
    rest_parts[0] = tie(rest_parts[0], outgoing)
    parts = ring_send(join(scalars(z), ff_parts, rest_parts), shift_z)
    piece = piece_rows(parts, returned)
    pieces = [piece] + [shift_second(piece, m) for m in (1, 2, 3)]
    outgoing = tie(outgoing, piece).reshape(all_count, slots, width)
    pieces[0] = tie(pieces[0], outgoing)
    block = order(scalars(second), pieces).reshape(-1, width)
    blocks = [block] + [shift_first(block, m) for m in (1, 2, 3)]
    incoming = lax.all_to_all(
        tie(outgoing, block), ("batch", "seq"), split_axis=0, concat_axis=0, tiled=True
    ).reshape(all_slots, width)
    returned[0] = tie(returned[0], block)
    pooled = pooled_rows(scalars(z), returned)[:num_sent, 0, : width // 4]
    hidden_out = unpermute(scalars(z), returned, local_len)
    incoming = tie(incoming, pooled, hidden_out)
    blocks[0] = tie(blocks[0], incoming)
    whole_own = order(scalars(first), blocks)
    incoming = tie(incoming, whole_own)
    whole_other = swap_core(whole_own)
    grad_table = table_grad(fetch[None, :], incoming, table_rows)
    whole_other = tie(whole_other, grad_table)
    (
        grad_outer,
        grad_inner,
        grad_query,
        grad_key,
        grad_value,
        grad_output,
        grad_positions,
        mine,
        inner_bias_sum,
        grad_pooler,
        pooler_bias_sum,
    ) = finish(scalars(core, z), whole_own, whole_other)

    return (
        hidden_out,
        pooled,
        grad_table,
        grad_positions,
        grad_query,
        grad_key,
        grad_value,
        mine[0],
        mine[1],
        grad_output,
        mine[2],
        mine[3],
        mine[4],
        grad_inner,
        inner_bias_sum[0],
        grad_outer,
        mine[5],
        mine[6],
        mine[7],
        grad_pooler,
        pooler_bias_sum[0],
    )


def solution(mesh):
    in_specs = (
        P("batch", "seq"),
        P("batch"),
        P(("batch", "seq"), None),
        P("seq", None),
        P(),
        P(),
        P(),
        P(),
        P(),
        P(),
        P(),
        P(),
        P(),
        P(),
        P(),
        P(),
        P(),
        P(),
        P(),
        P(),
        P(),
        P("batch", "seq", None),
        P("batch", "seq"),
    )
    out_specs = (
        P("batch", "seq", None),
        P("batch", "seq"),
        P(("batch", "seq"), None),
        P("seq", None),
        P("seq", None),
        P("seq", None),
        P("seq", None),
        P("seq"),
        P("seq"),
        P("seq", None),
        P("seq"),
        P("seq"),
        P("seq"),
        P("seq", None),
        P("seq"),
        P("seq", None),
        P("seq"),
        P("seq"),
        P("seq"),
        P("seq", None),
        P("seq"),
    )
    return jax.shard_map(
        per_device, mesh=mesh, in_specs=in_specs, out_specs=out_specs, check_vma=False
    )
```
